32 devices in a mesh: pipe: 2 (over core), dp: 4 (over z), seq: 2 (over x), mp: 2 (over y).
Axes of the slice: x: 2, y: 2, z: 4, core: 2. Of those that a mesh axis runs over, the one named last changes fastest.
Arguments:
- characters: bfloat16 [16, 2048, 768], P('dp', ('seq', 'mp'), 'pipe'), may hold values from -6 to 6
- row_lengths: int32 [16], P('dp'), may hold values from 204 to 2048, as said below
- w_query: bfloat16 [768, 768], P(None, 'mp'), may hold values from -0.21875 to 0.21875
- b_query: bfloat16 [768], P('mp'), may hold values from -1.75 to 1.75
- w_key: bfloat16 [768, 768], P(None, 'mp'), may hold values from -0.21875 to 0.21875
- w_value: bfloat16 [768, 768], P(None, 'mp'), may hold values from -0.21875 to 0.21875
- b_value: bfloat16 [768], P('mp'), may hold values from -1.75 to 1.75
- w_attn_out: bfloat16 [768, 768], P('mp'), may hold values from -0.875 to 0.875
- b_attn_out: bfloat16 [768], replicated, may hold values from -1.75 to 1.75
- gain_one: bfloat16 [768], replicated, may hold values from 0.5 to 1.5
- shift_one: bfloat16 [768], replicated, may hold values from -1.75 to 1.75
- w_inner: bfloat16 [768, 3072], P(None, 'mp'), may hold values from -0.21875 to 0.21875
- b_inner: bfloat16 [3072], P('mp'), may hold values from -1.75 to 1.75
- w_outer: bfloat16 [3072, 768], P('mp'), may hold values from -0.15625 to 0.15625
- b_outer: bfloat16 [768], replicated, may hold values from -1.75 to 1.75
- gain_two: bfloat16 [768], replicated, may hold values from 0.5 to 1.5
- shift_two: bfloat16 [768], replicated, may hold values from -1.75 to 1.75
- w_conv: bfloat16 [3072, 768], replicated, may hold values from -0.109375 to 0.109375
- b_conv: bfloat16 [768], replicated, may hold values from -1.75 to 1.75
- gain_three: bfloat16 [768], replicated, may hold values from 0.5 to 1.5
- shift_three: bfloat16 [768], replicated, may hold values from -1.75 to 1.75
- molecule_grad: bfloat16 [16, 512, 768], P('dp', ('seq', 'mp'), 'pipe'), may hold values from -6 to 6
Outputs:
- molecules: bfloat16 [16, 512, 768], P('dp', ('seq', 'mp'), 'pipe')
- chars_grad: float32 [16, 2048, 768], P('dp', ('seq', 'mp'), 'pipe')
- grad_w_query: float32 [768, 768], P(('pipe', 'dp', 'seq'), 'mp')
- grad_b_query: float32 [768], replicated
- grad_w_key: float32 [768, 768], P(('pipe', 'dp', 'seq'), 'mp')
- grad_w_value: float32 [768, 768], P(('pipe', 'dp', 'seq'), 'mp')
- grad_b_value: float32 [768], replicated
- grad_w_attn_out: float32 [768, 768], P('mp', ('pipe', 'dp', 'seq'))
- grad_b_attn_out: float32 [768], replicated
- grad_gain_one: float32 [768], replicated
- grad_shift_one: float32 [768], replicated
- grad_w_inner: float32 [768, 3072], P(('pipe', 'dp', 'seq'), 'mp')
- grad_b_inner: float32 [3072], replicated
- grad_w_outer: float32 [3072, 768], P('mp', ('pipe', 'dp', 'seq'))
- grad_b_outer: float32 [768], replicated
- grad_gain_two: float32 [768], replicated
- grad_shift_two: float32 [768], replicated
- grad_w_conv: float32 [3072, 768], P(('pipe', 'dp', 'seq', 'mp'))
- grad_b_conv: float32 [768], replicated
- grad_gain_three: float32 [768], replicated
- grad_shift_three: float32 [768], replicated
The draws below stay inside these ranges and needn't reach their ends.
Inputs may be any that keep to these rules, and one draw needn't show every extreme that they name: `row_lengths`: each aligned block of 4 rows holds one row of length 2048.
All inputs are finite; a program needn't handle non-finite values.
Results may differ from the reference program's by a relative error of at most 0.023.
Values may be sent and summed in bfloat16 or wider, within the bound.
No kernel may reach another device: no remote copies, remote signals or barrier semaphores. Data moves between devices by JAX's collectives and lax.ppermute only.
A program may use at most 448 MiB of HBM per device.

```python
import jax
import jax.numpy as jnp
from jax import lax

D = 768
HEADS = 12
HEAD = 64
FF = 3072
WINDOW = 128
KERNEL = 4
LEN = 2048
MOLS = 512
ROWS_DEV = 4
ROWS = 16


def draw_row_lengths(key, part):
    key = jax.random.fold_in(key, 7)
    base_key, pick_key = jax.random.split(key)
    lengths = jax.random.randint(base_key, (ROWS,), LEN // 10, LEN + 1)
    chosen = jax.random.randint(pick_key, (ROWS // ROWS_DEV, 1), 0, ROWS_DEV)
    slot_ids = jnp.arange(ROWS_DEV, dtype=jnp.int32)[None, :]
    is_full = (slot_ids == chosen).reshape(ROWS)
    return jnp.where(is_full, LEN, lengths).astype(jnp.int32)


def steps_of(own_key, dims, cuts, least, high):
    loudness = 1.0
    for dim, shards_of in cuts:
        draws = jax.random.uniform(jax.random.fold_in(jax.random.fold_in(own_key, 6), dim), (shards_of,), jnp.float32, least / len(cuts), high / len(cuts))
        loudness = loudness * jnp.repeat(jnp.exp(draws), dims[dim] // shards_of).reshape((-1,) + (1,) * (len(dims) - 1 - dim))
    return loudness


def centred(stream_key, dims, scale, limit, cuts=(), kind=jnp.bfloat16):
    drawn = jax.random.normal(stream_key, dims, jnp.float32) * scale
    if len(cuts) > 0:
        drawn = steps_of(stream_key, dims, cuts, -0.22, 0.18) * drawn
    return jnp.clip(drawn, min=-limit, max=limit).astype(kind)


def setup_inputs(seed: int = 0) -> dict:
    key_list = jax.random.split(jax.random.key(seed), 23)
    characters = centred(key_list[0], (ROWS, LEN, D), 1.0, 6.0, ((0, 4), (1, 4), (2, 2)))
    row_lengths = draw_row_lengths(jax.random.fold_in(key_list[22], 71), 0)
    w_query = centred(key_list[2], (D, D), D ** -0.5, 0.21875, ((1, 2),))
    b_query = centred(key_list[3], (D,), 0.3, 1.75, ((0, 2),))
    w_key = centred(key_list[4], (D, D), D ** -0.5, 0.21875, ((1, 2),))
    w_value = centred(key_list[5], (D, D), D ** -0.5, 0.21875, ((1, 2),))
    b_value = centred(key_list[6], (D,), 0.3, 1.75, ((0, 2),))
    w_attn_out = centred(key_list[7], (D, D), (D // 16) ** -0.5, 0.875, ((0, 2),))
    b_attn_out = centred(key_list[8], (D,), 0.3, 1.75)
    gain_one = jnp.clip(1.0 + 0.1 * jax.random.normal(key_list[9], (D,), jnp.float32), 0.5, 1.5).astype(jnp.bfloat16)
    shift_one = centred(key_list[10], (D,), 0.3, 1.75)
    w_inner = centred(key_list[11], (D, FF), D ** -0.5, 0.21875, ((1, 2),))
    b_inner = centred(key_list[12], (FF,), 0.3, 1.75, ((0, 2),))
    w_outer = centred(key_list[13], (FF, D), (FF // 2) ** -0.5, 0.15625, ((0, 2),))
    b_outer = centred(key_list[14], (D,), 0.3, 1.75)
    gain_two = jnp.clip(1.0 + 0.1 * jax.random.normal(key_list[15], (D,), jnp.float32), 0.5, 1.5).astype(jnp.bfloat16)
    shift_two = centred(key_list[16], (D,), 0.3, 1.75)
    w_conv = centred(key_list[17], (KERNEL * D, D), (KERNEL * D) ** -0.5, 0.109375)
    b_conv = centred(key_list[18], (D,), 0.3, 1.75)
    gain_three = jnp.clip(1.0 + 0.1 * jax.random.normal(key_list[19], (D,), jnp.float32), 0.5, 1.5).astype(jnp.bfloat16)
    shift_three = centred(key_list[20], (D,), 0.3, 1.75)
    molecule_grad = centred(key_list[21], (ROWS, MOLS, D), 1.0, 6.0, ((0, 4), (1, 4), (2, 2)))
    return dict(characters=characters, row_lengths=row_lengths, w_query=w_query, b_query=b_query, w_key=w_key, w_value=w_value, b_value=b_value, w_attn_out=w_attn_out, b_attn_out=b_attn_out, gain_one=gain_one, shift_one=shift_one, w_inner=w_inner, b_inner=b_inner, w_outer=w_outer, b_outer=b_outer, gain_two=gain_two, shift_two=shift_two, w_conv=w_conv, b_conv=b_conv, gain_three=gain_three, shift_three=shift_three, molecule_grad=molecule_grad)


@jax.custom_vjp
def low(v):
    return lax.optimization_barrier(v.astype(jnp.bfloat16)).astype(jnp.float32)

@jax.custom_vjp
def low_back(v):
    return v

def low_keep(v):
    return (low(v), None)

def low_pass(kept, grad):
    return (grad,)

def back_keep(v):
    return (v, None)

def back_low(kept, grad):
    return (low(grad),)
low.defvjp(low_keep, low_pass)
low_back.defvjp(back_keep, back_low)
epsilon = 1e-05
masked_score = -1e+30

def project(left, right):
    return jnp.einsum('...i,ij->...j', left, right, precision=lax.Precision.HIGHEST)

def normalize(values, gain, shift):
    centered = values - lax.optimization_barrier(jnp.mean(values, axis=-1, keepdims=True))
    spread = lax.optimization_barrier(jnp.mean(centered * centered, axis=-1, keepdims=True))
    return centered * lax.rsqrt(spread + epsilon) * gain + shift

def windows(padded, batch_size, blocks):
    shaped = padded.reshape(batch_size, blocks + 2, WINDOW, HEADS, HEAD)
    return jnp.concatenate([shaped[:, :-2], shaped[:, 1:-1], shaped[:, 2:]], axis=2)

def attend(queries, key_rows, value_rows, lengths):
    batch_size = queries.shape[0]
    blocks = LEN // WINDOW
    pad_edges = ((0, 0), (WINDOW, WINDOW), (0, 0))
    key_win = windows(jnp.pad(key_rows, pad_edges), batch_size, blocks)
    value_win = windows(jnp.pad(value_rows, pad_edges), batch_size, blocks)
    shaped = queries.reshape(batch_size, blocks, WINDOW, HEADS, HEAD)
    scores = jnp.einsum('bnqhe,bnkhe->bnhqk', shaped, key_win, precision=lax.Precision.HIGHEST) * HEAD ** (-0.5)
    scores = low_back(scores)
    block_starts = jnp.arange(blocks, dtype=jnp.int32)[:, None, None] * WINDOW
    query_pos = block_starts + jnp.arange(WINDOW, dtype=jnp.int32)[None, :, None]
    key_pos = block_starts - WINDOW + jnp.arange(3 * WINDOW, dtype=jnp.int32)[None, None, :]
    in_window = jnp.abs(query_pos - key_pos) < WINDOW
    allowed = in_window[None] & (key_pos[None] >= 0) & (key_pos[None] < lengths[:, None, None, None])
    scores = jnp.where(allowed[:, :, None], scores, masked_score)
    row_max = lax.optimization_barrier(jnp.max(scores, axis=-1, keepdims=True))
    weights = jnp.exp(scores - row_max)
    weights = low(weights / lax.optimization_barrier(jnp.sum(weights, axis=-1, keepdims=True)))
    attended = jnp.einsum('bnhqk,bnkhe->bnqhe', weights, value_win, precision=lax.Precision.HIGHEST)
    return attended.reshape(batch_size, LEN, D)

def first_section(characters, lengths, weights):
    w_query, b_query, w_key, w_value, b_value, w_attn_out, b_attn_out, gain_one, shift_one, w_inner, b_inner, w_outer, b_outer, gain_two, shift_two = weights
    queries = low_back(low(project(characters, w_query) + b_query))
    key_rows = low_back(low(project(characters, w_key)))
    value_rows = low_back(low(project(characters, w_value) + b_value))
    attended = low_back(low(attend(queries, key_rows, value_rows, lengths)))
    branch = low_back(project(attended, w_attn_out))
    middle = normalize(characters + branch + b_attn_out, gain_one, shift_one)
    hidden = low_back(project(low(middle), w_inner) + b_inner)
    activated = low(jax.nn.gelu(hidden, approximate=False))
    feed_out = low_back(project(activated, w_outer))
    live_rows = (jnp.arange(LEN, dtype=jnp.int32)[None, :] < lengths[:, None]).astype(jnp.float32)[:, :, None]
    return normalize(middle + feed_out + b_outer, gain_two, shift_two) * live_rows

def second_section(first_out, lengths, weights):
    w_conv, b_conv, gain_three, shift_three = weights
    sent_rows = low_back(low(first_out))
    grouped = sent_rows.reshape(sent_rows.shape[0], MOLS, KERNEL * D)
    conv_out = low_back(project(grouped, w_conv) + b_conv)
    mol_pos = jnp.arange(MOLS, dtype=jnp.int32) * KERNEL
    live_mols = (mol_pos[None, :] < lengths[:, None]).astype(jnp.float32)[:, :, None]
    return normalize(jax.nn.gelu(conv_out, approximate=False), gain_three, shift_three) * live_mols

def reference(characters, row_lengths, w_query, b_query, w_key, w_value, b_value, w_attn_out, b_attn_out, gain_one, shift_one, w_inner, b_inner, w_outer, b_outer, gain_two, shift_two, w_conv, b_conv, gain_three, shift_three, molecule_grad):
    first_weights = tuple((item.astype(jnp.float32) for item in (w_query, b_query, w_key, w_value, b_value, w_attn_out, b_attn_out, gain_one, shift_one, w_inner, b_inner, w_outer, b_outer, gain_two, shift_two)))
    second_weights = tuple((item.astype(jnp.float32) for item in (w_conv, b_conv, gain_three, shift_three)))
    pair_count = ROWS // 2
    paired_lengths = row_lengths.astype(jnp.int32).reshape(pair_count, 2)

    def forward(chars_float, first_params, second_params):

        def one_group(inputs):
            group_rows, lengths = inputs
            return second_section(first_section(group_rows, lengths, first_params), lengths, second_params)
        mapped = lax.map(jax.checkpoint(one_group), (chars_float.reshape(pair_count, 2, LEN, D), paired_lengths))
        return mapped.reshape(ROWS, MOLS, D)
    molecules, pullback = jax.vjp(forward, characters.astype(jnp.float32), first_weights, second_weights)
    chars_grad, grad_first, grad_second = pullback(molecule_grad.astype(jnp.float32))
    return (molecules.astype(jnp.bfloat16), chars_grad, grad_first[0], grad_first[1], grad_first[2], grad_first[3], grad_first[4], grad_first[5], grad_first[6], grad_first[7], grad_first[8], grad_first[9], grad_first[10], grad_first[11], grad_first[12], grad_first[13], grad_first[14], grad_second[0], grad_second[1], grad_second[2], grad_second[3])
```

```python
import functools

import jax
import jax.numpy as jnp
from jax import lax
from jax.experimental import pallas as pl
from jax.experimental.pallas import tpu as pltpu
from jax.sharding import PartitionSpec as P

HEAD = 64
WINDOW = 128
KERNEL = 4
PAIR = 2 * HEAD
VMEM_LIMIT = 56 << 20

epsilon = 1e-05
masked_score = -1e30
f32 = jnp.float32
bf16 = jnp.bfloat16


def mul(left, right):
    return jnp.dot(left, right, preferred_element_type=f32)


def mul_t(left, right):
    return lax.dot_general(left, right, (((1,), (1,)), ((), ())), preferred_element_type=f32)


def t_mul(left, right):
    return lax.dot_general(left, right, (((0,), (0,)), ((), ())), preferred_element_type=f32)


def gelu_parts(value):
    bell = jnp.exp(value * value * -0.5)
    t = 1.0 / (1.0 + jnp.abs(value) * 0.23164190)
    poly = t * (0.127414796 + t * (-0.142248368 + t * (0.7107068705 + t * (-0.7265760135 + t * 0.5307027145))))
    tail = poly * bell
    cdf = jnp.where(value < 0.0, tail, 1.0 - tail)
    return value * cdf, cdf + value * bell * 0.3989422804014327


def norm_parts(value):
    centered = value - jnp.mean(value, axis=-1, keepdims=True)
    scale = lax.rsqrt(jnp.mean(centered * centered, axis=-1, keepdims=True) + epsilon)
    return centered * scale, scale


def norm_back(cotangent, normal, scale):
    first = jnp.mean(cotangent, axis=-1, keepdims=True)
    second = jnp.mean(cotangent * normal, axis=-1, keepdims=True)
    return scale * (cotangent - first - normal * second)


def col_sum(value):
    return jnp.sum(value, axis=0, keepdims=True)


def low(value):
    return value.astype(bf16)


def call(body, grid, in_specs, out_specs, out_shape, args, scalars=(), scratch=(), flops=0, moved=0):
    return pl.pallas_call(
        body,
        grid_spec=pltpu.PrefetchScalarGridSpec(
            num_scalar_prefetch=len(scalars),
            grid=grid,
            in_specs=in_specs,
            out_specs=out_specs,
            scratch_shapes=scratch,
        ),
        out_shape=out_shape,
        compiler_params=pltpu.CompilerParams(vmem_limit_bytes=VMEM_LIMIT),
        cost_estimate=pl.CostEstimate(flops=int(flops), bytes_accessed=int(moved), transcendentals=0),
    )(*scalars, *args)


def whole_block(array):
    zeros = (0,) * array.ndim
    return pl.BlockSpec(array.shape, lambda *_: zeros, pipeline_mode=pl.Buffered(1))


def lead_block(array, size=1):
    rest = (0,) * (array.ndim - 1)
    return pl.BlockSpec((size,) + tuple(array.shape[1:]), lambda i, *_: (i,) + rest)


def chunk_block(array, size):
    return pl.BlockSpec((array.shape[0], size, array.shape[2]), lambda i, *_: (0, i, 0))


def shape_of(dims, kind):
    return jax.ShapeDtypeStruct(tuple(dims), kind)


def pair_lanes(rows):
    return lax.broadcasted_iota(jnp.int32, (rows, PAIR), 1) < HEAD


def split_pair(both, is_first):
    zero = jnp.zeros_like(both)
    return jnp.concatenate([jnp.where(is_first, both, zero), jnp.where(is_first, zero, both)], axis=0)


def join_pair(stacked, is_first):
    rows = stacked.shape[0] // 2
    return jnp.where(is_first, stacked[:rows], stacked[rows:])


def attend_kernel(span, block, last, info_ref, x_ref, w_ref, bq_ref, bv_ref, *refs):
    if last:
        part_ref, bo_ref, gain_ref, shift_ref = refs[:4]
        refs = refs[4:]
    q_ref, k_ref, v_ref, att_ref, lse_ref = refs[:5]
    refs = refs[5:]
    row = pl.program_id(0)
    length = info_ref[row + 1]
    start = info_ref[0]
    width = block + 2 * WINDOW
    pairs = q_ref.shape[2] // PAIR
    x = x_ref[0]
    own = x_ref[0, WINDOW : WINDOW + span]
    q_ref[0] = low(low(mul(own, w_ref[0]) + bq_ref[...]).astype(f32) * HEAD ** (-0.5))
    k_ref[0] = low(mul(x, w_ref[1]))
    v_ref[0] = low(mul(x, w_ref[2]) + bv_ref[...])
    is_first = pair_lanes(block)
    q_at = lax.broadcasted_iota(jnp.int32, (block, width), 0)
    k_at = lax.broadcasted_iota(jnp.int32, (block, width), 1) - WINDOW
    in_window = jnp.abs(q_at - k_at) < WINDOW
    lanes = lax.broadcasted_iota(jnp.int32, (block, PAIR), 1)

    def one_block(index, carry):
        at = pl.multiple_of(index * block, block)
        position = k_at + (start + at)
        bias = jnp.where(in_window & (position >= 0) & (position < length), 0.0, masked_score)
        bias = jnp.concatenate([bias, bias], axis=0)
        totals = jnp.zeros((block, PAIR), f32)
        for pair in range(pairs):
            cols = slice(pair * PAIR, (pair + 1) * PAIR)
            q2 = split_pair(q_ref[0, pl.ds(at, block), cols], is_first)
            scores = mul_t(q2, k_ref[0, pl.ds(at, width), cols]) + bias
            top = jnp.max(scores, axis=-1, keepdims=True)
            weights = jnp.exp(scores - top)
            total = jnp.sum(weights, axis=-1, keepdims=True)
            out = mul(low(weights), v_ref[0, pl.ds(at, width), cols]) * (1.0 / total)
            att_ref[0, pl.ds(at, block), cols] = low(join_pair(out, is_first))
            log_total = top + jnp.log(total)
            totals = jnp.where(lanes == 2 * pair, log_total[:block], totals)
            totals = jnp.where(lanes == 2 * pair + 1, log_total[block:], totals)
        lse_ref[0, index] = totals.T[:8]
        return carry

    lax.fori_loop(0, span // block, one_block, 0)
    branch = mul_t(att_ref[0], w_ref[3])
    if last:
        n_ref, s_ref, mid_ref = refs
        before = own.astype(f32) + part_ref[0] + branch + bo_ref[...]
        normal, scale = norm_parts(before)
        n_ref[0] = normal
        s_ref[0] = jnp.broadcast_to(scale, s_ref.shape[1:])
        mid_ref[0] = low(normal * gain_ref[...] + shift_ref[...])
    else:
        refs[0][0] = branch


def attend(info, x_ext, w4, b_query, b_value, span, block, tail=None):
    rows, extent, model = x_ext.shape
    local = w4.shape[2]
    out_shape = [
        shape_of((rows, span, local), bf16),
        shape_of((rows, extent, local), bf16),
        shape_of((rows, extent, local), bf16),
        shape_of((rows, span, local), bf16),
        shape_of((rows, span // block, 8, block), f32),
    ]
    args = [x_ext, w4, b_query, b_value]
    in_specs = [lead_block(x_ext)] + [whole_block(a) for a in args[1:]]
    if tail is None:
        out_shape += [shape_of((rows, span, model), f32)]
    else:
        out_shape += [
            shape_of((rows, span, model), f32),
            shape_of((rows, span, PAIR), f32),
            shape_of((rows, span, model), bf16),
        ]
        args += list(tail)
        in_specs += [lead_block(tail[0])] + [whole_block(a) for a in tail[1:]]
    flops = 2 * rows * local * (model * (2 * span + 2 * extent) + span * 4 * (block + 2 * WINDOW))
    return call(
        functools.partial(attend_kernel, span, block, tail is not None),
        (rows,),
        in_specs,
        [lead_block(o) for o in out_shape],
        out_shape,
        args,
        scalars=(info,),
        flops=3 * flops,
        moved=rows * extent * model * 8,
    )


def attend_back_kernel(span, block, info_ref, gb_ref, w_ref, q_ref, k_ref, v_ref, lse_ref, dq_ref, dk_ref, dv_ref, ga_ref, dk_acc, dv_acc):
    row = pl.program_id(0)
    length = info_ref[row + 1]
    start = info_ref[0]
    width = block + 2 * WINDOW
    pairs = q_ref.shape[2] // PAIR
    ga_ref[...] = low(mul(gb_ref[0], w_ref[0]))
    dk_acc[...] = jnp.zeros_like(dk_acc)
    dv_acc[...] = jnp.zeros_like(dv_acc)
    is_first = pair_lanes(block)
    q_at = lax.broadcasted_iota(jnp.int32, (width, block), 1)
    k_at = lax.broadcasted_iota(jnp.int32, (width, block), 0) - WINDOW
    in_window = jnp.abs(q_at - k_at) < WINDOW

    def one_block(index, carry):
        at = pl.multiple_of(index * block, block)
        position = k_at + (start + at)
        bias = jnp.where(in_window & (position >= 0) & (position < length), 0.0, masked_score)
        bias = jnp.concatenate([bias, bias], axis=1)
        for pair in range(pairs):
            cols = slice(pair * PAIR, (pair + 1) * PAIR)
            keys = k_ref[0, pl.ds(at, width), cols]
            q2 = split_pair(q_ref[0, pl.ds(at, block), cols], is_first)
            g2 = split_pair(ga_ref[pl.ds(at, block), cols], is_first)
            log_total = jnp.concatenate(
                [lse_ref[0, index, 2 * pair : 2 * pair + 1], lse_ref[0, index, 2 * pair + 1 : 2 * pair + 2]], axis=1
            )
            probs = jnp.exp(mul_t(keys, q2) + bias - log_total)
            grad_probs = mul_t(v_ref[0, pl.ds(at, width), cols], g2)
            inner = jnp.sum(probs * grad_probs, axis=0, keepdims=True)
            grad_scores = low(probs * (grad_probs - inner))
            dk_acc[pl.ds(at, width), cols] += mul(grad_scores, q2)
            dv_acc[pl.ds(at, width), cols] += mul(low(probs), g2)
            grad_q = t_mul(grad_scores, keys) * HEAD ** (-0.5)
            dq_ref[0, pl.ds(at, block), cols] = low(join_pair(grad_q, is_first))
        return carry

    lax.fori_loop(0, span // block, one_block, 0)
    dk_ref[0] = low(dk_acc[...])
    dv_ref[0] = low(dv_acc[...])


def attend_back(info, grad_branch, w4, queries, keys, values, log_totals, block):
    rows, span, local = queries.shape
    extent = keys.shape[1]
    model = grad_branch.shape[2]
    out_shape = [
        shape_of((rows, span, local), bf16),
        shape_of((rows, extent, local), bf16),
        shape_of((rows, extent, local), bf16),
    ]
    args = [grad_branch, w4, queries, keys, values, log_totals]
    in_specs = [lead_block(a) for a in args]
    in_specs[1] = pl.BlockSpec((1,) + tuple(w4.shape[1:]), lambda i, *_: (3, 0, 0))
    return call(
        functools.partial(attend_back_kernel, span, block),
        (rows,),
        in_specs,
        [lead_block(o) for o in out_shape],
        out_shape,
        args,
        scalars=(info,),
        scratch=[pltpu.VMEM((span, local), bf16), pltpu.VMEM((extent, local), f32), pltpu.VMEM((extent, local), f32)],
        flops=6 * rows * span * local * (model + 5 * (block + 2 * WINDOW)),
        moved=rows * extent * model * 8,
    )


def feed_kernel(last, x_ref, wi_ref, wo_ref, bi_ref, *refs):
    if last:
        part_ref, n_ref, live_ref, g1_ref, s1_ref, bo_ref, g2_ref, s2_ref = refs[:8]
        refs = refs[8:]
    act_ref, slope_ref = refs[:2]
    x = x_ref[...]
    units = wi_ref.shape[1]
    step = 512
    total = None
    for at in range(0, units, step):
        cols = slice(at, at + step)
        act, slope = gelu_parts(mul(x, wi_ref[:, cols]) + bi_ref[:, cols])
        act = low(act)
        act_ref[:, cols] = act
        slope_ref[:, cols] = low(slope)
        term = mul(act, wo_ref[cols, :])
        total = term if total is None else total + term
    if last:
        n2_ref, scale_ref, sent_ref = refs[2:]
        middle = n_ref[...] * g1_ref[...] + s1_ref[...]
        normal, scale = norm_parts(middle + part_ref[...] + total + bo_ref[...])
        n2_ref[...] = normal
        scale_ref[...] = jnp.broadcast_to(scale, scale_ref.shape)
        sent = (normal * g2_ref[...] + s2_ref[...]) * live_ref[:, :1]
        for c in range(sent_ref.shape[0]):
            sent_ref[c] = sent[:, c * PAIR : (c + 1) * PAIR]
    else:
        refs[2][...] = total


def feed(middle, w_inner, w_outer, b_inner, tile, tail=None):
    tokens, model = middle.shape
    units = w_inner.shape[1]
    args = [middle, w_inner, w_outer, b_inner]
    in_specs = [lead_block(middle, tile)] + [whole_block(a) for a in args[1:]]
    out_shape = [shape_of((tokens, units), bf16), shape_of((tokens, units), bf16)]
    if tail is None:
        out_shape += [shape_of((tokens, model), f32)]
    else:
        out_shape += [shape_of((tokens, model), f32), shape_of((tokens, PAIR), f32)]
        args += list(tail)
        in_specs += [lead_block(a, tile) for a in tail[:3]] + [whole_block(a) for a in tail[3:]]
    out_specs = [lead_block(o, tile) for o in out_shape]
    if tail is not None:
        out_shape.append(shape_of((model // PAIR, tokens, PAIR), f32))
        out_specs.append(chunk_block(out_shape[-1], tile))
    return call(
        functools.partial(feed_kernel, tail is not None),
        (tokens // tile,),
        in_specs,
        out_specs,
        out_shape,
        args,
        flops=4 * tokens * model * units * 1.5,
        moved=tokens * units * 8,
    )


def conv_kernel(mols, sent_ref, wc_ref, bc_ref, g3_ref, s3_ref, g2_ref, mg_ref, ml_ref, n2_ref, sc_ref, lv_ref,
                mol_ref, gc_ref, grp_ref, two_ref, feed_ref, vec_ref, back_ref):
    @pl.when(pl.program_id(0) == 0)
    def _():
        vec_ref[...] = jnp.zeros_like(vec_ref)

    chunks = range(sent_ref.shape[0])
    total = None
    for k in range(KERNEL):
        grouped = low(jnp.concatenate([sent_ref[c, pl.ds(k, mols, stride=KERNEL), :] for c in chunks], axis=1))
        grp_ref[k] = grouped
        term = mul(grouped, wc_ref[k])
        total = term if total is None else total + term
    value, slope = gelu_parts(total + bc_ref[...])
    normal, scale = norm_parts(value)
    alive = ml_ref[:, :1]
    cotangent = mg_ref[...].astype(f32) * alive
    mol_ref[...] = low((normal * g3_ref[...] + s3_ref[...]) * alive)
    grad = low(norm_back(cotangent * g3_ref[...], normal, scale) * slope)
    gc_ref[...] = grad
    for k in range(KERNEL):
        back = low(mul_t(grad, wc_ref[k])).astype(f32)
        for c in chunks:
            back_ref[c, pl.ds(k, mols, stride=KERNEL), :] = back[:, c * PAIR : (c + 1) * PAIR]
    masked = jnp.concatenate([back_ref[c] for c in chunks], axis=1) * lv_ref[:, :1]
    n2 = n2_ref[...]
    grad_two = norm_back(masked * g2_ref[...], n2, sc_ref[:, :1])
    two_ref[...] = grad_two
    feed_ref[...] = low(grad_two)
    vec_ref[...] += jnp.concatenate(
        [
            col_sum(grad.astype(f32)),
            col_sum(cotangent * normal),
            col_sum(cotangent),
            col_sum(masked * n2),
            col_sum(masked),
            col_sum(grad_two),
            jnp.zeros((2, grad_two.shape[1]), f32),
        ],
        axis=0,
    )


def conv(sent, w_conv, b_conv, gain_three, shift_three, gain_two, mol_grad, live_mols, n2, scale2, live, steps):
    chunks, tokens, _ = sent.shape
    model = chunks * PAIR
    tile = tokens // steps
    mols = tile // KERNEL
    all_mols = tokens // KERNEL
    args = [sent, w_conv, b_conv, gain_three, shift_three, gain_two, mol_grad, live_mols, n2, scale2, live]
    in_specs = (
        [chunk_block(sent, tile)]
        + [whole_block(a) for a in args[1:6]]
        + [lead_block(a, mols) for a in args[6:8]]
        + [lead_block(a, tile) for a in args[8:]]
    )
    out_shape = [
        shape_of((all_mols, model), bf16),
        shape_of((all_mols, model), bf16),
        shape_of((KERNEL, all_mols, model), bf16),
        shape_of((tokens, model), f32),
        shape_of((tokens, model), bf16),
        shape_of((8, model), f32),
    ]
    out_specs = [
        lead_block(out_shape[0], mols),
        lead_block(out_shape[1], mols),
        pl.BlockSpec((KERNEL, mols, model), lambda i, *_: (0, i, 0)),
        lead_block(out_shape[3], tile),
        lead_block(out_shape[4], tile),
        pl.BlockSpec((8, model), lambda i, *_: (0, 0)),
    ]
    return call(
        functools.partial(conv_kernel, mols),
        (steps,),
        in_specs,
        out_specs,
        out_shape,
        args,
        scratch=[pltpu.VMEM((chunks, tile, PAIR), f32)],
        flops=4 * tokens * model * model * 1.5,
        moved=tokens * model * 30,
    )


def conv_weight_kernel(side_ref, grp_ref, grad_ref, *refs):
    value = t_mul(grp_ref[0], grad_ref[...])
    if len(refs) == 2:
        value = value + refs[0][0].astype(f32)
    refs[-1][0] = low(value)


def conv_weight(side, grouped, grad, got=None):
    kernel, mols, model = grouped.shape
    half = kernel // 2
    args = [grouped, grad]
    in_specs = [pl.BlockSpec((1, mols, model), lambda i, side_ref: (side_ref[0] * half + i, 0, 0)), whole_block(grad)]
    out_shape = shape_of((half, model, model), bf16)
    if got is not None:
        args.append(got)
        in_specs.append(lead_block(got))
    return call(
        conv_weight_kernel,
        (half,),
        in_specs,
        lead_block(out_shape),
        out_shape,
        args,
        scalars=(side,),
        flops=2 * half * mols * model * model,
        moved=half * model * model * 8,
    )


def weight_kernel(side_ref, left_ref, *refs):
    rights, refs = refs[:2], refs[2:]
    for index in range(2):
        value = t_mul(left_ref[...], rights[index][...])
        if len(refs) == 2:
            value = value + refs[0][index].astype(f32)
        refs[-1][index] = low(value)


def weight(side, left, right_own, right_other, got=None, tile=512):
    tokens, model = left.shape
    columns = right_own.shape[1]
    half = model // 2
    args = [left, right_own, right_other]
    in_specs = [
        pl.BlockSpec((tokens, half), lambda i, side_ref: (0, side_ref[0])),
        pl.BlockSpec((tokens, tile), lambda i, *_: (0, i)),
        pl.BlockSpec((tokens, tile), lambda i, *_: (0, i)),
    ]
    out_shape = shape_of((2, half, columns), bf16)
    out_spec = pl.BlockSpec((2, half, tile), lambda i, *_: (0, 0, i))
    if got is not None:
        args.append(got)
        in_specs.append(out_spec)
    return call(
        weight_kernel,
        (columns // tile,),
        in_specs,
        out_spec,
        out_shape,
        args,
        scalars=(side,),
        flops=4 * tokens * half * columns,
        moved=tokens * columns * 4 + half * columns * 8,
    )


def project_weight_kernel(span, side_ref, x_ref, gb_ref, *refs):
    groups, refs = refs[:8], refs[8:]
    which = pl.program_id(0)
    rows = x_ref.shape[0]
    for index in range(2):

        @pl.when(which == index)
        def _(index=index):
            dq, dk, dv, att = groups[4 * index : 4 * index + 4]
            local = dq.shape[2]
            for place, right in enumerate((dq, dk, dv, att)):
                value = None
                for row in range(rows):
                    if place == 0:
                        left = x_ref[row, WINDOW : WINDOW + span]
                    elif place == 3:
                        left = gb_ref[row]
                    else:
                        left = x_ref[row]
                    term = t_mul(left, right[row])
                    value = term if value is None else value + term
                cols = slice(place * local, (place + 1) * local)
                if len(refs) == 2:
                    value = value + refs[0][0, :, cols].astype(f32)
                refs[-1][0, :, cols] = low(value)


def project_weight(side, x_ext, grad_branch, own, other, span, got=None):
    rows, extent, model = x_ext.shape
    half = model // 2
    local = own[0].shape[2]
    args = [x_ext, grad_branch, *own, *other]
    in_specs = [
        pl.BlockSpec((rows, extent, half), lambda i, side_ref: (0, 0, side_ref[0])),
        pl.BlockSpec((rows, span, half), lambda i, side_ref: (0, 0, side_ref[0])),
    ] + [whole_block(a) for a in args[2:]]
    out_shape = shape_of((2, half, 4 * local), bf16)
    if got is not None:
        args.append(got)
        in_specs.append(lead_block(got))
    return call(
        functools.partial(project_weight_kernel, span),
        (2,),
        in_specs,
        lead_block(out_shape),
        out_shape,
        args,
        scalars=(side,),
        flops=16 * rows * extent * half * local,
        moved=rows * extent * model * 12,
    )


def feed_back_kernel(gf_ref, two_ref, sl_own, sl_other, n_ref, sc_ref, wo_own, wo_other, wi_own, wi_other, g1_ref,
                     gh_own, gh_other, one_ref, gb_ref, vec_ref, bi_own, bi_other):
    @pl.when(pl.program_id(0) == 0)
    def _():
        vec_ref[...] = jnp.zeros_like(vec_ref)
        bi_own[...] = jnp.zeros_like(bi_own)
        bi_other[...] = jnp.zeros_like(bi_other)

    grad_feed = gf_ref[...]
    units = wo_own.shape[0]
    step = 512
    total = two_ref[...]
    for slope_ref, wo_ref, wi_ref, gh_ref, bi_ref in (
        (sl_own, wo_own, wi_own, gh_own, bi_own),
        (sl_other, wo_other, wi_other, gh_other, bi_other),
    ):
        for at in range(0, units, step):
            cols = slice(at, at + step)
            grad = low(mul_t(grad_feed, wo_ref[cols, :]) * slope_ref[:, cols].astype(f32))
            gh_ref[:, cols] = grad
            bi_ref[:1, cols] += col_sum(grad.astype(f32))
            total = total + mul_t(grad, wi_ref[:, cols])
    normal = n_ref[...]
    grad_one = norm_back(total * g1_ref[...], normal, sc_ref[:, :1])
    one_ref[...] = grad_one
    gb_ref[...] = low(grad_one)
    vec_ref[...] += jnp.concatenate(
        [col_sum(grad_one), col_sum(total * normal), col_sum(total), jnp.zeros((5, total.shape[1]), f32)], axis=0
    )


def feed_back(grad_feed, grad_two, slopes, n1, scale1, outers, inners, gain_one, tile):
    tokens, model = grad_feed.shape
    units = outers[0].shape[0]
    args = [grad_feed, grad_two, *slopes, n1, scale1, *outers, *inners, gain_one]
    in_specs = [lead_block(a, tile) for a in args[:6]] + [whole_block(a) for a in args[6:]]
    out_shape = [
        shape_of((tokens, units), bf16),
        shape_of((tokens, units), bf16),
        shape_of((tokens, model), f32),
        shape_of((tokens, model), bf16),
        shape_of((8, model), f32),
        shape_of((8, units), f32),
        shape_of((8, units), f32),
    ]
    out_specs = [lead_block(o, tile) for o in out_shape[:4]] + [
        pl.BlockSpec(o.shape, lambda i, *_: (0, 0)) for o in out_shape[4:]
    ]
    return call(
        feed_back_kernel,
        (tokens // tile,),
        in_specs,
        out_specs,
        out_shape,
        args,
        flops=8 * tokens * model * units * 1.2,
        moved=tokens * units * 8,
    )


def input_back_kernel(span, one_ref, *refs):
    groups, (own_w, other_w), (mid_ref, left_ref, right_ref, vec_ref) = refs[:6], refs[6:8], refs[8:]

    @pl.when(pl.program_id(0) == 0)
    def _():
        vec_ref[...] = jnp.zeros_like(vec_ref)

    total = None
    center = one_ref[0]
    sums = []
    for (dq, dk, dv), w_ref in ((groups[:3], own_w), (groups[3:], other_w)):
        center = center + mul_t(dq[0], w_ref[0])
        term = mul_t(dk[0], w_ref[1]) + mul_t(dv[0], w_ref[2])
        total = term if total is None else total + term
        sums.append(jnp.concatenate([col_sum(dq[0].astype(f32)), col_sum(dv[0].astype(f32))], axis=0))
    mid_ref[0] = center + total[WINDOW : WINDOW + span]
    left_ref[0] = low(total[:WINDOW])
    right_ref[0] = low(total[WINDOW + span :])
    rest = jnp.zeros((4, sums[0].shape[1]), f32)
    vec_ref[...] += jnp.concatenate(sums + [rest], axis=0)


def input_back(grad_one, own, other, w_own, w_other, span):
    rows, extent, local = own[1].shape
    model = grad_one.shape[2]
    args = [grad_one, *own, *other, w_own, w_other]
    in_specs = [lead_block(a) for a in args[:7]] + [whole_block(a) for a in args[7:]]
    out_shape = [
        shape_of((rows, span, model), f32),
        shape_of((rows, WINDOW, model), bf16),
        shape_of((rows, WINDOW, model), bf16),
        shape_of((8, local), f32),
    ]
    out_specs = [lead_block(o) for o in out_shape[:3]] + [pl.BlockSpec(out_shape[3].shape, lambda i, *_: (0, 0))]
    return call(
        functools.partial(input_back_kernel, span),
        (rows,),
        in_specs,
        out_specs,
        out_shape,
        args,
        flops=12 * rows * extent * model * local,
        moved=rows * extent * model * 12,
    )


def swapped(block, axis, bit=0):
    count = lax.axis_size(axis)
    return lax.ppermute(block, axis, [(i, i ^ (1 << bit)) for i in range(count)])


def from_chunk(block, distance):
    axes = ("seq", "mp")
    count = lax.axis_size("seq") * lax.axis_size("mp")
    return lax.ppermute(block, axes, [(i + distance, i) for i in range(count) if 0 <= i + distance < count])


def pick(array, index, dim):
    return lax.dynamic_index_in_dim(array, index, dim, keepdims=False)


def bits_of(axis):
    return lax.axis_size(axis).bit_length() - 1


def reduce_bit(parts, dim, axis, bit):
    mine = (lax.axis_index(axis) >> bit) & 1
    got = swapped(pick(parts, 1 - mine, dim), axis, bit)
    return low(pick(parts, mine, dim).astype(f32) + got.astype(f32))


def reduce_axis(parts, dim, axis):
    count = lax.axis_size(axis)
    for bit in range(bits_of(axis)):
        low_count = parts.shape[dim] // 2
        shaped = parts.reshape(parts.shape[:dim] + (low_count, 2) + parts.shape[dim + 1 :])
        parts = reduce_bit(shaped, dim + 1, axis, bit)
    return parts.reshape(parts.shape[:dim] + parts.shape[dim + 1 :])


def gather_quarters(quarter, shape):
    first = swapped(quarter, "mp")
    seq_bit = lax.axis_index("seq") & 1
    pipe = lax.axis_index("pipe")
    me = 2 * seq_bit + pipe
    second = swapped(first, "seq")
    third = swapped(jnp.stack([first, second]), "pipe")
    full = jnp.zeros((4,) + quarter.shape, quarter.dtype)
    for block, place in ((first, me), (second, me ^ 2), (third[0], me ^ 1), (third[1], me ^ 3)):
        full = lax.dynamic_update_slice_in_dim(full, block[None], place, 0)
    return full.reshape(shape)


def in_order(first, mine, recv, axis):
    return jnp.where(
        first == 0, jnp.concatenate([mine, recv], axis=axis), jnp.concatenate([recv, mine], axis=axis)
    )


def summed(vectors):
    return jnp.sum(lax.all_gather(vectors, ("pipe", "dp", "seq", "mp")), axis=0)


def on_device(
    characters,
    row_lengths,
    w_query,
    b_query,
    w_key,
    w_value,
    b_value,
    w_attn_out,
    b_attn_out,
    gain_one,
    shift_one,
    w_inner,
    b_inner,
    w_outer,
    b_outer,
    gain_two,
    shift_two,
    w_conv,
    b_conv,
    gain_three,
    shift_three,
    molecule_grad,
):
    pipe = lax.axis_index("pipe")
    seq = lax.axis_index("seq")
    mp = lax.axis_index("mp")
    all_rows, span, half_model = characters.shape
    rows = all_rows // 2
    model = 2 * half_model
    local = w_query.shape[1]
    units = w_inner.shape[1]
    tokens = rows * span
    mols = tokens // KERNEL
    block = min(WINDOW, span)
    tile = min(256, tokens)
    own_start = (seq * lax.axis_size("mp") + mp) * span

    def line(vector):
        return vector.astype(f32)[None, :]

    def rows_of(array, index):
        return lax.dynamic_slice_in_dim(array, index * rows, rows, 0)

    chars = in_order(pipe, rows_of(characters, pipe), swapped(rows_of(characters, 1 - pipe), "pipe"), 2)
    mol_grad = in_order(pipe, rows_of(molecule_grad, pipe), swapped(rows_of(molecule_grad, 1 - pipe), "pipe"), 2)
    mol_grad = mol_grad.reshape(mols, model)

    me = 2 * (seq & 1) + pipe
    w4 = jnp.stack([w_query, w_key, w_value, w_attn_out.T])
    w4_other = gather_quarters(pick(w4, me, 0), w4.shape)
    inner_other = gather_quarters(pick(w_inner.reshape(4, model // 4, units), me, 0), w_inner.shape)
    outer_other = gather_quarters(pick(w_outer.reshape(4, units // 4, model), me, 0), w_outer.shape)
    small = jnp.concatenate([b_query, b_value, b_inner]).astype(f32)[None, :]
    small_other = swapped(small, "mp")
    bq = (small[:, :local], small_other[:, :local])
    bv = (small[:, local : 2 * local], small_other[:, local : 2 * local])
    bi = (small[:, 2 * local :], small_other[:, 2 * local :])

    hops = -(-WINDOW // span)
    pieces = [chars]
    for hop in range(1, hops + 1):
        width = min(span, WINDOW - (hop - 1) * span)
        pieces.insert(0, from_chunk(chars[:, span - width :], -hop))
        pieces.append(from_chunk(chars[:, :width], hop))
    x_ext = jnp.concatenate(pieces, axis=1)

    lengths = rows_of(row_lengths, pipe)
    info = jnp.concatenate([own_start[None].astype(jnp.int32), lengths])
    positions = own_start + jnp.arange(span, dtype=jnp.int32)
    live = (positions[None, :] < lengths[:, None]).astype(f32).reshape(tokens, 1)
    live_mols = live.reshape(mols, KERNEL)[:, :1]
    live = jnp.broadcast_to(live, (tokens, PAIR))
    live_mols = jnp.broadcast_to(live_mols, (mols, PAIR))

    q_own, k_own, v_own, att_own, lse_own, part = attend(info, x_ext, w4, bq[0], bv[0], span, block)
    q_other, k_other, v_other, att_other, lse_other, n1, scale1, middle = attend(
        info, x_ext, w4_other, bq[1], bv[1], span, block, (part, line(b_attn_out), line(gain_one), line(shift_one))
    )
    n1, scale1, middle = (a.reshape(tokens, -1) for a in (n1, scale1, middle))
    act_own, slope_own, part = feed(middle, w_inner, w_outer, bi[0], tile)
    act_other, slope_other, n2, scale2, sent = feed(
        middle,
        inner_other,
        outer_other,
        bi[1],
        tile,
        (part, n1, live, line(gain_one), line(shift_one), line(b_outer), line(gain_two), line(shift_two)),
    )
    mol_out, grad_conv, grouped, grad_two, grad_feed, vec_conv = conv(
        sent,
        w_conv.reshape(KERNEL, model, model),
        line(b_conv),
        line(gain_three),
        line(shift_three),
        line(gain_two),
        mol_grad,
        live_mols,
        n2,
        scale2,
        live,
        2,
    )

    mine_side = pipe.astype(jnp.int32)[None]
    their_side = 1 - mine_side

    def over_pipe(product):
        return product(mine_side, swapped(product(their_side, None), "pipe"))

    dp_size, seq_size, mp_size = (lax.axis_size(a) for a in ("dp", "seq", "mp"))
    conv_part = over_pipe(lambda side, got: conv_weight(side, grouped, grad_conv, got))
    conv_part = conv_part.reshape(dp_size, seq_size, mp_size, -1, model)
    conv_part = reduce_axis(conv_part, 0, "dp")
    conv_part = reduce_axis(conv_part, 0, "seq")
    grad_w_conv = reduce_axis(conv_part, 0, "mp")

    outer_part = over_pipe(lambda side, got: weight(side, grad_feed, act_own, act_other, got))

    gh_own, gh_other, grad_one, grad_branch, vec_one, bi_own, bi_other = feed_back(
        grad_feed,
        grad_two,
        (slope_own, slope_other),
        n1,
        scale1,
        (w_outer, outer_other),
        (w_inner, inner_other),
        line(gain_one),
        tile,
    )
    inner_part = over_pipe(lambda side, got: weight(side, middle, gh_own, gh_other, got))

    def head_rows(part, axes):
        part = part.reshape(2, dp_size, seq_size, -1, part.shape[2])
        dims = ["mp", "dp", "seq"]
        for axis in axes:
            dim = dims.index(axis)
            if axis == "mp":
                part = low(part[0].astype(f32) + swapped(part[1], "mp").astype(f32))
            else:
                part = reduce_axis(part, dim, axis)
            dims.remove(axis)
        return part

    outer_sum = head_rows(outer_part, ("seq", "mp", "dp"))
    inner_sum = head_rows(inner_part, ("mp", "seq", "dp"))

    grad_branch = grad_branch.reshape(rows, span, model)
    grad_one = grad_one.reshape(rows, span, model)
    back_other = attend_back(info, grad_branch, w4_other, q_other, k_other, v_other, lse_other, block)
    back_own = attend_back(info, grad_branch, w4, q_own, k_own, v_own, lse_own, block)
    head_part = over_pipe(
        lambda side, got: project_weight(
            side, x_ext, grad_branch, (*back_own, att_own), (*back_other, att_other), span, got
        )
    )
    head_sum = head_rows(head_part, ("mp", "seq", "dp"))
    center, left, right, vec_late = input_back(grad_one, back_own, back_other, w4, w4_other, span)

    for hop in range(1, hops + 1):
        width = min(span, WINDOW - (hop - 1) * span)
        top = WINDOW - (hop - 1) * span
        to_tail = from_chunk(left[:, top - width : top], hop).astype(f32)
        to_head = from_chunk(right[:, WINDOW - top : WINDOW - top + width], -hop).astype(f32)
        pad = ((0, 0), (0, span - width), (0, 0))
        center = center + jnp.pad(to_head, pad) + jnp.pad(to_tail, (pad[0], pad[1][::-1], pad[2]))
    center = center.reshape(rows, span, 2, half_model)
    chars_got = swapped(low(pick(center, 1 - pipe, 2)), "pipe").astype(f32)
    chars_grad = in_order(pipe, pick(center, pipe, 2), chars_got, 0)
    mol_out = mol_out.reshape(rows, span // KERNEL, 2, half_model)
    mol_got = swapped(pick(mol_out, 1 - pipe, 2), "pipe")
    molecules = in_order(pipe, pick(mol_out, pipe, 2), mol_got, 0)

    inner_vec = in_order(mp, bi_own[:1], bi_other[:1], 1).reshape(-1, model)
    early = summed(jnp.concatenate([vec_conv[:6], vec_one[:3], inner_vec], axis=0))
    late = summed(in_order(mp, vec_late[:2], vec_late[2:4], 1))
    grad_b_conv, grad_gain_three, grad_shift_three, grad_gain_two, grad_shift_two, grad_b_outer = early[:6]
    grad_b_attn_out, grad_gain_one, grad_shift_one = early[6:9]
    grad_b_inner = early[9:].reshape(-1)

    head_sum = head_sum.astype(f32)
    grad_w_query, grad_w_key, grad_w_value, grad_w_attn = (
        head_sum[:, i * local : (i + 1) * local] for i in range(4)
    )
    return (
        molecules,
        chars_grad,
        grad_w_query,
        late[0],
        grad_w_key,
        grad_w_value,
        late[1],
        grad_w_attn.T,
        grad_b_attn_out,
        grad_gain_one,
        grad_shift_one,
        inner_sum.astype(f32),
        grad_b_inner,
        outer_sum.astype(f32).T,
        grad_b_outer,
        grad_gain_two,
        grad_shift_two,
        grad_w_conv.astype(f32),
        grad_b_conv,
        grad_gain_three,
        grad_shift_three,
    )


def solution(mesh):
    return jax.shard_map(
        on_device,
        mesh=mesh,
        in_specs=(
            P("dp", ("seq", "mp"), "pipe"),
            P("dp"),
            P(None, "mp"),
            P("mp"),
            P(None, "mp"),
            P(None, "mp"),
            P("mp"),
            P("mp", None),
            P(),
            P(),
            P(),
            P(None, "mp"),
            P("mp"),
            P("mp", None),
            P(),
            P(),
            P(),
            P(),
            P(),
            P(),
            P(),
            P("dp", ("seq", "mp"), "pipe"),
        ),
        out_specs=(
            P("dp", ("seq", "mp"), "pipe"),
            P("dp", ("seq", "mp"), "pipe"),
            P(("pipe", "dp", "seq"), "mp"),
            P(),
            P(("pipe", "dp", "seq"), "mp"),
            P(("pipe", "dp", "seq"), "mp"),
            P(),
            P("mp", ("pipe", "dp", "seq")),
            P(),
            P(),
            P(),
            P(("pipe", "dp", "seq"), "mp"),
            P(),
            P("mp", ("pipe", "dp", "seq")),
            P(),
            P(),
            P(),
            P(("pipe", "dp", "seq", "mp"), None),
            P(),
            P(),
            P(),
        ),
        check_vma=False,
    )
```

```python
import functools

import jax
import jax.numpy as jnp
from jax import lax
from jax.experimental import pallas as pl
from jax.experimental.pallas import tpu as pltpu
from jax.sharding import PartitionSpec as P

HEAD = 64
WINDOW = 128
KERNEL = 4
PAIR = 2 * HEAD
VMEM_LIMIT = 20 << 20
FAR = True
COST = 1000
PARTS = 1

epsilon = 1e-05
masked_score = -1e30
f32 = jnp.float32
bf16 = jnp.bfloat16


def mul(left, right):
    return jnp.dot(left, right, preferred_element_type=f32)


def mul_t(left, right):
    return lax.dot_general(left, right, (((1,), (1,)), ((), ())), preferred_element_type=f32)


def t_mul(left, right):
    return lax.dot_general(left, right, (((0,), (0,)), ((), ())), preferred_element_type=f32)


def gelu_parts(value):
    cdf = 0.5 + 0.5 * lax.erf(value * 2.0**-0.5)
    return value * cdf, cdf + value * jnp.exp(value * value * -0.5) * 0.3989422804014327


def norm_parts(value):
    centered = value - jnp.mean(value, axis=-1, keepdims=True)
    scale = lax.rsqrt(jnp.mean(centered * centered, axis=-1, keepdims=True) + epsilon)
    return centered * scale, scale


def norm_back(cotangent, normal, scale):
    first = jnp.mean(cotangent, axis=-1, keepdims=True)
    second = jnp.mean(cotangent * normal, axis=-1, keepdims=True)
    return scale * (cotangent - first - normal * second)


def col_sum(value):
    return jnp.sum(value, axis=0, keepdims=True)


def low(value):
    return value.astype(bf16)


START, PIPE, QUARTER, DP, MP, LENGTHS = range(6)


def call(body, grid, in_specs, out_specs, out_shape, args, info, scratch=(), flops=0, moved=0, limit=VMEM_LIMIT, kept=()):
    if FAR:
        if isinstance(out_shape, list):
            out_shape = [far_shape(o.shape, o.dtype) if i in kept else o for i, o in enumerate(out_shape)]
    return pl.pallas_call(
        body,
        grid_spec=pltpu.PrefetchScalarGridSpec(
            num_scalar_prefetch=1,
            grid=grid,
            in_specs=in_specs,
            out_specs=out_specs,
            scratch_shapes=scratch,
        ),
        out_shape=out_shape,
        compiler_params=pltpu.CompilerParams(vmem_limit_bytes=limit),
        cost_estimate=pl.CostEstimate(flops=int(flops) // COST, bytes_accessed=int(moved) // COST, transcendentals=0),
    )(info, *args)


def whole_block(array):
    zeros = (0,) * array.ndim
    return pl.BlockSpec(array.shape, lambda *_: zeros, pipeline_mode=pl.Buffered(1))


def lead_block(array, size=1):
    rest = (0,) * (array.ndim - 1)
    return pl.BlockSpec((size,) + tuple(array.shape[1:]), lambda i, *_: (i,) + rest)


def core_block(array, steps, size=1):
    rest = (0,) * (array.ndim - 1)
    return pl.BlockSpec((size,) + tuple(array.shape[1:]), lambda i, info: (info[PIPE] * steps + i,) + rest)


def chunk_block(array, size):
    return pl.BlockSpec((array.shape[0], size, array.shape[2]), lambda i, *_: (0, i, 0))


def fixed_block(array):
    zeros = (0,) * array.ndim
    return pl.BlockSpec(array.shape, lambda *_: zeros)


ANYWHERE = pl.BlockSpec(memory_space=pl.ANY)


def far(array):
    return pltpu.with_memory_space_constraint(array, pltpu.HBM) if FAR else array


def far_shape(dims, kind):
    return pltpu.HBM(tuple(dims), kind)


def shape_of(dims, kind):
    return jax.ShapeDtypeStruct(tuple(dims), kind)


def fetch(plan, sems):
    copies = [pltpu.make_async_copy(source, target, sems.at[i]) for i, (source, target) in enumerate(plan)]
    for copy in copies:
        copy.start()
    return copies


def placed(info_ref, index, size):
    return pl.ds(pl.multiple_of((info_ref[QUARTER] ^ (0, 2, 1, 3)[index]) * size, size), size)


def plan_square(info_ref, pieces, targets):
    size = targets[0].shape[0] // 4
    return [
        (piece.at[pl.ds(which * size, size)], target.at[placed(info_ref, i, size)])
        for i, piece in enumerate(pieces)
        for which, target in enumerate(targets)
    ]


def plan_inner(info_ref, pieces, target):
    size = target.shape[0] // 4
    return [(piece.at[pl.ds(0, size)], target.at[placed(info_ref, i, size)]) for i, piece in enumerate(pieces)]


def plan_outer(info_ref, pieces, target):
    size = target.shape[0] // 4
    return [(piece, target.at[placed(info_ref, i, size)]) for i, piece in enumerate(pieces)]


def plan_attn_out(info_ref, pieces, target):
    model = target.shape[1]
    size = target.shape[0] // 4
    columns = model // 2
    return [
        (
            piece.at[pl.ds(piece.shape[0] - 16 - (2 - side) * size, size)],
            target.at[placed(info_ref, i, size), pl.ds(side * columns, columns)],
        )
        for i, piece in enumerate(pieces)
        for side in range(2)
    ]


def pack_kernel(plan_of, info_ref, *refs):
    sems = refs[-1]
    for copy in fetch(plan_of(info_ref, *refs[:-1]), sems):
        copy.wait()


def pack(info, plan_of, args, out_shape, copies):
    return call(
        functools.partial(pack_kernel, plan_of),
        (1,),
        [ANYWHERE] * len(args),
        [fixed_block(o) for o in out_shape],
        out_shape,
        [far(a) for a in args],
        info,
        scratch=[pltpu.SemaphoreType.DMA((copies,))],
        moved=sum(o.size * 4 for o in out_shape),
    )


def gather_small_kernel(bq, bv, bi, *refs):
    vectors, (bias_ref, vec_ref) = refs[:-2], refs[-2:]
    local = bias_ref.shape[1]
    rows = [bq[...].reshape(1, local), bv[...].reshape(1, local)]
    inner = bi[...].reshape(1, -1)
    rows += [inner[:, i * local : (i + 1) * local] for i in range(inner.shape[1] // local)]
    rows = [row.astype(f32) for row in rows]
    rows.append(jnp.zeros((16 - len(rows), local), f32))
    bias_ref[...] = low(jnp.concatenate(rows, axis=0))
    rows = [v[...].reshape(1, -1).astype(f32) for v in vectors]
    rows.append(jnp.zeros((16 - len(rows), vec_ref.shape[1]), f32))
    vec_ref[...] = jnp.concatenate(rows, axis=0)


def gather_small(b_query, b_value, b_inner, vectors):
    return pl.pallas_call(
        gather_small_kernel,
        out_shape=[shape_of((16, b_query.shape[0]), bf16), shape_of((16, vectors[0].shape[0]), f32)],
    )(b_query, b_value, b_inner, *vectors)


def inner_bias(bias_ref, units):
    local = bias_ref.shape[1]
    return jnp.concatenate([bias_ref[2 + i : 3 + i] for i in range(units // local)], axis=1).astype(f32)


def quarter_of(info_ref, array):
    size = array.shape[0] // 4
    return pl.ds(pl.multiple_of(info_ref[QUARTER] * size, size), size)


def pack_first(info, weights, w_out, biases):
    model, local = weights[0].shape
    size, out_size, half = model // 4, w_out.shape[0] // 4, w_out.shape[1] // 2

    def plan_of(info_ref, wq, wk, wv, wo, bias, packet):
        plan = [(bias, packet.at[pl.ds(3 * size + 2 * out_size, 16)])]
        plan += [
            (w.at[quarter_of(info_ref, w)], packet.at[pl.ds(i * size, size)]) for i, w in enumerate((wq, wk, wv))
        ]
        return plan + [
            (
                wo.at[quarter_of(info_ref, wo), pl.ds(side * half, half)],
                packet.at[pl.ds(3 * size + side * out_size, out_size)],
            )
            for side in range(2)
        ]

    out_shape = [shape_of((3 * size + 2 * out_size + 16, local), bf16)]
    return pack(info, plan_of, [*weights, w_out, biases], out_shape, 6)[0]


def pack_second(info, w_inner, w_outer, characters, molecule_grad):
    rows = characters.shape[0] // 2

    def plan_of(info_ref, wi, wo, chars, mols, inner, outer, center, mol_center):
        theirs = pl.ds((1 - info_ref[PIPE]) * rows, rows)
        return [
            (wi.at[quarter_of(info_ref, wi)], inner),
            (wo.at[quarter_of(info_ref, wo)], outer),
            (chars.at[theirs], center),
            (mols.at[theirs], mol_center),
        ]

    out_shape = [shape_of((a.shape[0] // 4, a.shape[1]), bf16) for a in (w_inner, w_outer)]
    out_shape += [shape_of((rows,) + tuple(a.shape[1:]), bf16) for a in (characters, molecule_grad)]
    return pack(info, plan_of, [w_inner, w_outer, characters, molecule_grad], out_shape, 4)


def pair_lanes(rows):
    return lax.broadcasted_iota(jnp.int32, (rows, PAIR), 1) < HEAD


def split_pair(both, is_first):
    zero = jnp.zeros_like(both)
    return jnp.concatenate([jnp.where(is_first, both, zero), jnp.where(is_first, zero, both)], axis=0)


def join_pair(stacked, is_first):
    rows = stacked.shape[0] // 2
    return jnp.where(is_first, stacked[:rows], stacked[rows:])


def attend_kernel(span, block, last, info_ref, *refs):
    first_step = pl.program_id(0) == 0
    if last:
        x_ref, bias_ref, part_ref, vec_ref = refs[:4]
        pieces, refs = refs[4:8], refs[8:]
        q_ref, k_ref, v_ref, att_ref, lse_ref, n_ref, s_ref, mid_ref, wq_ref, wk_ref, wv_ref, wo_ref, sems = refs

        @pl.when(first_step)
        def _():
            plan = plan_square(info_ref, pieces, (wq_ref, wk_ref, wv_ref)) + plan_attn_out(info_ref, pieces, wo_ref)
            for copy in fetch(plan, sems):
                copy.wait()

    else:
        center, center_got, left, right, rims_got, wq_ref, wk_ref, wv_ref, wo_ref, bias_ref = refs[:10]
        q_ref, k_ref, v_ref, att_ref, lse_ref, part_ref, x_ref = refs[10:]
        half = center.shape[2]

        def place(mine, got):
            x_ref[0, :WINDOW, mine] = left[0]
            x_ref[0, :WINDOW, got] = rims_got[0, 0]
            x_ref[0, WINDOW : WINDOW + span, mine] = center[0]
            x_ref[0, WINDOW : WINDOW + span, got] = center_got[0]
            x_ref[0, WINDOW + span :, mine] = right[0]
            x_ref[0, WINDOW + span :, got] = rims_got[1, 0]

        lower, upper = slice(0, half), slice(half, 2 * half)
        pl.when(info_ref[PIPE] == 0)(lambda: place(lower, upper))
        pl.when(info_ref[PIPE] == 1)(lambda: place(upper, lower))

    length = info_ref[LENGTHS + pl.program_id(0)]
    start = info_ref[START]
    width = block + 2 * WINDOW
    pairs = q_ref.shape[2] // PAIR
    x = x_ref[0]
    own = x_ref[0, WINDOW : WINDOW + span]
    q_ref[0] = low(low(mul(own, wq_ref[...]) + bias_ref[0:1].astype(f32)).astype(f32) * HEAD ** (-0.5))
    k_ref[0] = low(mul(x, wk_ref[...]))
    v_ref[0] = low(mul(x, wv_ref[...]) + bias_ref[1:2].astype(f32))
    is_first = pair_lanes(block)
    q_at = lax.broadcasted_iota(jnp.int32, (block, width), 0)
    k_at = lax.broadcasted_iota(jnp.int32, (block, width), 1) - WINDOW
    in_window = jnp.abs(q_at - k_at) < WINDOW
    lanes = lax.broadcasted_iota(jnp.int32, (block, PAIR), 1)

    def one_block(index, carry):
        at = pl.multiple_of(index * block, block)
        position = k_at + (start + at)
        bias = jnp.where(in_window & (position >= 0) & (position < length), 0.0, masked_score)
        bias = jnp.concatenate([bias, bias], axis=0)
        totals = jnp.zeros((block, PAIR), f32)
        for pair in range(pairs):
            cols = slice(pair * PAIR, (pair + 1) * PAIR)
            q2 = split_pair(q_ref[0, pl.ds(at, block), cols], is_first)
            scores = mul_t(q2, k_ref[0, pl.ds(at, width), cols]) + bias
            top = jnp.max(scores, axis=-1, keepdims=True)
            weights = jnp.exp(scores - top)
            total = jnp.sum(weights, axis=-1, keepdims=True)
            out = mul(low(weights), v_ref[0, pl.ds(at, width), cols]) * (1.0 / total)
            att_ref[0, pl.ds(at, block), cols] = low(join_pair(out, is_first))
            log_total = top + jnp.log(total)
            totals = jnp.where(lanes == 2 * pair, log_total[:block], totals)
            totals = jnp.where(lanes == 2 * pair + 1, log_total[block:], totals)
        lse_ref[0, index] = totals.T[:8]
        return carry

    lax.fori_loop(0, span // block, one_block, 0, unroll=True)
    branch = mul(att_ref[0], wo_ref[...])
    if last:
        before = own.astype(f32) + part_ref[0] + branch + vec_ref[0:1]
        normal, scale = norm_parts(before)
        n_ref[0] = normal
        s_ref[0] = jnp.broadcast_to(scale, s_ref.shape[1:])
        mid_ref[0] = low(normal * vec_ref[1:2] + vec_ref[2:3])
    else:
        part_ref[0] = branch


def attend_shapes(rows, span, extent, local, block):
    return [
        shape_of((rows, span, local), bf16),
        shape_of((rows, extent, local), bf16),
        shape_of((rows, extent, local), bf16),
        shape_of((rows, span, local), bf16),
        shape_of((rows, span // block, 8, block), f32),
    ]


def attend_cost(rows, span, extent, local, model, block):
    flops = 2 * rows * local * (model * (2 * span + 2 * extent) + span * 4 * (block + 2 * WINDOW))
    return dict(flops=3 * flops, moved=rows * extent * model * 8)


def attend_own(info, x_parts, weights, biases, span, block):
    center, center_got, left, right, rims_got = x_parts
    rows, _, half = center_got.shape
    model, local = weights[0].shape
    extent = span + 2 * WINDOW
    out_shape = attend_shapes(rows, span, extent, local, block) + [
        shape_of((rows, span, model), f32),
        shape_of((rows, extent, model), bf16),
    ]
    args = [*map(far, (center, center_got, left, right, rims_got, *weights)), biases]
    in_specs = [
        core_block(center, rows),
        lead_block(center_got),
        core_block(left, rows),
        core_block(right, rows),
        pl.BlockSpec((2, 1, WINDOW, half), lambda i, *_: (0, i, 0, 0)),
    ] + [whole_block(a) for a in args[5:]]
    return call(
        functools.partial(attend_kernel, span, block, False),
        (rows,),
        in_specs,
        [lead_block(o) for o in out_shape],
        out_shape,
        args,
        info,
        kept=(0, 1, 2, 3, 4, 5, 6),
        **attend_cost(rows, span, extent, local, model, block),
    )


def attend_other(info, x_ext, pieces, biases, part, vectors, span, block):
    rows, extent, model = x_ext.shape
    local = biases.shape[1]
    out_shape = attend_shapes(rows, span, extent, local, block) + [
        shape_of((rows, span, model), f32),
        shape_of((rows, span, PAIR), f32),
        shape_of((rows, span, model), bf16),
    ]
    args = [far(x_ext), biases, far(part), vectors, *map(far, pieces)]
    in_specs = [
        lead_block(x_ext),
        whole_block(biases),
        lead_block(part),
        whole_block(vectors),
    ] + [ANYWHERE] * 4
    return call(
        functools.partial(attend_kernel, span, block, True),
        (rows,),
        in_specs,
        [lead_block(o) for o in out_shape],
        out_shape,
        args,
        info,
        scratch=[pltpu.VMEM((model, local), bf16)] * 3
        + [pltpu.VMEM((local, model), bf16), pltpu.SemaphoreType.DMA((20,))],
        kept=(0, 1, 2, 3, 4, 5, 6),
        **attend_cost(rows, span, extent, local, model, block),
    )


def attend_back_kernel(span, block, other, info_ref, gb_ref, q_ref, k_ref, v_ref, lse_ref, *refs):
    first_step = pl.program_id(0) == 0
    if other:
        pieces, refs = refs[:4], refs[4:]
        dq_ref, dk_ref, dv_ref, vec_ref, ga_ref, dk_acc, dv_acc, wo_ref, sems = refs

        @pl.when(first_step)
        def _():
            for copy in fetch(plan_attn_out(info_ref, pieces, wo_ref), sems):
                copy.wait()

    else:
        wo_ref, *vecs, dq_ref, dk_ref, dv_ref, all_ref, ga_ref, dk_acc, dv_acc, vec_ref = refs

    @pl.when(first_step)
    def _():
        vec_ref[...] = jnp.zeros_like(vec_ref)

    length = info_ref[LENGTHS + pl.program_id(0)]
    start = info_ref[START]
    width = block + 2 * WINDOW
    pairs = q_ref.shape[2] // PAIR
    ga_ref[...] = low(mul_t(gb_ref[0], wo_ref[...]))
    dk_acc[...] = jnp.zeros_like(dk_acc)
    dv_acc[...] = jnp.zeros_like(dv_acc)
    is_first = pair_lanes(block)
    q_at = lax.broadcasted_iota(jnp.int32, (width, block), 1)
    k_at = lax.broadcasted_iota(jnp.int32, (width, block), 0) - WINDOW
    in_window = jnp.abs(q_at - k_at) < WINDOW

    def one_block(index, carry):
        at = pl.multiple_of(index * block, block)
        position = k_at + (start + at)
        bias = jnp.where(in_window & (position >= 0) & (position < length), 0.0, masked_score)
        bias = jnp.concatenate([bias, bias], axis=1)
        for pair in range(pairs):
            cols = slice(pair * PAIR, (pair + 1) * PAIR)
            keys = k_ref[0, pl.ds(at, width), cols]
            q2 = split_pair(q_ref[0, pl.ds(at, block), cols], is_first)
            g2 = split_pair(ga_ref[pl.ds(at, block), cols], is_first)
            log_total = jnp.concatenate(
                [lse_ref[0, index, 2 * pair : 2 * pair + 1], lse_ref[0, index, 2 * pair + 1 : 2 * pair + 2]], axis=1
            )
            probs = jnp.exp(mul_t(keys, q2) + bias - log_total)
            grad_probs = mul_t(v_ref[0, pl.ds(at, width), cols], g2)
            inner = jnp.sum(probs * grad_probs, axis=0, keepdims=True)
            grad_scores = low(probs * (grad_probs - inner))
            dk_acc[pl.ds(at, width), cols] += mul(grad_scores, q2)
            dv_acc[pl.ds(at, width), cols] += mul(low(probs), g2)
            grad_q = t_mul(grad_scores, keys) * HEAD ** (-0.5)
            dq_ref[0, pl.ds(at, block), cols] = low(join_pair(grad_q, is_first))
        return carry

    lax.fori_loop(0, span // block, one_block, 0, unroll=True)
    dk_ref[0] = low(dk_acc[...])
    grad_values = low(dv_acc[...])
    dv_ref[0] = grad_values
    vec_ref[0:1] += col_sum(dq_ref[0].astype(f32))
    vec_ref[1:2] += col_sum(grad_values.astype(f32))
    if other:
        return

    vec_conv, vec_one, inner_own, inner_other, vec_other = vecs
    local = q_ref.shape[2]
    model = vec_one.shape[1]

    def collect(first, second, inner_first, inner_second):
        all_ref[...] = jnp.zeros_like(all_ref)
        all_ref[0:6, :model] = vec_conv[0:6]
        all_ref[6:9, :model] = vec_one[0:3]
        all_ref[0:2, model : model + local] = first[0:2]
        all_ref[0:2, model + local :] = second[0:2]
        all_ref[9:10] = inner_first[0:1]
        all_ref[10:11] = inner_second[0:1]

    last_step = pl.program_id(0) == pl.num_programs(0) - 1
    pl.when(last_step & (info_ref[MP] == 0))(lambda: collect(vec_ref, vec_other, inner_own, inner_other))
    pl.when(last_step & (info_ref[MP] == 1))(lambda: collect(vec_other, vec_ref, inner_other, inner_own))


def attend_back(info, grad_branch, queries, keys, values, log_totals, w_out, block, vecs=None):
    rows, span, local = queries.shape
    extent = keys.shape[1]
    model = grad_branch.shape[2]
    other = isinstance(w_out, (list, tuple))
    out_shape = [
        shape_of((rows, span, local), bf16),
        shape_of((rows, extent, local), bf16),
        shape_of((rows, extent, local), bf16),
        shape_of((8, local) if other else (16, 2 * model), f32),
    ]
    args = [grad_branch, *map(far, (queries, keys, values, log_totals))]
    in_specs = [lead_block(a) for a in args]
    scratch = [pltpu.VMEM((span, local), bf16), pltpu.VMEM((extent, local), f32), pltpu.VMEM((extent, local), f32)]
    if other:
        args += list(map(far, w_out))
        in_specs += [ANYWHERE] * 4
        scratch += [pltpu.VMEM((local, model), bf16), pltpu.SemaphoreType.DMA((8,))]
    else:
        args += [far(w_out), *vecs]
        in_specs += [whole_block(a) for a in args[5:]]
        scratch += [pltpu.VMEM((8, local), f32)]
    return call(
        functools.partial(attend_back_kernel, span, block, other),
        (rows,),
        in_specs,
        [lead_block(o) for o in out_shape[:3]] + [fixed_block(out_shape[3])],
        out_shape,
        args,
        info,
        scratch=scratch,
        flops=6 * rows * span * local * (model + 5 * (block + 2 * WINDOW)),
        moved=rows * extent * model * 8,
    )


B_ATTN, GAIN_ONE, SHIFT_ONE, B_OUTER, GAIN_TWO, SHIFT_TWO, B_CONV, GAIN_THREE, SHIFT_THREE = range(9)


def feed_kernel(last, info_ref, x_ref, bi_ref, *refs):
    if last:
        part_ref, n_ref, live_ref, vec_ref = refs[:4]
        inner_pieces, outer_pieces, refs = refs[4:8], refs[8:12], refs[12:]
        act_ref, slope_ref, n2_ref, scale_ref, sent_ref, wi_ref, wo_ref, sems = refs

        @pl.when(pl.program_id(0) == 0)
        def _():
            plan = plan_inner(info_ref, inner_pieces, wi_ref) + plan_outer(info_ref, outer_pieces, wo_ref)
            for copy in fetch(plan, sems):
                copy.wait()

    else:
        wi_ref, wo_ref, act_ref, slope_ref, part_ref = refs
    x = x_ref[...]
    units = wi_ref.shape[1]
    bias = inner_bias(bi_ref, units)
    step = 512
    total = None
    for at in range(0, units, step):
        cols = slice(at, at + step)
        act, slope = gelu_parts(mul(x, wi_ref[:, cols]) + bias[:, cols])
        act = low(act)
        act_ref[:, cols] = act
        slope_ref[:, cols] = low(slope)
        term = mul(act, wo_ref[cols, :])
        total = term if total is None else total + term
    if last:
        middle = n_ref[...] * vec_ref[GAIN_ONE : GAIN_ONE + 1] + vec_ref[SHIFT_ONE : SHIFT_ONE + 1]
        normal, scale = norm_parts(middle + part_ref[...] + total + vec_ref[B_OUTER : B_OUTER + 1])
        n2_ref[...] = normal
        scale_ref[...] = jnp.broadcast_to(scale, scale_ref.shape)
        sent = (normal * vec_ref[GAIN_TWO : GAIN_TWO + 1] + vec_ref[SHIFT_TWO : SHIFT_TWO + 1]) * live_ref[:, :1]
        for c in range(sent_ref.shape[0]):
            sent_ref[c] = sent[:, c * PAIR : (c + 1) * PAIR]
    else:
        part_ref[...] = total


def feed(info, middle, biases, units, tile, w_inner=None, w_outer=None, tail=None, pieces=None):
    tokens, model = middle.shape
    args = [middle, biases]
    in_specs = [lead_block(middle, tile), whole_block(biases)]
    out_shape = [shape_of((tokens, units), bf16), shape_of((tokens, units), bf16), shape_of((tokens, model), f32)]
    scratch = []
    if tail is None:
        args += [far(w_inner), far(w_outer)]
        in_specs += [whole_block(w_inner), whole_block(w_outer)]
        out_specs = [lead_block(o, tile) for o in out_shape]
    else:
        out_shape += [shape_of((tokens, PAIR), f32), shape_of((model // PAIR, tokens, PAIR), f32)]
        args += [tail[0], *map(far, tail[1:3]), tail[3], *map(far, pieces)]
        in_specs += [lead_block(a, tile) for a in tail[:3]] + [whole_block(tail[3])] + [ANYWHERE] * 8
        out_specs = [lead_block(o, tile) for o in out_shape[:4]] + [chunk_block(out_shape[4], tile)]
        scratch = [pltpu.VMEM((model, units), bf16), pltpu.VMEM((units, model), bf16), pltpu.SemaphoreType.DMA((8,))]
    return call(
        functools.partial(feed_kernel, tail is not None),
        (tokens // tile,),
        in_specs,
        out_specs,
        out_shape,
        args,
        info,
        scratch=scratch,
        kept=(0, 1),
        flops=4 * tokens * model * units * 1.5,
        moved=tokens * units * 8,
    )


def conv_kernel(mols, info_ref, sent_ref, wc_ref, vecs_ref, mg_ref, mg_got_ref, ml_ref, n2_ref, sc_ref, lv_ref,
                mol_ref, mol_out_ref, gc_ref, grp_ref, two_ref, feed_ref, vec_ref, back_ref, mg_all):
    @pl.when(pl.program_id(0) == 0)
    def _():
        vec_ref[...] = jnp.zeros_like(vec_ref)

    half = mg_ref.shape[1]
    lower, upper = slice(0, half), slice(half, 2 * half)

    def place(mine, got):
        mg_all[:, mine] = mg_ref[...]
        mg_all[:, got] = mg_got_ref[...]

    pl.when(info_ref[PIPE] == 0)(lambda: place(lower, upper))
    pl.when(info_ref[PIPE] == 1)(lambda: place(upper, lower))

    def vector(index):
        return vecs_ref[index : index + 1]

    chunks = range(sent_ref.shape[0])
    total = None
    for k in range(KERNEL):
        grouped = low(jnp.concatenate([sent_ref[c, pl.ds(k, mols, stride=KERNEL), :] for c in chunks], axis=1))
        grp_ref[k] = grouped
        term = mul(grouped, wc_ref[k])
        total = term if total is None else total + term
    value, slope = gelu_parts(total + vector(B_CONV))
    normal, scale = norm_parts(value)
    alive = ml_ref[:, :1]
    cotangent = mg_all[...].astype(f32) * alive
    molecules = low((normal * vector(GAIN_THREE) + vector(SHIFT_THREE)) * alive)

    def split(mine, got):
        mol_ref[...] = molecules[:, mine]
        mol_out_ref[...] = molecules[:, got]

    pl.when(info_ref[PIPE] == 0)(lambda: split(lower, upper))
    pl.when(info_ref[PIPE] == 1)(lambda: split(upper, lower))
    grad = low(norm_back(cotangent * vector(GAIN_THREE), normal, scale) * slope)
    gc_ref[...] = grad
    for k in range(KERNEL):
        back = low(mul_t(grad, wc_ref[k])).astype(f32)
        for c in chunks:
            back_ref[c, pl.ds(k, mols, stride=KERNEL), :] = back[:, c * PAIR : (c + 1) * PAIR]
    masked = jnp.concatenate([back_ref[c] for c in chunks], axis=1) * lv_ref[:, :1]
    n2 = n2_ref[...]
    grad_two = norm_back(masked * vector(GAIN_TWO), n2, sc_ref[:, :1])
    two_ref[...] = grad_two
    feed_ref[...] = low(grad_two)
    vec_ref[...] += jnp.concatenate(
        [
            col_sum(grad.astype(f32)),
            col_sum(cotangent * normal),
            col_sum(cotangent),
            col_sum(masked * n2),
            col_sum(masked),
            col_sum(grad_two),
            jnp.zeros((2, grad_two.shape[1]), f32),
        ],
        axis=0,
    )


def conv(info, sent, w_conv, vectors, mol_grad, mol_got, live_mols, n2, scale2, live, steps):
    chunks, tokens, _ = sent.shape
    model = chunks * PAIR
    tile = tokens // steps
    mols = tile // KERNEL
    all_mols = tokens // KERNEL
    args = [sent, far(w_conv), vectors, far(mol_grad), far(mol_got), far(live_mols), n2, scale2, far(live)]
    in_specs = (
        [chunk_block(sent, tile), whole_block(w_conv), whole_block(vectors), core_block(mol_grad, steps, mols)]
        + [lead_block(a, mols) for a in args[4:6]]
        + [lead_block(a, tile) for a in args[6:]]
    )
    out_shape = [
        shape_of((all_mols, model // 2), bf16),
        shape_of((all_mols, model // 2), bf16),
        shape_of((all_mols, model), bf16),
        shape_of((KERNEL, all_mols, model), bf16),
        shape_of((tokens, model), f32),
        shape_of((tokens, model), bf16),
        shape_of((8, model), f32),
    ]
    out_specs = [
        lead_block(out_shape[0], mols),
        lead_block(out_shape[1], mols),
        lead_block(out_shape[2], mols),
        chunk_block(out_shape[3], mols),
        lead_block(out_shape[4], tile),
        lead_block(out_shape[5], tile),
        fixed_block(out_shape[6]),
    ]
    return call(
        functools.partial(conv_kernel, mols),
        (steps,),
        in_specs,
        out_specs,
        out_shape,
        args,
        info,
        scratch=[pltpu.VMEM((chunks, tile, PAIR), f32), pltpu.VMEM((mols, model), bf16)],
        kept=(4,),
        flops=4 * tokens * model * model * 1.5,
        moved=tokens * model * 30,
    )


def dp_place(info_ref, index, count):
    away = info_ref[DP] ^ index
    place, bits = 0, count.bit_length() - 1
    for bit in range(bits):
        place = place + (((away >> bit) & 1) << (bits - 1 - bit))
    return place


def cut(width):
    size = width // PARTS
    return [slice(i * size, (i + 1) * size) for i in range(PARTS)]


def conv_weight_kernel(mine, per_step, info_ref, grp_ref, grad_ref, *refs):
    value = t_mul(grp_ref[0], grad_ref[...])
    gots, outs = (refs[:PARTS], refs[PARTS:]) if mine else ((), refs)
    count, size = outs[0].shape[:2]
    for j in range(per_step):
        place = dp_place(info_ref, pl.program_id(0) * per_step + j, count)
        part = value[j * size : (j + 1) * size]
        for i, cols in enumerate(cut(value.shape[1])):
            if mine:
                outs[0][place, :, cols] = low(part[:, cols] + gots[i][place].astype(f32))
            else:
                outs[i][place] = low(part[:, cols])


def conv_weight(info, other_side, grouped, grad, dp_size, got=()):
    kernel, mols, model = grouped.shape
    half = kernel // 2
    args = [grouped, grad, *got]
    in_specs = [
        pl.BlockSpec((1, mols, model), lambda i, info_ref: ((info_ref[PIPE] ^ other_side) * half + i, 0, 0)),
    ] + [whole_block(a) for a in args[1:]]
    dims = (dp_size, half * model // dp_size)
    out_shape = [shape_of(dims + (model,), bf16)] if got else [shape_of(dims + (model // PARTS,), bf16)] * PARTS
    return call(
        functools.partial(conv_weight_kernel, bool(got), dp_size // half),
        (half,),
        in_specs,
        [fixed_block(o) for o in out_shape],
        out_shape,
        args,
        info,
        flops=2 * half * mols * model * model,
        moved=half * model * model * 8,
    )


def weight_kernel(mine, info_ref, left_ref, *refs):
    rights, refs = refs[:2], refs[2:]
    gots, outs = (refs[:PARTS], refs[PARTS:]) if mine else ((), refs)
    count, size = outs[0].shape[1:3]
    for index in range(2):
        value = t_mul(left_ref[...], rights[index][...])
        for d in range(count):
            place = dp_place(info_ref, d, count)
            part = value[d * size : (d + 1) * size]
            if mine:
                for i, got in enumerate(gots):

                    @pl.when(pl.program_id(0) == i)
                    def _(got=got, part=part, place=place):
                        outs[0][index, place] = low(part + got[index, place].astype(f32))

            else:
                for i, out in enumerate(outs):

                    @pl.when(pl.program_id(0) == i)
                    def _(out=out, part=part, place=place):
                        out[index, place] = low(part)


def weight(info, other_side, left, right_own, right_other, dp_size, got=()):
    tokens, model = left.shape
    columns = right_own.shape[1]
    half = model // 2
    tile = columns // PARTS
    args = [left, right_own, right_other, *got]
    in_specs = [
        pl.BlockSpec((tokens, half), lambda i, info_ref: (0, info_ref[PIPE] ^ other_side)),
        pl.BlockSpec((tokens, tile), lambda i, *_: (0, i)),
        pl.BlockSpec((tokens, tile), lambda i, *_: (0, i)),
    ] + [whole_block(a) for a in got]
    dims = (2, dp_size, half // dp_size)
    if got:
        out_shape = [shape_of(dims + (columns,), bf16)]
        out_specs = [pl.BlockSpec(dims + (tile,), lambda i, *_: (0, 0, 0, i))]
    else:
        out_shape = [shape_of(dims + (tile,), bf16)] * PARTS
        out_specs = [fixed_block(o) for o in out_shape]
    return call(
        functools.partial(weight_kernel, bool(got)),
        (PARTS,),
        in_specs,
        out_specs,
        out_shape,
        args,
        info,
        flops=4 * tokens * half * columns,
        moved=tokens * columns * 4 + half * columns * 8,
    )


def project_weight_kernel(span, dp_size, mine, extra, info_ref, x_ref, gb_ref, dq, dk, dv, att, *refs):
    gots, refs = (refs[:PARTS], refs[PARTS:]) if mine else ((), refs)
    extra_ref, outs = (refs[0], refs[1:]) if extra else (None, refs)
    rows = x_ref.shape[0]
    local = dq.shape[2]
    size = x_ref.shape[2] // dp_size
    tile = 4 * local // PARTS
    for index, right in enumerate((dq, dk, dv, att)):
        value = None
        for row in range(rows):
            if index == 0:
                left = x_ref[row, WINDOW : WINDOW + span]
            elif index == 3:
                left = gb_ref[row]
            else:
                left = x_ref[row]
            term = t_mul(left, right[row])
            value = term if value is None else value + term
        for d in range(dp_size):
            at = pl.ds(pl.multiple_of(dp_place(info_ref, d, dp_size) * size, size), size)
            part = value[d * size : (d + 1) * size]
            first = index * local
            while first < (index + 1) * local:
                which = first // tile
                stop = min((which + 1) * tile, (index + 1) * local)
                piece = part[:, first - index * local : stop - index * local]
                inside = slice(first - which * tile, stop - which * tile)
                if mine:
                    outs[0][at, first:stop] = low(piece + gots[which][at, inside].astype(f32))
                else:
                    outs[which][at, inside] = low(piece)
                first = stop
    if extra:
        outs[0][dp_size * size :] = extra_ref[...]


def project_weight(info, other_side, x_ext, grad_branch, grads, span, dp_size, got=(), extra=None):
    rows, extent, model = x_ext.shape
    half = model // 2
    columns = 4 * grads[0].shape[2]
    args = [x_ext, grad_branch, *grads, *got] + ([] if extra is None else [extra])
    in_specs = [
        pl.BlockSpec((rows, extent, half), lambda i, info_ref: (0, 0, info_ref[PIPE] ^ other_side)),
        pl.BlockSpec((rows, span, half), lambda i, info_ref: (0, 0, info_ref[PIPE] ^ other_side)),
    ] + [whole_block(a) for a in args[2:]]
    if got:
        out_shape = [shape_of((half + (0 if extra is None else extra.shape[0]), columns), bf16)]
    else:
        out_shape = [shape_of((half, columns // PARTS), bf16)] * PARTS
    return call(
        functools.partial(project_weight_kernel, span, dp_size, bool(got), extra is not None),
        (1,),
        in_specs,
        [fixed_block(o) for o in out_shape],
        out_shape,
        args,
        info,
        flops=2 * rows * extent * half * columns,
        moved=rows * extent * model * 6,
    )


def feed_back_kernel(info_ref, gf_ref, two_ref, sl_own, sl_other, n_ref, sc_ref, wo_own, wi_own, vecs_ref, *refs):
    inner_pieces, outer_pieces, refs = refs[:4], refs[4:8], refs[8:]
    gh_own, gh_other, one_ref, gb_ref, vec_ref, bi_own, bi_other, wi_other, wo_other, sems = refs
    plan = plan_inner(info_ref, inner_pieces, wi_other) + plan_outer(info_ref, outer_pieces, wo_other)
    first_step = pl.program_id(0) == 0

    @pl.when(first_step)
    def _():
        fetch(plan, sems)
        vec_ref[...] = jnp.zeros_like(vec_ref)
        bi_own[...] = jnp.zeros_like(bi_own)
        bi_other[...] = jnp.zeros_like(bi_other)

    grad_feed = gf_ref[...]
    units = wo_own.shape[0]
    step = 512

    def half(total, slope_ref, wo_ref, wi_ref, gh_ref, bi_ref):
        for at in range(0, units, step):
            cols = slice(at, at + step)
            grad = low(mul_t(grad_feed, wo_ref[cols, :]) * slope_ref[:, cols].astype(f32))
            gh_ref[:, cols] = grad
            bi_ref[:1, cols] += col_sum(grad.astype(f32))
            total = total + mul_t(grad, wi_ref[:, cols])
        return total

    total = half(two_ref[...], sl_own, wo_own, wi_own, gh_own, bi_own)

    @pl.when(first_step)
    def _():
        for i, (source, target) in enumerate(plan):
            pltpu.make_async_copy(source, target, sems.at[i]).wait()

    total = half(total, sl_other, wo_other, wi_other, gh_other, bi_other)
    normal = n_ref[...]
    grad_one = norm_back(total * vecs_ref[GAIN_ONE : GAIN_ONE + 1], normal, sc_ref[:, :1])
    one_ref[...] = grad_one
    gb_ref[...] = low(grad_one)
    vec_ref[...] += jnp.concatenate(
        [col_sum(grad_one), col_sum(total * normal), col_sum(total), jnp.zeros((5, total.shape[1]), f32)], axis=0
    )


def feed_back(info, grad_feed, grad_two, slopes, n1, scale1, w_outer, w_inner, vectors, pieces, tile):
    tokens, model = grad_feed.shape
    units = w_outer.shape[0]
    args = [grad_feed, far(grad_two), *map(far, (*slopes, n1, scale1, w_outer, w_inner)), vectors, *map(far, pieces)]
    in_specs = [lead_block(a, tile) for a in args[:6]] + [whole_block(a) for a in args[6:9]] + [ANYWHERE] * 8
    out_shape = [
        shape_of((tokens, units), bf16),
        shape_of((tokens, units), bf16),
        shape_of((tokens, model), f32),
        shape_of((tokens, model), bf16),
        shape_of((8, model), f32),
        shape_of((8, units), f32),
        shape_of((8, units), f32),
    ]
    return call(
        feed_back_kernel,
        (tokens // tile,),
        in_specs,
        [lead_block(o, tile) for o in out_shape[:4]] + [fixed_block(o) for o in out_shape[4:]],
        out_shape,
        args,
        info,
        scratch=[pltpu.VMEM((model, units), bf16), pltpu.VMEM((units, model), bf16), pltpu.SemaphoreType.DMA((8,))],
        flops=8 * tokens * model * units * 1.2,
        moved=tokens * units * 8,
        limit=26 << 20,
        kept=(2,),
    )


def input_back_kernel(span, info_ref, one_ref, *refs):
    groups, weights, pieces, refs = (refs[:3], refs[3:6]), refs[6:9], refs[9:13], refs[13:]
    mine_ref, theirs_ref, left_ref, right_ref, wq_ref, wk_ref, wv_ref, sems = refs
    first_step = pl.program_id(0) == 0
    plan = plan_square(info_ref, pieces, (wq_ref, wk_ref, wv_ref))

    @pl.when(first_step)
    def _():
        fetch(plan, sems)

    def terms(grads, wq, wk, wv):
        dq, dk, dv = grads
        return mul_t(dq[0], wq[...]), mul_t(dk[0], wk[...]) + mul_t(dv[0], wv[...])

    center, total = terms(groups[0], *weights)

    @pl.when(first_step)
    def _():
        for i, (source, target) in enumerate(plan):
            pltpu.make_async_copy(source, target, sems.at[i]).wait()

    center_other, total_other = terms(groups[1], wq_ref, wk_ref, wv_ref)
    total = total + total_other
    center = one_ref[0] + center + center_other + total[WINDOW : WINDOW + span]
    left_ref[0] = low(total[:WINDOW])
    right_ref[0] = low(total[WINDOW + span :])
    half = mine_ref.shape[2]
    lower, upper = slice(0, half), slice(half, 2 * half)

    def split(mine, theirs):
        mine_ref[0] = center[:, mine]
        theirs_ref[0] = low(center[:, theirs])

    pl.when(info_ref[PIPE] == 0)(lambda: split(lower, upper))
    pl.when(info_ref[PIPE] == 1)(lambda: split(upper, lower))


def input_back(info, grad_one, own, other, weights, pieces, span):
    rows, extent, local = own[1].shape
    model = grad_one.shape[2]
    args = [far(grad_one), *own, *other, *map(far, (*weights, *pieces))]
    in_specs = [lead_block(a) for a in args[:7]] + [whole_block(a) for a in args[7:10]] + [ANYWHERE] * 4
    out_shape = [
        shape_of((rows, span, model // 2), f32),
        shape_of((rows, span, model // 2), bf16),
        shape_of((rows, WINDOW, model), bf16),
        shape_of((rows, WINDOW, model), bf16),
    ]
    return call(
        functools.partial(input_back_kernel, span),
        (rows,),
        in_specs,
        [lead_block(o) for o in out_shape],
        out_shape,
        args,
        info,
        scratch=[pltpu.VMEM((model, local), bf16)] * 3 + [pltpu.SemaphoreType.DMA((12,))],
        flops=12 * rows * extent * model * local,
        moved=rows * extent * model * 12,
    )


def finish_kernel(rows, info_ref, mine, got, head, tail, head_got, tail_got, mol, mol_got, out_ref, mol_ref):
    row = pl.program_id(0)
    width = head.shape[1]
    own = (row >= rows) == (info_ref[PIPE] == 1)

    def write(center, first, last, molecules):
        out_ref[0] = center[0].astype(f32)
        out_ref[0, :width] += first[0].astype(f32)
        out_ref[0, out_ref.shape[1] - width :] += last[0].astype(f32)
        mol_ref[0] = molecules[0]

    pl.when(own)(lambda: write(mine, head, tail, mol))
    pl.when(jnp.logical_not(own))(lambda: write(got, head_got, tail_got, mol_got))


def finish(info, mine, got, head, tail, head_got, tail_got, mol, mol_got):
    rows, span, half = mine.shape
    width = head.shape[1]

    def core_rows(array):
        return pl.BlockSpec((1,) + tuple(array.shape[1:]), lambda i, info_ref: (i % rows, 0, 0))

    rims = pl.BlockSpec((1, width, half), lambda i, info_ref: (i % rows, 0, info_ref[PIPE]))
    out_shape = [shape_of((2 * rows, span, half), f32), shape_of((2 * rows,) + tuple(mol.shape[1:]), bf16)]
    return call(
        functools.partial(finish_kernel, rows),
        (2 * rows,),
        [core_rows(mine), core_rows(got), rims, rims] + [core_rows(a) for a in (head_got, tail_got, mol, mol_got)],
        [lead_block(o) for o in out_shape],
        out_shape,
        [mine, got, head, tail, head_got, tail_got, mol, mol_got],
        info,
        moved=rows * span * half * 20,
    )


def swapped(block, axis, bit=0):
    count = lax.axis_size(axis)
    return lax.ppermute(block, axis, [(i, i ^ (1 << bit)) for i in range(count)])


def to_core(blocks):
    return [swapped(block, "pipe") for block in blocks]


def from_chunk(block, distance):
    axes = ("seq", "mp")
    count = lax.axis_size("seq") * lax.axis_size("mp")
    return lax.ppermute(block, axes, [(i + distance, i) for i in range(count) if 0 <= i + distance < count])


def pick(array, index, dim):
    return lax.dynamic_index_in_dim(array, index, dim, keepdims=False)


def add(left, right):
    return low(left.astype(f32) + right.astype(f32))


def bits_of(axis):
    return lax.axis_size(axis).bit_length() - 1


class Halving:
    def __init__(self, parts, dim, axis):
        self.dim, self.axis = dim, axis
        self.keep, self.sent = self.split(parts, 0)
        self.got = swapped(self.sent, axis)

    def split(self, parts, bit):
        dim = self.dim
        shaped = parts.reshape(parts.shape[:dim] + (parts.shape[dim] // 2, 2) + parts.shape[dim + 1 :])
        mine = (lax.axis_index(self.axis) >> bit) & 1
        return pick(shaped, mine, dim + 1), pick(shaped, 1 - mine, dim + 1)

    def finish(self, *gates):
        parts = add(self.keep, after(self.got, *gates))
        for bit in range(1, bits_of(self.axis)):
            keep, sent = self.split(parts, bit)
            parts = add(keep, swapped(sent, self.axis, bit))
        return parts.reshape(parts.shape[: self.dim] + parts.shape[self.dim + 1 :])


class HalvingDp:
    def __init__(self, parts):
        self.bit = 0
        self.start(parts)

    def start(self, parts):
        half = parts.shape[0] // 2
        self.keep, self.sent = parts[:half], parts[half:]
        self.got = swapped(self.sent, "dp", self.bit)
        self.bit += 1

    def step(self, *gates):
        self.start(add(self.keep, after(self.got, *gates)))

    def finish(self, *gates):
        while self.keep.shape[0] > 1:
            self.step()
        return add(self.keep, after(self.got, *gates))[0]


def relay(quarter):
    first = swapped(quarter, "mp")
    return first, swapped(first, "seq")


def all_pieces(first, second):
    return [first, second, swapped(first, "pipe"), swapped(second, "pipe")]


def in_order(first, mine, recv, axis):
    return jnp.where(
        first == 0, jnp.concatenate([mine, recv], axis=axis), jnp.concatenate([recv, mine], axis=axis)
    )


def after(value, *others):
    return lax.optimization_barrier((value, *others))[0] if others else value


def tie(*values):
    return lax.optimization_barrier(values)


def on_device(
    characters,
    row_lengths,
    w_query,
    b_query,
    w_key,
    w_value,
    b_value,
    w_attn_out,
    b_attn_out,
    gain_one,
    shift_one,
    w_inner,
    b_inner,
    w_outer,
    b_outer,
    gain_two,
    shift_two,
    w_conv,
    b_conv,
    gain_three,
    shift_three,
    molecule_grad,
):
    pipe = lax.axis_index("pipe")
    seq = lax.axis_index("seq")
    mp = lax.axis_index("mp")
    dp_size, seq_size, mp_size = (lax.axis_size(a) for a in ("dp", "seq", "mp"))
    all_rows, span, half_model = characters.shape
    rows = all_rows // 2
    model = 2 * half_model
    local = w_query.shape[1]
    units = w_inner.shape[1]
    tokens = rows * span
    mols = tokens // KERNEL
    block = min(WINDOW, span)
    tile = min(256, tokens)
    own_start = (seq * lax.axis_size("mp") + mp) * span

    def rows_of(array, index):
        return lax.dynamic_slice_in_dim(array, index * rows, rows, 0)

    me = 2 * (seq & 1) + pipe
    lengths = rows_of(row_lengths, pipe)
    scalars = jnp.stack([own_start, pipe, me, lax.axis_index("dp"), mp]).astype(jnp.int32)
    info = jnp.concatenate([scalars, lengths])
    squares = (w_query, w_key, w_value)
    biases, vectors = gather_small(
        b_query,
        b_value,
        b_inner,
        (b_attn_out, gain_one, shift_one, b_outer, gain_two, shift_two, b_conv, gain_three, shift_three),
    )
    hops = -(-WINDOW // span)
    width = min(span, WINDOW)
    tail, head = characters[:, span - width :], characters[:, :width]

    left, right = [], []
    for hop in range(1, hops + 1):
        left.insert(0, from_chunk(tail, -hop))
        right.append(from_chunk(head, hop))
    left, right = (a[0] if hops == 1 else jnp.concatenate(a, axis=1) for a in (left, right))
    packet = pack_first(after(info, tail, head), squares, w_attn_out, biases)
    square_first = swapped(packet, "mp")
    inner_packet, outer_packet, center_send, mol_send = pack_second(
        info, w_inner, w_outer, after(characters, packet), molecule_grad
    )
    center_got = swapped(center_send, "pipe")
    rims_got = swapped(jnp.stack([rows_of(left, 1 - pipe), rows_of(right, 1 - pipe)]), "pipe")
    mol_grad = molecule_grad.reshape(2 * mols, half_model)

    positions = own_start + jnp.arange(span, dtype=jnp.int32)
    live = (positions[None, :] < lengths[:, None]).astype(f32)
    live_mols = jnp.broadcast_to(live[:, ::KERNEL].reshape(mols, 1), (mols, PAIR))
    live = jnp.broadcast_to(live.reshape(tokens, 1), (tokens, PAIR))
    square_second = swapped(square_first, "seq")
    inner_first = swapped(after(inner_packet, square_first), "mp")
    q_own, k_own, v_own, att_own, lse_own, part, x_ext = attend_own(
        info,
        (characters, after(center_got, square_first, live, live_mols), left, right, rims_got),
        (*squares, w_attn_out),
        biases,
        span,
        block,
    )
    biases_other = square_first[square_first.shape[0] - 16 :]
    square_pieces = all_pieces(square_first, after(square_second, x_ext))
    inner_first = after(inner_first, x_ext)
    inner_second = swapped(inner_first, "seq")
    outer_first = swapped(after(outer_packet, inner_first), "mp")
    q_other, k_other, v_other, att_other, lse_other, n1, scale1, middle = attend_other(
        info, after(x_ext, inner_first), square_pieces, biases_other, part, vectors, span, block
    )
    outer_first = after(outer_first, middle)
    outer_second = swapped(outer_first, "seq")
    inner_pieces = all_pieces(inner_first, after(inner_second, middle))
    n1, scale1, middle = (a.reshape(tokens, -1) for a in (n1, scale1, middle))
    act_own, slope_own, part = feed(
        info, after(middle, outer_first, *inner_pieces), biases, units, tile, w_inner, w_outer
    )
    pieces = (*inner_pieces, *all_pieces(outer_first, after(outer_second, part)))
    mol_got = swapped(after(mol_send, part), "pipe").reshape(mols, half_model)
    act_other, slope_other, n2, scale2, sent = feed(
        info, middle, biases_other, units, tile, tail=(part, n1, live, vectors), pieces=pieces
    )
    mol_mine, mol_theirs, grad_conv, grouped, grad_two, grad_feed, vec_conv = conv(
        info, sent, w_conv.reshape(KERNEL, model, model), vectors, mol_grad, mol_got, live_mols, n2, scale2, live, 2
    )
    mol_shape = (rows, span // KERNEL, half_model)
    mol_mine = mol_mine.reshape(mol_shape)
    mol_theirs = mol_theirs.reshape(mol_shape)

    conv_theirs = conv_weight(info, 1, grouped, grad_conv, dp_size)
    conv_got = to_core(conv_theirs)
    outer_theirs = weight(info, 1, after(grad_feed, *conv_theirs), act_own, act_other, dp_size)
    outer_got = to_core(outer_theirs)
    (conv_part,) = conv_weight(info, 0, grouped, after(grad_conv, *outer_theirs), dp_size, conv_got)
    conv_halving = Halving(conv_part.reshape(dp_size, seq_size, mp_size, -1, model), 2, "mp")
    gh_own, gh_other, grad_one, grad_branch, vec_one, bi_own, bi_other = feed_back(
        info,
        after(grad_feed, conv_halving.sent),
        grad_two,
        (slope_own, slope_other),
        n1,
        scale1,
        w_outer,
        w_inner,
        vectors,
        pieces,
        tile,
    )
    (outer_part,) = weight(info, 0, after(grad_feed, gh_own), act_own, act_other, dp_size, outer_got)
    outer_halving = Halving(outer_part.reshape(2, dp_size, seq_size, -1, units), 2, "seq")
    conv_part = conv_halving.finish(outer_halving.sent)
    conv_halving = Halving(conv_part, 1, "seq")
    inner_theirs = weight(
        info, 1, after(middle, outer_halving.sent, conv_halving.sent), gh_own, gh_other, dp_size
    )
    inner_got = to_core(inner_theirs)

    grad_branch = grad_branch.reshape(rows, span, model)
    grad_one = grad_one.reshape(rows, span, model)
    *back_other, vec_other = attend_back(
        info, after(grad_branch, *inner_theirs), q_other, k_other, v_other, lse_other, square_pieces, block
    )
    (inner_part,) = weight(info, 0, after(middle, vec_other), gh_own, gh_other, dp_size, inner_got)
    inner_sent = inner_part[1]
    inner_got = swapped(inner_sent, "mp")
    outer_part = outer_halving.finish(inner_sent)
    outer_sent = outer_part[1]
    outer_got = swapped(outer_sent, "mp")
    conv_part = conv_halving.finish(inner_sent)
    head_args = (x_ext, grad_branch)
    gated, conv_part, outer_sent, inner_sent = tie(x_ext, conv_part, outer_sent, inner_sent)
    other_theirs = project_weight(info, 1, gated, grad_branch, (*back_other, att_other), span, dp_size)
    other_got = to_core(other_theirs)
    *back_own, vec = attend_back(
        info,
        after(grad_branch, *other_theirs),
        q_own,
        k_own,
        v_own,
        lse_own,
        w_attn_out,
        block,
        (vec_conv, vec_one, bi_own, bi_other, vec_other),
    )
    inner_part = add(inner_part[0], after(inner_got, vec))
    inner_halving = Halving(inner_part.reshape(dp_size, seq_size, -1, units), 1, "seq")
    outer_part = add(outer_part[0], after(outer_got, vec)).reshape(dp_size, -1, units)

    def narrow(part):
        return jnp.concatenate([part[:, :, :model], part[:, :, model:]], axis=1)

    merged = jnp.concatenate([conv_part, narrow(outer_part)], axis=1)
    merged_halving = HalvingDp(merged)
    vec = low(vec + swapped(vec, "pipe"))
    own_theirs = project_weight(
        info,
        1,
        after(x_ext, inner_halving.sent, merged_halving.sent),
        grad_branch,
        (*back_own, att_own),
        span,
        dp_size,
    )
    own_got = to_core(own_theirs)
    (other_part,) = project_weight(
        info, 0, after(x_ext, *own_theirs), grad_branch, (*back_other, att_other), span, dp_size, other_got, vec
    )
    got = swapped(other_part, "mp")
    (own_part,) = project_weight(
        info, 0, after(x_ext, other_part), grad_branch, (*back_own, att_own), span, dp_size, own_got
    )
    merged_halving.step(own_part)
    mine, theirs, left, right = input_back(
        info, after(grad_one, own_part, merged_halving.sent), back_own, back_other, squares, square_pieces, span
    )
    head_part = add(own_part, after(got[: model // 2], mine)).reshape(dp_size, seq_size, -1, units)
    vec = add(vec, got[model // 2 :])

    def with_vec(part):
        return jnp.concatenate([part.reshape(-1, units), vec], axis=0)

    inner_halving = HalvingDp(inner_halving.finish(mine))
    merged = merged_halving.finish(mine)
    for bit in range(bits_of("seq")):
        shaped = head_part.reshape(dp_size, head_part.shape[1] // 2, 2, -1, units)
        bit_mine = (seq >> bit) & 1
        got = swapped(with_vec(pick(shaped, 1 - bit_mine, 2)), "seq", bit)
        count = got.shape[0] - 16
        head_part = add(pick(shaped, bit_mine, 2), got[:count].reshape(dp_size, shaped.shape[1], -1, units))
        vec = add(vec, got[count:])
    head_part = head_part.reshape(dp_size, -1, units)
    inner_sum = inner_halving.finish()
    for bit in range(bits_of("dp")):
        half = head_part.shape[0] // 2
        got = swapped(with_vec(head_part[half:]), "dp", bit)
        count = got.shape[0] - 16
        head_part = add(head_part[:half], got[:count].reshape(head_part[:half].shape))
        vec = add(vec, got[count:])
    head_sum = head_part[0].astype(f32)
    vec = vec.astype(f32)
    grad_b_conv, grad_gain_three, grad_shift_three, grad_gain_two, grad_shift_two, grad_b_outer = (
        vec[i, :model] for i in range(6)
    )
    grad_b_attn_out, grad_gain_one, grad_shift_one = (vec[i, :model] for i in range(6, 9))
    grad_b_query, grad_b_value = (vec[i, model:] for i in range(2))
    grad_b_inner = vec[9:11].reshape(-1)
    size = conv_part.shape[1]
    grad_w_conv = merged[:size].astype(f32)
    outer_sum = jnp.concatenate([merged[size : size + size // 2], merged[size + size // 2 :]], axis=1).astype(f32)
    inner_sum = inner_sum.astype(f32)

    head, tail = None, None
    for hop in range(1, hops + 1):
        top = WINDOW - (hop - 1) * span
        to_tail = from_chunk(left[:, top - width : top], hop)
        to_head = from_chunk(right[:, WINDOW - top : WINDOW - top + width], -hop)
        head = to_head if head is None else add(head, to_head)
        tail = to_tail if tail is None else add(tail, to_tail)
    rims, mol_theirs = tie(jnp.stack([head, tail]), mol_theirs)
    rims_got = swapped(lax.dynamic_slice_in_dim(rims, (1 - pipe) * half_model, half_model, 3), "pipe")
    chars_grad, molecules = finish(
        info,
        mine,
        swapped(theirs, "pipe"),
        head,
        tail,
        rims_got[0],
        rims_got[1],
        mol_mine,
        swapped(mol_theirs, "pipe"),
    )

    grad_w_query, grad_w_key, grad_w_value, grad_w_attn = (
        head_sum[:, i * local : (i + 1) * local] for i in range(4)
    )
    return (
        molecules,
        chars_grad,
        grad_w_query,
        grad_b_query,
        grad_w_key,
        grad_w_value,
        grad_b_value,
        grad_w_attn.T,
        grad_b_attn_out,
        grad_gain_one,
        grad_shift_one,
        inner_sum,
        grad_b_inner,
        outer_sum.T,
        grad_b_outer,
        grad_gain_two,
        grad_shift_two,
        grad_w_conv,
        grad_b_conv,
        grad_gain_three,
        grad_shift_three,
    )


def solution(mesh):
    return jax.shard_map(
        on_device,
        mesh=mesh,
        in_specs=(
            P("dp", ("seq", "mp"), "pipe"),
            P("dp"),
            P(None, "mp"),
            P("mp"),
            P(None, "mp"),
            P(None, "mp"),
            P("mp"),
            P("mp", None),
            P(),
            P(),
            P(),
            P(None, "mp"),
            P("mp"),
            P("mp", None),
            P(),
            P(),
            P(),
            P(),
            P(),
            P(),
            P(),
            P("dp", ("seq", "mp"), "pipe"),
        ),
        out_specs=(
            P("dp", ("seq", "mp"), "pipe"),
            P("dp", ("seq", "mp"), "pipe"),
            P(("pipe", "dp", "seq"), "mp"),
            P(),
            P(("pipe", "dp", "seq"), "mp"),
            P(("pipe", "dp", "seq"), "mp"),
            P(),
            P("mp", ("pipe", "dp", "seq")),
            P(),
            P(),
            P(),
            P(("pipe", "dp", "seq"), "mp"),
            P(),
            P("mp", ("pipe", "dp", "seq")),
            P(),
            P(),
            P(),
            P(("pipe", "dp", "seq", "mp"), None),
            P(),
            P(),
            P(),
        ),
        check_vma=False,
    )
```

```python
import functools

import jax
import jax.numpy as jnp
from jax import lax
from jax.experimental import pallas as pl
from jax.experimental.pallas import tpu as pltpu
from jax.sharding import PartitionSpec as P

HEAD = 64
WINDOW = 128
KERNEL = 4
PAIR = 2 * HEAD
VMEM_LIMIT = 20 << 20
COST = 1000
HEADS_NEAR = True
UNITS_NEAR = True
PARTS = 1

epsilon = 1e-05
masked_score = -1e30
f32 = jnp.float32
bf16 = jnp.bfloat16


def mul(left, right):
    return jnp.dot(left, right, preferred_element_type=f32)


def mul_t(left, right):
    return lax.dot_general(left, right, (((1,), (1,)), ((), ())), preferred_element_type=f32)


def t_mul(left, right):
    return lax.dot_general(left, right, (((0,), (0,)), ((), ())), preferred_element_type=f32)


def gelu_parts(value):
    cdf = 0.5 + 0.5 * lax.erf(value * 2.0**-0.5)
    return value * cdf, cdf + value * jnp.exp(value * value * -0.5) * 0.3989422804014327


def norm_parts(value):
    centered = value - jnp.mean(value, axis=-1, keepdims=True)
    scale = lax.rsqrt(jnp.mean(centered * centered, axis=-1, keepdims=True) + epsilon)
    return centered * scale, scale


def norm_back(cotangent, normal, scale):
    first = jnp.mean(cotangent, axis=-1, keepdims=True)
    second = jnp.mean(cotangent * normal, axis=-1, keepdims=True)
    return scale * (cotangent - first - normal * second)


def col_sum(value):
    return jnp.sum(value, axis=0, keepdims=True)


def low(value):
    return value.astype(bf16)


START, PIPE, QUARTER, DP, MP, LENGTHS = range(6)


def call(body, grid, in_specs, out_specs, out_shape, args, info, scratch=(), flops=0, moved=0, limit=VMEM_LIMIT, kept=None):
    if kept:
        out_shape = [kept[i](tuple(o.shape), o.dtype) if i in kept else o for i, o in enumerate(out_shape)]
    return pl.pallas_call(
        body,
        grid_spec=pltpu.PrefetchScalarGridSpec(
            num_scalar_prefetch=1,
            grid=grid,
            in_specs=in_specs,
            out_specs=out_specs,
            scratch_shapes=scratch,
        ),
        out_shape=out_shape,
        compiler_params=pltpu.CompilerParams(vmem_limit_bytes=limit),
        cost_estimate=pl.CostEstimate(flops=int(flops) // COST, bytes_accessed=int(moved) // COST, transcendentals=0),
    )(info, *args)


def whole_block(array):
    zeros = (0,) * array.ndim
    return pl.BlockSpec(array.shape, lambda *_: zeros, pipeline_mode=pl.Buffered(1))


def lead_block(array, size=1):
    rest = (0,) * (array.ndim - 1)
    return pl.BlockSpec((size,) + tuple(array.shape[1:]), lambda i, *_: (i,) + rest)


def core_block(array, steps, size=1):
    rest = (0,) * (array.ndim - 1)
    return pl.BlockSpec((size,) + tuple(array.shape[1:]), lambda i, info: (info[PIPE] * steps + i,) + rest)


def chunk_block(array, size):
    return pl.BlockSpec((array.shape[0], size, array.shape[2]), lambda i, *_: (0, i, 0))


def fixed_block(array):
    zeros = (0,) * array.ndim
    return pl.BlockSpec(array.shape, lambda *_: zeros)


ANYWHERE = pl.BlockSpec(memory_space=pl.ANY)


def far(array):
    return pltpu.with_memory_space_constraint(array, pltpu.HBM)


def heads(array):
    return pltpu.with_memory_space_constraint(array, HEADS_MEMORY)


def hidden(array):
    return pltpu.with_memory_space_constraint(array, UNITS_MEMORY)


HEADS_MEMORY = pltpu.VMEM if HEADS_NEAR else pltpu.HBM
UNITS_MEMORY = pltpu.VMEM if UNITS_NEAR else pltpu.HBM


def shape_of(dims, kind):
    return jax.ShapeDtypeStruct(tuple(dims), kind)


def fetch(plan, sems):
    copies = [pltpu.make_async_copy(source, target, sems.at[i]) for i, (source, target) in enumerate(plan)]
    for copy in copies:
        copy.start()
    return copies


class Loads:
    def __init__(self, sems, *groups):
        self.groups, count = [], 0
        for group in groups:
            self.groups.append([(source, target, sems.at[count + i]) for i, (source, target) in enumerate(group)])
            count += len(group)

    def start(self):
        for group in self.groups:
            for copy in group:
                pltpu.make_async_copy(*copy).start()

    def ready(self, *indices):
        for index in indices:
            for copy in self.groups[index]:
                pltpu.make_async_copy(*copy).wait()

    def fill(self):
        @pl.when(pl.program_id(0) == 0)
        def _():
            self.start()
            self.ready(*range(len(self.groups)))

    def run(self, body):
        @pl.when(pl.program_id(0) == 0)
        def _():
            self.start()
            body(self.ready)

        @pl.when(pl.program_id(0) != 0)
        def _():
            body(lambda *indices: None)


def placed(info_ref, index, size):
    return pl.ds(pl.multiple_of((info_ref[QUARTER] ^ (0, 2, 1, 3)[index]) * size, size), size)


def plan_square(info_ref, pieces, targets, first=0):
    size = targets[0].shape[0] // 4
    return [
        [
            (piece.at[pl.ds((first + which) * size, size)], target.at[placed(info_ref, i, size)])
            for i, piece in enumerate(pieces)
        ]
        for which, target in enumerate(targets)
    ]


def plan_columns(source, target, step):
    return [[(source.at[:, pl.ds(at, step)], target.at[:, pl.ds(at, step)])] for at in range(0, target.shape[1], step)]


def plan_rows(source, target, step):
    return [[(source.at[pl.ds(at, step)], target.at[pl.ds(at, step)])] for at in range(0, target.shape[0], step)]


def plan_inner(info_ref, pieces, target):
    size = target.shape[0] // 4
    return [(piece.at[pl.ds(0, size)], target.at[placed(info_ref, i, size)]) for i, piece in enumerate(pieces)]


def plan_outer(info_ref, pieces, target):
    size = target.shape[0] // 2
    return [
        (piece, target.at[pl.ds(pl.multiple_of((info_ref[PIPE] ^ i) * size, size), size)])
        for i, piece in enumerate(pieces)
    ]


def plan_attn_out(info_ref, pieces, target):
    model = target.shape[1]
    size = target.shape[0] // 4
    columns = model // 2
    return [
        (
            piece.at[pl.ds(piece.shape[0] - 16 - (2 - side) * size, size)],
            target.at[placed(info_ref, i, size), pl.ds(side * columns, columns)],
        )
        for i, piece in enumerate(pieces)
        for side in range(2)
    ]


def pack_kernel(plan_of, info_ref, *refs):
    sems = refs[-1]
    for copy in fetch(plan_of(info_ref, *refs[:-1]), sems):
        copy.wait()


def pack(info, plan_of, args, out_shape, copies):
    return call(
        functools.partial(pack_kernel, plan_of),
        (1,),
        [ANYWHERE] * len(args),
        [fixed_block(o) for o in out_shape],
        out_shape,
        [far(a) for a in args],
        info,
        scratch=[pltpu.SemaphoreType.DMA((copies,))],
        moved=sum(o.size * 4 for o in out_shape),
    )


def gather_small_kernel(bq, bv, bi, *refs):
    vectors, (bias_ref, vec_ref) = refs[:-2], refs[-2:]
    local = bias_ref.shape[1]
    rows = [bq[...].reshape(1, local), bv[...].reshape(1, local)]
    inner = bi[...].reshape(1, -1)
    rows += [inner[:, i * local : (i + 1) * local] for i in range(inner.shape[1] // local)]
    rows = [row.astype(f32) for row in rows]
    rows.append(jnp.zeros((16 - len(rows), local), f32))
    bias_ref[...] = low(jnp.concatenate(rows, axis=0))
    rows = [v[...].reshape(1, -1).astype(f32) for v in vectors]
    rows.append(jnp.zeros((16 - len(rows), vec_ref.shape[1]), f32))
    vec_ref[...] = jnp.concatenate(rows, axis=0)


def gather_small(b_query, b_value, b_inner, vectors):
    return pl.pallas_call(
        gather_small_kernel,
        out_shape=[shape_of((16, b_query.shape[0]), bf16), shape_of((16, vectors[0].shape[0]), f32)],
    )(b_query, b_value, b_inner, *vectors)


def inner_bias(bias_ref, units):
    local = bias_ref.shape[1]
    return jnp.concatenate([bias_ref[2 + i : 3 + i] for i in range(units // local)], axis=1).astype(f32)


def quarter_of(info_ref, array):
    size = array.shape[0] // 4
    return pl.ds(pl.multiple_of(info_ref[QUARTER] * size, size), size)


def pack_first(info, weights, w_out, biases):
    model, local = weights[0].shape
    size, out_size, half = model // 4, w_out.shape[0] // 4, w_out.shape[1] // 2

    def plan_of(info_ref, wq, wk, wv, wo, bias, packet):
        plan = [(bias, packet.at[pl.ds(3 * size + 2 * out_size, 16)])]
        plan += [
            (w.at[quarter_of(info_ref, w)], packet.at[pl.ds(i * size, size)]) for i, w in enumerate((wq, wk, wv))
        ]
        return plan + [
            (
                wo.at[quarter_of(info_ref, wo), pl.ds(side * half, half)],
                packet.at[pl.ds(3 * size + side * out_size, out_size)],
            )
            for side in range(2)
        ]

    out_shape = [shape_of((3 * size + 2 * out_size + 16, local), bf16)]
    return pack(info, plan_of, [*weights, w_out, biases], out_shape, 6)[0]


def pack_second(info, w_inner, w_outer):
    def plan_of(info_ref, wi, wo, inner, outer):
        size = wo.shape[0] // 2
        half = pl.ds(pl.multiple_of(info_ref[PIPE] * size, size), size)
        return [(wi.at[quarter_of(info_ref, wi)], inner), (wo.at[half], outer)]

    out_shape = [shape_of((a.shape[0] // n, a.shape[1]), bf16) for a, n in ((w_inner, 4), (w_outer, 2))]
    return pack(info, plan_of, [w_inner, w_outer], out_shape, 2)


def pack_rows(info, arrays):
    rows = arrays[0].shape[0] // 2

    def plan_of(info_ref, *refs):
        theirs = pl.ds((1 - info_ref[PIPE]) * rows, rows)
        return [(ref.at[theirs], out) for ref, out in zip(refs[: len(arrays)], refs[len(arrays) :])]

    out_shape = [shape_of((rows,) + tuple(a.shape[1:]), bf16) for a in arrays]
    return pack(info, plan_of, arrays, out_shape, len(arrays))


def pack_rims(info, characters, center_got, width):
    rows, span, half = center_got.shape

    def plan_of(info_ref, chars, got, tail, head):
        mine = pl.ds(info_ref[PIPE] * rows, rows)
        return [
            (source, target.at[which])
            for target, at in ((tail, pl.ds(span - width, width)), (head, pl.ds(0, width)))
            for which, source in enumerate((chars.at[mine, at], got.at[:, at]))
        ]

    out_shape = [shape_of((2, rows, width, half), bf16)] * 2
    return pack(info, plan_of, [characters, center_got], out_shape, 4)


def pair_lanes(rows):
    return lax.broadcasted_iota(jnp.int32, (rows, PAIR), 1) < HEAD


def split_pair(both, is_first):
    zero = jnp.zeros_like(both)
    return jnp.concatenate([jnp.where(is_first, both, zero), jnp.where(is_first, zero, both)], axis=0)


def join_rows(stacked):
    block = stacked.shape[1] // 2
    return jnp.concatenate([stacked[:HEAD, :block], stacked[HEAD:, block:]], axis=0)


def window_of(block):
    dims = (block + 2 * WINDOW, block)
    q_at = lax.broadcasted_iota(jnp.int32, dims, 1)
    k_at = lax.broadcasted_iota(jnp.int32, dims, 0) - WINDOW
    return jnp.abs(q_at - k_at) < WINDOW, k_at


def window_bias(in_window, position, length):
    bias = jnp.where(in_window & (position >= 0) & (position < length), 0.0, masked_score)
    return jnp.concatenate([bias, bias], axis=1)


def alive(info_ref, span, size, stride):
    per_row = span // stride
    step = pl.program_id(0)
    first = step * size
    pieces = []
    for j in range(max(1, size // per_row)):
        index = lax.broadcasted_iota(jnp.int32, (min(size, per_row), 1), 0) + lax.rem(first, per_row)
        length = info_ref[LENGTHS + first // per_row + j]
        pieces.append((info_ref[START] + index * stride < length).astype(f32))
    return pieces[0] if len(pieces) == 1 else jnp.concatenate(pieces, axis=0)


def inner_blocks(span, block):
    return [i for i in range(span // block) if i * block >= WINDOW and (i + 1) * block + WINDOW <= span]


def attend_block(index, block, info_ref, q_ref, att_ref, lse_ref, keys_of, values_of):
    width = block + 2 * WINDOW
    rows = slice(index * block, (index + 1) * block)
    is_first = pair_lanes(block)
    lanes = lax.broadcasted_iota(jnp.int32, (block, PAIR), 1)
    q_at = lax.broadcasted_iota(jnp.int32, (block, width), 0)
    k_at = lax.broadcasted_iota(jnp.int32, (block, width), 1) - WINDOW
    position = k_at + (info_ref[START] + index * block)
    length = info_ref[LENGTHS + pl.program_id(0)]
    allowed = (jnp.abs(q_at - k_at) < WINDOW) & (position >= 0) & (position < length)
    bias = jnp.where(allowed, 0.0, masked_score)
    bias = jnp.concatenate([bias, bias], axis=0)
    totals = jnp.zeros((block, PAIR), f32)
    for pair in range(q_ref.shape[2] // PAIR):
        cols = slice(pair * PAIR, (pair + 1) * PAIR)
        scores = mul_t(split_pair(q_ref[0, rows, cols], is_first), keys_of(cols)) + bias
        top = jnp.max(scores, axis=-1, keepdims=True)
        weights = jnp.exp(scores - top)
        total = jnp.sum(weights, axis=-1, keepdims=True)
        out = mul(low(weights), values_of(cols)) * (1.0 / total)
        att_ref[0, rows, cols] = low(jnp.where(is_first, out[:block], out[block:]))
        log_total = top + jnp.log(total)
        totals = jnp.where(lanes == 2 * pair, log_total[:block], totals)
        totals = jnp.where(lanes == 2 * pair + 1, log_total[block:], totals)
    lse_ref[0, index] = totals.T[:8]


def by_core(info_ref, half, work):
    lower, upper = slice(0, half), slice(half, 2 * half)
    pl.when(info_ref[PIPE] == 0)(lambda: work(lower, upper))
    pl.when(info_ref[PIPE] == 1)(lambda: work(upper, lower))


def attend_inner_kernel(span, block, other, info_ref, center, center_got, bias_ref, *refs):
    sources, refs = (refs[:4], refs[4:]) if other else (refs[:3], refs[3:])
    q_ref, k_ref, v_ref, att_ref, lse_ref, wq_ref, wk_ref, wv_ref, x_ref, sems = refs
    targets = (wq_ref, wk_ref, wv_ref)
    plan = plan_square(info_ref, sources, targets) if other else [[pair] for pair in zip(sources, targets)]

    def place(mine, got):
        x_ref[:, mine] = center[0]
        x_ref[:, got] = center_got[0]

    by_core(info_ref, center.shape[2], place)

    def work(ready):
        x = x_ref[...]
        ready(0)
        q_ref[0] = low(low(mul(x, wq_ref[...]) + bias_ref[0:1].astype(f32)).astype(f32) * HEAD ** (-0.5))
        ready(1)
        k_ref[0] = low(mul(x, wk_ref[...]))
        ready(2)
        v_ref[0] = low(mul(x, wv_ref[...]) + bias_ref[1:2].astype(f32))
        for index in inner_blocks(span, block):
            window = slice(index * block - WINDOW, (index + 1) * block + WINDOW)
            attend_block(
                index,
                block,
                info_ref,
                q_ref,
                att_ref,
                lse_ref,
                lambda cols, window=window: k_ref[0, window, cols],
                lambda cols, window=window: v_ref[0, window, cols],
            )

    Loads(sems, *plan).run(work)


def attend_inner(info, center, center_got, sources, biases, span, block):
    rows, _, half = center_got.shape
    local = biases.shape[1]
    model = 2 * half
    other = len(sources) == 4
    out_shape = [shape_of((rows, span, local), bf16)] * 4 + [shape_of((rows, span // block, 8, block), f32)]
    return call(
        functools.partial(attend_inner_kernel, span, block, other),
        (rows,),
        [core_block(center, rows), lead_block(center_got), whole_block(biases)] + [ANYWHERE] * len(sources),
        [lead_block(o) for o in out_shape],
        out_shape,
        [far(center), center_got, biases, *map(far, sources)],
        info,
        scratch=[pltpu.VMEM((model, local), bf16)] * 3
        + [pltpu.VMEM((span, model), bf16), pltpu.SemaphoreType.DMA((12,))],
        kept=dict.fromkeys(range(5), HEADS_MEMORY),
        flops=6 * rows * span * model * local,
        moved=rows * span * model * 8,
    )


def attend_outer_kernel(span, block, info_ref, center, center_got, left, right, vec_ref, *refs):
    biases, refs = refs[:2], refs[2:]
    groups, refs = (refs[:5], refs[5:10]), refs[10:]
    own_sources, pieces, refs = refs[:3], refs[3:7], refs[7:]
    outs, refs = (refs[:4], refs[4:8]), refs[8:]
    n_ref, s_ref, mid_ref, x_ref, *refs = refs
    own_w, other_w, (k_all, v_all, sems) = refs[:3], refs[3:6], refs[6:]
    loads = Loads(
        sems,
        list(zip(own_sources[:2], own_w)),
        [(own_sources[2], own_w[2])],
        sum(plan_square(info_ref, pieces, other_w[:2], 1), []),
        plan_attn_out(info_ref, pieces, other_w[2]),
    )

    def place(mine, got):
        for at, mine_part, got_part in (
            (slice(0, WINDOW), left[0, 0], left[1, 0]),
            (slice(WINDOW, WINDOW + span), center[0], center_got[0]),
            (slice(WINDOW + span, 2 * WINDOW + span), right[0, 0], right[1, 0]),
        ):
            x_ref[0, at, mine] = mine_part
            x_ref[0, at, got] = got_part

    by_core(info_ref, center.shape[2], place)
    inner = inner_blocks(span, block)
    width = block + 2 * WINDOW

    def work(ready):
        rims = jnp.concatenate([x_ref[0, :WINDOW], x_ref[0, WINDOW + span :]], axis=0)
        branch = None
        for half, (bias_ref, group, (wk_ref, wv_ref, wo_ref), out) in enumerate(
            zip(biases, groups, (own_w, other_w), outs)
        ):
            q_ref, k_ref, v_ref, att_in, lse_in = group
            krim_ref, vrim_ref, att_ref, lse_ref = out
            ready(2 * half)
            krim_ref[0] = low(mul(rims, wk_ref[...]))
            vrim_ref[0] = low(mul(rims, wv_ref[...]) + bias_ref[1:2].astype(f32))
            join_rims(k_all, k_ref, krim_ref, span)
            join_rims(v_all, v_ref, vrim_ref, span)
            for index in range(span // block):
                rows = slice(index * block, (index + 1) * block)
                if index in inner:
                    att_ref[0, rows] = att_in[0, rows]
                    lse_ref[0, index] = lse_in[0, index]
                    continue
                window = slice(index * block, index * block + width)
                attend_block(
                    index,
                    block,
                    info_ref,
                    q_ref,
                    att_ref,
                    lse_ref,
                    lambda cols, window=window: k_all[window, cols],
                    lambda cols, window=window: v_all[window, cols],
                )
            ready(2 * half + 1)
            term = mul(att_ref[0], wo_ref[...])
            branch = term if branch is None else branch + term
        before = x_ref[0, WINDOW : WINDOW + span].astype(f32) + branch + vec_ref[B_ATTN : B_ATTN + 1]
        normal, scale = norm_parts(before)
        n_ref[0] = low(normal)
        s_ref[0] = jnp.broadcast_to(scale, s_ref.shape[1:])
        mid_ref[0] = low(normal * vec_ref[GAIN_ONE : GAIN_ONE + 1] + vec_ref[SHIFT_ONE : SHIFT_ONE + 1])

    loads.run(work)


def join_rims(target, center, rims, span):
    target[:WINDOW] = rims[0, :WINDOW]
    target[WINDOW : WINDOW + span] = center[0]
    target[WINDOW + span :] = rims[0, WINDOW:]


def attend_outer(info, x_parts, vectors, biases, groups, own_sources, pieces, span, block):
    center, center_got, left, right = x_parts
    rows, _, half = center_got.shape
    local = biases[0].shape[1]
    model = 2 * half
    extent = span + 2 * WINDOW
    per_group = [
        shape_of((rows, 2 * WINDOW, local), bf16),
        shape_of((rows, 2 * WINDOW, local), bf16),
        shape_of((rows, span, local), bf16),
        shape_of((rows, span // block, 8, block), f32),
    ]
    out_shape = 2 * per_group + [
        shape_of((rows, span, model), bf16),
        shape_of((rows, span, PAIR), f32),
        shape_of((rows, span, model), bf16),
        shape_of((rows, extent, model), bf16),
    ]
    flat = [a for group in groups for a in group]
    rim = pl.BlockSpec((2, 1, WINDOW, half), lambda i, *_: (0, i, 0, 0))
    return call(
        functools.partial(attend_outer_kernel, span, block),
        (rows,),
        [core_block(center, rows), lead_block(center_got), rim, rim, whole_block(vectors)]
        + [whole_block(a) for a in biases]
        + [lead_block(a) for a in flat]
        + [ANYWHERE] * 7,
        [lead_block(o) for o in out_shape],
        out_shape,
        [far(center), center_got, left, right, vectors, *biases, *map(heads, flat), *map(far, (*own_sources, *pieces))],
        info,
        scratch=[pltpu.VMEM((model, local), bf16), pltpu.VMEM((model, local), bf16), pltpu.VMEM((local, model), bf16)] * 2
        + [pltpu.VMEM((extent, local), bf16)] * 2
        + [pltpu.SemaphoreType.DMA((19,))],
        kept=dict.fromkeys((0, 1, 2, 3, 4, 5, 6, 7, 8, 9, 11), HEADS_MEMORY),
        flops=6 * rows * span * model * local,
        moved=rows * extent * model * 8,
        limit=28 << 20,
    )


def attend_back_kernel(span, block, other, info_ref, gb_ref, q_ref, kc_ref, kr_ref, vc_ref, vr_ref, lse_ref, *refs):
    first_step = pl.program_id(0) == 0
    if other:
        pieces, refs = refs[:4], refs[4:]
        dq_ref, dk_ref, dv_ref, vec_ref, ga_ref, k_ref, v_ref, kt_ref, dk_acc, dv_acc, wo_ref, sems = refs

        Loads(sems, plan_attn_out(info_ref, pieces, wo_ref)).fill()

    else:
        wo_ref, *vecs, dq_ref, dk_ref, dv_ref, all_ref, ga_ref, k_ref, v_ref, kt_ref, dk_acc, dv_acc, vec_ref = refs

    @pl.when(first_step)
    def _():
        vec_ref[...] = jnp.zeros_like(vec_ref)

    length = info_ref[LENGTHS + pl.program_id(0)]
    start = info_ref[START]
    width = block + 2 * WINDOW
    pairs = q_ref.shape[2] // PAIR
    ga_ref[...] = low(mul_t(gb_ref[0], wo_ref[...]))
    dk_acc[...] = jnp.zeros_like(dk_acc)
    dv_acc[...] = jnp.zeros_like(dv_acc)
    join_rims(k_ref, kc_ref, kr_ref, span)
    join_rims(v_ref, vc_ref, vr_ref, span)
    kt_ref[...] = k_ref[...].T
    is_first = pair_lanes(block)
    in_window, k_at = window_of(block)
    for index in range(span // block):
        at = index * block
        keep = slice(at, at + width)
        bias = window_bias(in_window, k_at + (start + at), length)
        for pair in range(pairs):
            cols = slice(pair * PAIR, (pair + 1) * PAIR)
            q2 = split_pair(q_ref[0, at : at + block, cols], is_first)
            g2 = split_pair(ga_ref[at : at + block, cols], is_first)
            log_total = jnp.concatenate(
                [lse_ref[0, index, 2 * pair : 2 * pair + 1], lse_ref[0, index, 2 * pair + 1 : 2 * pair + 2]], axis=1
            )
            probs = jnp.exp(mul_t(k_ref[keep, cols], q2) + bias - log_total)
            grad_probs = mul_t(v_ref[keep, cols], g2)
            inner = jnp.sum(probs * grad_probs, axis=0, keepdims=True)
            grad_scores = low(probs * (grad_probs - inner))
            dk_acc[keep, cols] += mul(grad_scores, q2)
            dv_acc[keep, cols] += mul(low(probs), g2)
            grad_q = join_rows(mul(kt_ref[cols, keep], grad_scores)) * HEAD ** (-0.5)
            dq_ref[0, at : at + block, cols] = low(grad_q.T)

    dk_ref[0] = low(dk_acc[...])
    grad_values = low(dv_acc[...])
    dv_ref[0] = grad_values
    vec_ref[0:1] += col_sum(dq_ref[0].astype(f32))
    vec_ref[1:2] += col_sum(grad_values.astype(f32))
    if other:
        return

    vec_conv, vec_one, inner_own, inner_other, vec_other = vecs
    local = q_ref.shape[2]
    model = vec_one.shape[1]

    def collect(first, second, inner_first, inner_second):
        all_ref[...] = jnp.zeros_like(all_ref)
        all_ref[0:6] = vec_conv[0:6]
        all_ref[6:9] = vec_one[0:3]
        per_half = inner_first.shape[1] // model
        for half, inner in enumerate((inner_first, inner_second)):
            for i in range(per_half):
                row = 9 + half * per_half + i
                all_ref[row : row + 1] = inner[0:1, i * model : (i + 1) * model]
        row = 9 + 2 * per_half
        all_ref[row : row + 2, :local] = first[0:2]
        all_ref[row : row + 2, local:] = second[0:2]

    last_step = pl.program_id(0) == pl.num_programs(0) - 1
    pl.when(last_step & (info_ref[MP] == 0))(lambda: collect(vec_ref, vec_other, inner_own, inner_other))
    pl.when(last_step & (info_ref[MP] == 1))(lambda: collect(vec_other, vec_ref, inner_other, inner_own))


def attend_back(info, grad_branch, kept, w_out, block, vecs=None):
    rows, span, local = kept[0].shape
    extent = span + 2 * WINDOW
    model = grad_branch.shape[2]
    other = isinstance(w_out, (list, tuple))
    out_shape = [
        shape_of((rows, span, local), bf16),
        shape_of((rows, extent, local), bf16),
        shape_of((rows, extent, local), bf16),
        shape_of((8, local) if other else (16, model), f32),
    ]
    args = [grad_branch, *map(heads, kept)]
    in_specs = [lead_block(a) for a in args]
    scratch = [
        pltpu.VMEM((span, local), bf16),
        pltpu.VMEM((extent, local), bf16),
        pltpu.VMEM((extent, local), bf16),
        pltpu.VMEM((local, extent), bf16),
        pltpu.VMEM((extent, local), f32),
        pltpu.VMEM((extent, local), f32),
    ]
    if other:
        args += list(map(far, w_out))
        in_specs += [ANYWHERE] * 4
        scratch += [pltpu.VMEM((local, model), bf16), pltpu.SemaphoreType.DMA((8,))]
    else:
        args += [far(w_out), *vecs]
        in_specs += [whole_block(a) for a in args[7:]]
        scratch += [pltpu.VMEM((8, local), f32)]
    return call(
        functools.partial(attend_back_kernel, span, block, other),
        (rows,),
        in_specs,
        [lead_block(o) for o in out_shape[:3]] + [fixed_block(out_shape[3])],
        out_shape,
        args,
        info,
        scratch=scratch,
        flops=6 * rows * span * local * (model + 5 * (block + 2 * WINDOW)),
        moved=rows * extent * model * 8,
    )


B_ATTN, GAIN_ONE, SHIFT_ONE, B_OUTER, GAIN_TWO, SHIFT_TWO, B_CONV, GAIN_THREE, SHIFT_THREE = range(9)


def feed_kernel(last, span, info_ref, x_ref, bi_ref, *refs):
    if last:
        part_ref, n_ref, vec_ref = refs[:3]
        inner_pieces, outer_pieces, refs = refs[3:7], refs[7:9], refs[9:]
        act_ref, slope_ref, n2_ref, scale_ref, grp_ref, wi_ref, wo_ref, sems, sent_ref = refs
    else:
        wi, wo, act_ref, slope_ref, part_ref, wi_ref, wo_ref, sems = refs
    x = x_ref[...]
    units = wi_ref.shape[1]
    step = 512
    count = units // step
    if last:
        plans = [plan_inner(info_ref, inner_pieces, wi_ref), plan_outer(info_ref, outer_pieces, wo_ref)]
        inner_at, outer_at = [[0]] + [[]] * count, [[1]] + [[]] * count
    else:
        plans = plan_columns(wi, wi_ref, step) + plan_rows(wo, wo_ref, step)
        inner_at, outer_at = [[i] for i in range(count)], [[count + i] for i in range(count)]
    def work(ready):
        bias = inner_bias(bi_ref, units)
        total = None
        for i in range(count):
            cols = slice(i * step, (i + 1) * step)
            ready(*inner_at[i])
            act, slope = gelu_parts(mul(x, wi_ref[:, cols]) + bias[:, cols])
            act = low(act)
            act_ref[:, cols] = act
            slope_ref[:, cols] = low(slope)
            ready(*outer_at[i])
            term = mul(act, wo_ref[cols, :])
            total = term if total is None else total + term
        if not last:
            part_ref[...] = low(total)
            return

        middle = n_ref[...].astype(f32) * vec_ref[GAIN_ONE : GAIN_ONE + 1] + vec_ref[SHIFT_ONE : SHIFT_ONE + 1]
        before = middle + part_ref[...].astype(f32) + total + vec_ref[B_OUTER : B_OUTER + 1]
        normal, scale = norm_parts(before)
        n2_ref[...] = low(normal)
        scale_ref[...] = jnp.broadcast_to(scale, scale_ref.shape)
        size = x.shape[0]
        sent = normal * vec_ref[GAIN_TWO : GAIN_TWO + 1] + vec_ref[SHIFT_TWO : SHIFT_TWO + 1]
        sent = sent * alive(info_ref, span, size, 1)
        chunks = range(sent_ref.shape[0])
        for c in chunks:
            sent_ref[c] = sent[:, c * PAIR : (c + 1) * PAIR]
        for k in range(KERNEL):
            rows = pl.ds(k, size // KERNEL, stride=KERNEL)
            grp_ref[k] = low(jnp.concatenate([sent_ref[c, rows, :] for c in chunks], axis=1))

    Loads(sems, *plans).run(work)


def feed(info, middle, biases, units, span, tile, w_inner=None, w_outer=None, tail=None, pieces=None):
    tokens, model = middle.shape
    args = [middle, biases]
    in_specs = [lead_block(middle, tile), whole_block(biases)]
    out_shape = [shape_of((tokens, units), bf16), shape_of((tokens, units), bf16), shape_of((tokens, model), bf16)]
    scratch = [
        pltpu.VMEM((model, units), bf16),
        pltpu.VMEM((units, model), bf16),
        pltpu.SemaphoreType.DMA((8,)),
    ]
    if tail is None:
        args += [far(w_inner), far(w_outer)]
        in_specs += [ANYWHERE] * 2
        out_specs = [lead_block(o, tile) for o in out_shape]
    else:
        out_shape += [shape_of((tokens, PAIR), f32), shape_of((KERNEL, tokens // KERNEL, model), bf16)]
        args += [tail[0], heads(tail[1]), tail[2], *map(far, pieces)]
        in_specs += [lead_block(a, tile) for a in tail[:2]] + [whole_block(tail[2])] + [ANYWHERE] * 6
        out_specs = [lead_block(o, tile) for o in out_shape[:4]] + [chunk_block(out_shape[4], tile // KERNEL)]
        scratch.append(pltpu.VMEM((model // PAIR, tile, PAIR), f32))
    return call(
        functools.partial(feed_kernel, tail is not None, span),
        (tokens // tile,),
        in_specs,
        out_specs,
        out_shape,
        args,
        info,
        scratch=scratch,
        kept=dict.fromkeys((0, 1), UNITS_MEMORY),
        flops=4 * tokens * model * units * 1.5,
        moved=tokens * units * 8,
    )


def conv_kernel(mols, span, info_ref, grp_ref, wc_ref, vecs_ref, mg_ref, mg_got_ref, n2_ref, sc_ref,
                mol_ref, mol_out_ref, gc_ref, feed_ref, vec_ref, back_ref, mg_all):

    @pl.when(pl.program_id(0) == 0)
    def _():
        vec_ref[...] = jnp.zeros_like(vec_ref)

    half = mg_ref.shape[1]
    lower, upper = slice(0, half), slice(half, 2 * half)

    def place(mine, got):
        mg_all[:, mine] = mg_ref[...]
        mg_all[:, got] = mg_got_ref[...]

    pl.when(info_ref[PIPE] == 0)(lambda: place(lower, upper))
    pl.when(info_ref[PIPE] == 1)(lambda: place(upper, lower))

    def vector(index):
        return vecs_ref[index : index + 1]

    total = None
    for k in range(KERNEL):
        term = mul(grp_ref[k], wc_ref[k])
        total = term if total is None else total + term
    value, slope = gelu_parts(total + vector(B_CONV))
    normal, scale = norm_parts(value)
    live = alive(info_ref, span, mols, KERNEL)
    cotangent = mg_all[...].astype(f32) * live
    molecules = low((normal * vector(GAIN_THREE) + vector(SHIFT_THREE)) * live)

    def split(mine, got):
        mol_ref[...] = molecules[:, mine]
        mol_out_ref[...] = molecules[:, got]

    pl.when(info_ref[PIPE] == 0)(lambda: split(lower, upper))
    pl.when(info_ref[PIPE] == 1)(lambda: split(upper, lower))
    grad = low(norm_back(cotangent * vector(GAIN_THREE), normal, scale) * slope)
    gc_ref[...] = grad
    chunks = range(back_ref.shape[0])
    for k in range(KERNEL):
        back = low(mul_t(grad, wc_ref[k])).astype(f32)
        for c in chunks:
            back_ref[c, pl.ds(k, mols, stride=KERNEL), :] = back[:, c * PAIR : (c + 1) * PAIR]
    masked = jnp.concatenate([back_ref[c] for c in chunks], axis=1) * alive(info_ref, span, KERNEL * mols, 1)
    n2 = n2_ref[...].astype(f32)
    grad_two = norm_back(masked * vector(GAIN_TWO), n2, sc_ref[:, :1])
    feed_ref[...] = low(grad_two)
    vec_ref[...] += jnp.concatenate(
        [
            col_sum(grad.astype(f32)),
            col_sum(cotangent * normal),
            col_sum(cotangent),
            col_sum(masked * n2),
            col_sum(masked),
            col_sum(grad_two),
            jnp.zeros((2, grad_two.shape[1]), f32),
        ],
        axis=0,
    )


def conv(info, grouped, w_conv, vectors, mol_grad, mol_got, n2, scale2, span, steps):
    _, all_mols, model = grouped.shape
    tokens = KERNEL * all_mols
    tile = tokens // steps
    mols = tile // KERNEL
    args = [grouped, w_conv, vectors, far(mol_grad), far(mol_got), n2, scale2]
    in_specs = [
        chunk_block(grouped, mols),
        whole_block(w_conv),
        whole_block(vectors),
        core_block(mol_grad, steps, mols),
        lead_block(mol_got, mols),
        lead_block(n2, tile),
        lead_block(scale2, tile),
    ]
    out_shape = [
        shape_of((all_mols, model // 2), bf16),
        shape_of((all_mols, model // 2), bf16),
        shape_of((all_mols, model), bf16),
        shape_of((tokens, model), bf16),
        shape_of((8, model), f32),
    ]
    out_specs = [lead_block(o, mols) for o in out_shape[:3]] + [lead_block(out_shape[3], tile), fixed_block(out_shape[4])]
    return call(
        functools.partial(conv_kernel, mols, span),
        (steps,),
        in_specs,
        out_specs,
        out_shape,
        args,
        info,
        scratch=[
            pltpu.VMEM((model // PAIR, tile, PAIR), f32),
            pltpu.VMEM((mols, model), bf16),
        ],
        flops=4 * tokens * model * model * 1.5,
        moved=tokens * model * 30,
    )


def dp_place(info_ref, index, count):
    away = info_ref[DP] ^ index
    place, bits = 0, count.bit_length() - 1
    for bit in range(bits):
        place = place + (((away >> bit) & 1) << (bits - 1 - bit))
    return place


def cut(width):
    size = width // PARTS
    return [slice(i * size, (i + 1) * size) for i in range(PARTS)]


def conv_weight_kernel(mine, per_step, info_ref, grp_ref, grad_ref, *refs):
    value = t_mul(grp_ref[0], grad_ref[...])
    gots, outs = (refs[:PARTS], refs[PARTS:]) if mine else ((), refs)
    count, size = outs[0].shape[:2]
    for j in range(per_step):
        place = dp_place(info_ref, pl.program_id(0) * per_step + j, count)
        part = value[j * size : (j + 1) * size]
        for i, cols in enumerate(cut(value.shape[1])):
            if mine:
                outs[0][place, :, cols] = low(part[:, cols] + gots[i][place].astype(f32))
            else:
                outs[i][place] = low(part[:, cols])


def conv_weight(info, other_side, grouped, grad, dp_size, got=()):
    kernel, mols, model = grouped.shape
    half = kernel // 2
    args = [grouped, grad, *got]
    in_specs = [
        pl.BlockSpec((1, mols, model), lambda i, info_ref: ((info_ref[PIPE] ^ other_side) * half + i, 0, 0)),
    ] + [whole_block(a) for a in args[1:]]
    dims = (dp_size, half * model // dp_size)
    out_shape = [shape_of(dims + (model,), bf16)] if got else [shape_of(dims + (model // PARTS,), bf16)] * PARTS
    return call(
        functools.partial(conv_weight_kernel, bool(got), dp_size // half),
        (half,),
        in_specs,
        [fixed_block(o) for o in out_shape],
        out_shape,
        args,
        info,
        flops=2 * half * mols * model * model,
        moved=half * model * model * 8,
    )


def weight_kernel(mine, info_ref, left_ref, *refs):
    rights, refs = refs[:2], refs[2:]
    gots, outs = (refs[:PARTS], refs[PARTS:]) if mine else ((), refs)
    count, size = outs[0].shape[1:3]
    for index in range(2):
        value = t_mul(left_ref[...], rights[index][...])
        for d in range(count):
            place = dp_place(info_ref, d, count)
            part = value[d * size : (d + 1) * size]
            if mine:
                for i, got in enumerate(gots):

                    @pl.when(pl.program_id(0) == i)
                    def _(got=got, part=part, place=place):
                        outs[0][index, place] = low(part + got[index, place].astype(f32))

            else:
                for i, out in enumerate(outs):

                    @pl.when(pl.program_id(0) == i)
                    def _(out=out, part=part, place=place):
                        out[index, place] = low(part)


def weight(info, other_side, left, right_own, right_other, dp_size, got=()):
    tokens, model = left.shape
    columns = right_own.shape[1]
    half = model // 2
    tile = columns // PARTS
    args = [left, hidden(right_own), hidden(right_other), *got]
    in_specs = [
        pl.BlockSpec((tokens, half), lambda i, info_ref: (0, info_ref[PIPE] ^ other_side)),
        pl.BlockSpec((tokens, tile), lambda i, *_: (0, i)),
        pl.BlockSpec((tokens, tile), lambda i, *_: (0, i)),
    ] + [whole_block(a) for a in got]
    dims = (2, dp_size, half // dp_size)
    if got:
        out_shape = [shape_of(dims + (columns,), bf16)]
        out_specs = [pl.BlockSpec(dims + (tile,), lambda i, *_: (0, 0, 0, i))]
    else:
        out_shape = [shape_of(dims + (tile,), bf16)] * PARTS
        out_specs = [fixed_block(o) for o in out_shape]
    return call(
        functools.partial(weight_kernel, bool(got)),
        (PARTS,),
        in_specs,
        out_specs,
        out_shape,
        args,
        info,
        flops=4 * tokens * half * columns,
        moved=tokens * columns * 4 + half * columns * 8,
    )


def project_weight_kernel(span, dp_size, mine, extra, info_ref, x_ref, gb_ref, dq, dk, dv, att, *refs):
    got_ref, refs = (refs[0], refs[1:]) if mine else (None, refs)
    extra_ref, outs = (refs[0], refs[1:]) if extra else (None, refs)
    rows = x_ref.shape[0]
    local = dq.shape[2]
    size = x_ref.shape[2] // dp_size
    for index, right in enumerate((dq, dk, dv, att)):
        value = None
        for row in range(rows):
            if index == 0:
                left = x_ref[row, WINDOW : WINDOW + span]
            elif index == 3:
                left = gb_ref[row]
            else:
                left = x_ref[row]
            term = t_mul(left, right[row])
            value = term if value is None else value + term
        cols = slice(index * local, (index + 1) * local)
        inside = slice(index % 2 * local, (index % 2 + 1) * local)
        for d in range(dp_size):
            at = pl.ds(pl.multiple_of(dp_place(info_ref, d, dp_size) * size, size), size)
            part = value[d * size : (d + 1) * size]
            if mine:
                outs[index // 2][at, inside] = low(part + got_ref[at, cols].astype(f32))
            else:
                outs[0][at, cols] = low(part)
    if extra:
        outs[0][dp_size * size :] = extra_ref[...]


def project_weight(info, other_side, x_ext, grad_branch, grads, span, dp_size, got=None, extra=None):
    rows, extent, model = x_ext.shape
    half = model // 2
    local = grads[0].shape[2]
    mine = got is not None
    more = ([got] if mine else []) + ([] if extra is None else [extra])
    args = [heads(x_ext), grad_branch, *grads[:3], heads(grads[3]), *more]
    in_specs = [
        pl.BlockSpec((rows, extent, half), lambda i, info_ref: (0, 0, info_ref[PIPE] ^ other_side)),
        pl.BlockSpec((rows, span, half), lambda i, info_ref: (0, 0, info_ref[PIPE] ^ other_side)),
    ] + [whole_block(a) for a in args[2:]]
    if mine:
        extra_rows = 0 if extra is None else extra.shape[0]
        out_shape = [shape_of((half + extra_rows, 2 * local), bf16), shape_of((half, 2 * local), bf16)]
    else:
        out_shape = [shape_of((half, 4 * local), bf16)]
    return call(
        functools.partial(project_weight_kernel, span, dp_size, mine, extra is not None),
        (1,),
        in_specs,
        [fixed_block(o) for o in out_shape],
        out_shape,
        args,
        info,
        flops=8 * rows * extent * half * local,
        moved=rows * extent * model * 6,
    )


def feed_back_kernel(info_ref, gf_ref, sl_own, sl_other, n_ref, sc_ref, wo, wi, vecs_ref, *refs):
    inner_pieces, outer_pieces, refs = refs[:4], refs[4:6], refs[6:]
    gh_own, gh_other, gb_ref, vec_ref, bi_own, bi_other, wi_own, wo_own, wi_other, wo_other, sems = refs
    units = wo_own.shape[0]
    step = 512
    count = units // step
    loads = Loads(
        sems,
        *plan_rows(wo, wo_own, step),
        *plan_columns(wi, wi_own, step),
        plan_outer(info_ref, outer_pieces, wo_other),
        plan_inner(info_ref, inner_pieces, wi_other),
    )

    @pl.when(pl.program_id(0) == 0)
    def _():
        vec_ref[...] = jnp.zeros_like(vec_ref)
        bi_own[...] = jnp.zeros_like(bi_own)
        bi_other[...] = jnp.zeros_like(bi_other)

    def half(ready, total, slope_ref, wo_ref, wi_ref, gh_ref, bi_ref, outer_at, inner_at):
        for i in range(count):
            cols = slice(i * step, (i + 1) * step)
            ready(*outer_at[i])
            grad = low(mul_t(gf_ref[...], wo_ref[cols, :]) * slope_ref[:, cols].astype(f32))
            gh_ref[:, cols] = grad
            bi_ref[:1, cols] += col_sum(grad.astype(f32))
            ready(*inner_at[i])
            total = total + mul_t(grad, wi_ref[:, cols])
        return total

    def work(ready):
        chunks = [[i] for i in range(count)], [[count + i] for i in range(count)]
        total = half(ready, gf_ref[...].astype(f32), sl_own, wo_own, wi_own, gh_own, bi_own, *chunks)
        chunks = [[2 * count]] + [[]] * count, [[2 * count + 1]] + [[]] * count
        total = half(ready, total, sl_other, wo_other, wi_other, gh_other, bi_other, *chunks)
        normal = n_ref[...].astype(f32)
        grad_one = norm_back(total * vecs_ref[GAIN_ONE : GAIN_ONE + 1], normal, sc_ref[:, :1])
        gb_ref[...] = low(grad_one)
        vec_ref[...] += jnp.concatenate(
            [col_sum(grad_one), col_sum(total * normal), col_sum(total), jnp.zeros((5, total.shape[1]), f32)], axis=0
        )

    loads.run(work)


def feed_back(info, grad_feed, slopes, n1, scale1, w_outer, w_inner, vectors, pieces, tile):
    tokens, model = grad_feed.shape
    units = w_outer.shape[0]
    args = [grad_feed, *map(hidden, slopes), heads(n1), heads(scale1), far(w_outer), far(w_inner), vectors, *map(far, pieces)]
    in_specs = [lead_block(a, tile) for a in args[:5]] + [ANYWHERE] * 2 + [whole_block(vectors)] + [ANYWHERE] * 6
    out_shape = [
        shape_of((tokens, units), bf16),
        shape_of((tokens, units), bf16),
        shape_of((tokens, model), bf16),
        shape_of((8, model), f32),
        shape_of((8, units), f32),
        shape_of((8, units), f32),
    ]
    return call(
        feed_back_kernel,
        (tokens // tile,),
        in_specs,
        [lead_block(o, tile) for o in out_shape[:3]] + [fixed_block(o) for o in out_shape[3:]],
        out_shape,
        args,
        info,
        scratch=[pltpu.VMEM((model, units), bf16), pltpu.VMEM((units, model), bf16)] * 2
        + [pltpu.SemaphoreType.DMA((8 + 2 * (units // 512),))],
        flops=8 * tokens * model * units * 1.2,
        moved=tokens * units * 8,
        limit=26 << 20,
        kept=dict.fromkeys((0, 1), UNITS_MEMORY),
    )


def input_rims_kernel(span, info_ref, *refs):
    groups, weights, pieces, refs = (refs[:2], refs[2:4]), refs[4:6], refs[6:10], refs[10:]
    left_ref, right_ref, wk_ref, wv_ref, sems = refs
    loads = Loads(sems, *plan_square(info_ref, pieces, (wk_ref, wv_ref), 1))
    loads.start()
    ranges = (pl.ds(0, WINDOW), pl.ds(WINDOW + span, WINDOW))
    rows = left_ref.shape[0]

    def rims(grads, *weights):
        total = None
        for grad, weight in zip(grads, weights):
            cells = jnp.concatenate([grad[row, at] for at in ranges for row in range(rows)], axis=0)
            term = mul_t(cells, weight[...])
            total = term if total is None else total + term
        return total

    total = rims(groups[0], *weights)
    loads.ready(0, 1)
    total = low(total + rims(groups[1], wk_ref, wv_ref))
    for row in range(rows):
        left_ref[row] = total[row * WINDOW : (row + 1) * WINDOW]
        right_ref[row] = total[(rows + row) * WINDOW : (rows + row + 1) * WINDOW]


def input_rims(info, own, other, weights, pieces, span):
    rows, _, local = own[1].shape
    model = weights[0].shape[0]
    args = [own[1], own[2], other[1], other[2], *map(far, (*weights[1:], *pieces))]
    in_specs = [whole_block(a) for a in args[:6]] + [ANYWHERE] * 4
    out_shape = [shape_of((rows, WINDOW, model), bf16)] * 2
    return call(
        functools.partial(input_rims_kernel, span),
        (1,),
        in_specs,
        [fixed_block(o) for o in out_shape],
        out_shape,
        args,
        info,
        scratch=[pltpu.VMEM((model, local), bf16)] * 2 + [pltpu.SemaphoreType.DMA((8,))],
        flops=16 * rows * WINDOW * model * local,
        moved=rows * WINDOW * model * 12,
    )


def input_center_kernel(span, info_ref, one_ref, *refs):
    groups, weights, pieces, refs = (refs[:3], refs[3:6]), refs[6:9], refs[9:13], refs[13:]
    mine_ref, theirs_ref, *scratch, sems = refs
    plan = [[pair] for pair in zip(weights, scratch[:3])]
    loads = Loads(sems, *plan, *plan_square(info_ref, pieces, scratch[3:]))
    own_rows = pl.ds(WINDOW, span)
    half = mine_ref.shape[2]
    lower, upper = slice(0, half), slice(half, 2 * half)

    def work(ready):
        center = one_ref[0].astype(f32)
        for which, (dq, dk, dv) in enumerate(groups):
            for i, cells in enumerate((dq[0], dk[0, own_rows], dv[0, own_rows])):
                ready(3 * which + i)
                center = center + mul_t(cells, scratch[3 * which + i][...])

        def split(mine, theirs):
            mine_ref[0] = center[:, mine]
            theirs_ref[0] = low(center[:, theirs])

        pl.when(info_ref[PIPE] == 0)(lambda: split(lower, upper))
        pl.when(info_ref[PIPE] == 1)(lambda: split(upper, lower))

    loads.run(work)


def input_center(info, grad_one, own, other, weights, pieces, span):
    rows, extent, local = own[1].shape
    model = grad_one.shape[2]
    args = [grad_one, *own, *other, *map(far, (*weights, *pieces))]
    in_specs = [lead_block(a) for a in args[:7]] + [ANYWHERE] * 7
    out_shape = [shape_of((rows, span, model // 2), f32), shape_of((rows, span, model // 2), bf16)]
    return call(
        functools.partial(input_center_kernel, span),
        (rows,),
        in_specs,
        [lead_block(o) for o in out_shape],
        out_shape,
        args,
        info,
        scratch=[pltpu.VMEM((model, local), bf16)] * 6 + [pltpu.SemaphoreType.DMA((15,))],
        flops=12 * rows * span * model * local,
        moved=rows * extent * model * 12,
    )


def finish_kernel(rows, info_ref, mine, got, head, tail, head_got, tail_got, mol, mol_got, out_ref, mol_ref):
    row = pl.program_id(0)
    width = head.shape[1]
    own = (row >= rows) == (info_ref[PIPE] == 1)

    def write(center, first, last, molecules):
        out_ref[0] = center[0].astype(f32)
        out_ref[0, :width] += first[0].astype(f32)
        out_ref[0, out_ref.shape[1] - width :] += last[0].astype(f32)
        mol_ref[0] = molecules[0]

    pl.when(own)(lambda: write(mine, head, tail, mol))
    pl.when(jnp.logical_not(own))(lambda: write(got, head_got, tail_got, mol_got))


def finish(info, mine, got, head, tail, head_got, tail_got, mol, mol_got):
    rows, span, half = mine.shape
    width = head.shape[1]

    def core_rows(array):
        return pl.BlockSpec((1,) + tuple(array.shape[1:]), lambda i, info_ref: (i % rows, 0, 0))

    rims = pl.BlockSpec((1, width, half), lambda i, info_ref: (i % rows, 0, info_ref[PIPE]))
    out_shape = [shape_of((2 * rows, span, half), f32), shape_of((2 * rows,) + tuple(mol.shape[1:]), bf16)]
    return call(
        functools.partial(finish_kernel, rows),
        (2 * rows,),
        [core_rows(mine), core_rows(got), rims, rims] + [core_rows(a) for a in (head_got, tail_got, mol, mol_got)],
        [lead_block(o) for o in out_shape],
        out_shape,
        [mine, got, head, tail, head_got, tail_got, mol, mol_got],
        info,
        moved=rows * span * half * 20,
    )


def swapped(block, axis, bit=0):
    count = lax.axis_size(axis)
    return lax.ppermute(block, axis, [(i, i ^ (1 << bit)) for i in range(count)])


def to_core(blocks):
    return [swapped(block, "pipe") for block in blocks]


def from_chunk(block, distance):
    axes = ("seq", "mp")
    count = lax.axis_size("seq") * lax.axis_size("mp")
    return lax.ppermute(block, axes, [(i + distance, i) for i in range(count) if 0 <= i + distance < count])


def pick(array, index, dim):
    return lax.dynamic_index_in_dim(array, index, dim, keepdims=False)


def add(left, right):
    return low(left.astype(f32) + right.astype(f32))


def bits_of(axis):
    return lax.axis_size(axis).bit_length() - 1


class Halving:
    def __init__(self, parts, dim, axis):
        self.dim, self.axis = dim, axis
        self.keep, self.sent = self.split(parts, 0)

    def go(self):
        self.got = swapped(self.sent, self.axis)

    def split(self, parts, bit):
        dim = self.dim
        shaped = parts.reshape(parts.shape[:dim] + (parts.shape[dim] // 2, 2) + parts.shape[dim + 1 :])
        mine = (lax.axis_index(self.axis) >> bit) & 1
        return pick(shaped, mine, dim + 1), pick(shaped, 1 - mine, dim + 1)

    def finish(self, *gates):
        parts = add(self.keep, after(self.got, *gates))
        for bit in range(1, bits_of(self.axis)):
            keep, sent = self.split(parts, bit)
            parts = add(keep, swapped(sent, self.axis, bit))
        return parts.reshape(parts.shape[: self.dim] + parts.shape[self.dim + 1 :])


class HalvingDp:
    def __init__(self, parts):
        self.bit = 0
        self.split(parts)

    def split(self, parts):
        half = parts.shape[0] // 2
        self.keep, self.sent = parts[:half], parts[half:]

    def go(self):
        self.got = swapped(self.sent, "dp", self.bit)
        self.bit += 1

    def landed(self, *gates):
        return add(self.keep, after(self.got, *gates))

    def step(self, *gates):
        self.split(self.landed(*gates))

    def finish(self, *gates):
        while self.keep.shape[0] > 1:
            self.step()
            self.go()
        return self.landed(*gates)[0]


def sending(value, *halvings):
    value, *sent = tie(value, *(h.sent for h in halvings))
    for halving, block in zip(halvings, sent):
        halving.sent = block
        halving.go()
    return value


def relay(quarter):
    first = swapped(quarter, "mp")
    return first, swapped(first, "seq")


def all_pieces(first, second):
    return [first, second, swapped(first, "pipe"), swapped(second, "pipe")]


def in_order(first, mine, recv, axis):
    return jnp.where(
        first == 0, jnp.concatenate([mine, recv], axis=axis), jnp.concatenate([recv, mine], axis=axis)
    )


def after(value, *others):
    return lax.optimization_barrier((value, *others))[0] if others else value


def tie(*values):
    return lax.optimization_barrier(values)


def on_device(
    characters,
    row_lengths,
    w_query,
    b_query,
    w_key,
    w_value,
    b_value,
    w_attn_out,
    b_attn_out,
    gain_one,
    shift_one,
    w_inner,
    b_inner,
    w_outer,
    b_outer,
    gain_two,
    shift_two,
    w_conv,
    b_conv,
    gain_three,
    shift_three,
    molecule_grad,
):
    pipe = lax.axis_index("pipe")
    seq = lax.axis_index("seq")
    mp = lax.axis_index("mp")
    dp_size, seq_size, mp_size = (lax.axis_size(a) for a in ("dp", "seq", "mp"))
    all_rows, span, half_model = characters.shape
    rows = all_rows // 2
    model = 2 * half_model
    local = w_query.shape[1]
    units = w_inner.shape[1]
    tokens = rows * span
    mols = tokens // KERNEL
    block = min(WINDOW, span)
    tile = min(256, tokens)
    own_start = (seq * lax.axis_size("mp") + mp) * span

    def rows_of(array, index):
        return lax.dynamic_slice_in_dim(array, index * rows, rows, 0)

    me = 2 * (seq & 1) + pipe
    lengths = rows_of(row_lengths, pipe)
    scalars = jnp.stack([own_start, pipe, me, lax.axis_index("dp"), mp]).astype(jnp.int32)
    info = jnp.concatenate([scalars, lengths])
    squares = (w_query, w_key, w_value)
    biases, vectors = gather_small(
        b_query,
        b_value,
        b_inner,
        (b_attn_out, gain_one, shift_one, b_outer, gain_two, shift_two, b_conv, gain_three, shift_three),
    )
    hops = -(-WINDOW // span)
    width = min(span, WINDOW)

    center_send, mol_send = pack_rows(info, [characters, molecule_grad])
    center_got = swapped(center_send, "pipe")
    packet = pack_first(after(info, center_send), squares, w_attn_out, biases)
    tail, head = pack_rims(after(info, packet), characters, center_got, width)
    square_first = swapped(packet, "mp")
    inner_packet, outer_packet = pack_second(after(info, tail), w_inner, w_outer)
    center_got, tail, head, inner_packet, outer_packet = tie(center_got, tail, head, inner_packet, outer_packet)
    inner_own = attend_inner(info, characters, center_got, squares, biases, span, block)
    *inner_own, square_first = tie(*inner_own, square_first)
    square_second = swapped(square_first, "seq")
    square_first, tail, head = tie(square_first, tail, head)
    left, right = [], []
    for hop in range(1, hops + 1):
        left.insert(0, from_chunk(tail, -hop))
        right.append(from_chunk(head, hop))
    left, right = (a[0] if hops == 1 else jnp.concatenate(a, axis=2) for a in (left, right))
    square_second, left, right, inner_packet, outer_packet = tie(square_second, left, right, inner_packet, outer_packet)
    inner_first = swapped(inner_packet, "mp")
    outer_first = swapped(outer_packet, "mp")
    mol_grad = molecule_grad.reshape(2 * mols, half_model)

    square_pieces = all_pieces(square_first, square_second)
    biases_other = square_first[square_first.shape[0] - 16 :]
    inner_other = attend_inner(info, characters, center_got, square_pieces, biases_other, span, block)
    (kr_own, vr_own, att_own, lse_own, kr_other, vr_other, att_other, lse_other, n1, scale1, middle, x_ext) = attend_outer(
        info,
        (characters, center_got, left, right),
        vectors,
        (biases, biases_other),
        (inner_own, inner_other),
        (w_key, w_value, w_attn_out),
        square_pieces,
        span,
        block,
    )
    kept_own = (inner_own[0], inner_own[1], kr_own, inner_own[2], vr_own, lse_own)
    kept_other = (inner_other[0], inner_other[1], kr_other, inner_other[2], vr_other, lse_other)
    middle, inner_first = tie(middle, inner_first)
    inner_second = swapped(inner_first, "seq")
    n1, scale1, middle = (a.reshape(tokens, -1) for a in (n1, scale1, middle))
    act_own, slope_own, part = feed(
        info, middle, biases, units, span, tile, w_inner, w_outer
    )
    part, inner_second, outer_first = tie(part, inner_second, outer_first)
    pieces = (*all_pieces(inner_first, inner_second), outer_first, swapped(outer_first, "pipe"))
    mol_got = swapped(after(mol_send, part), "pipe").reshape(mols, half_model)
    act_other, slope_other, n2, scale2, grouped = feed(
        info, middle, biases_other, units, span, tile, tail=(part, n1, vectors), pieces=pieces
    )
    mol_mine, mol_theirs, grad_conv, grad_feed, vec_conv = conv(
        info, grouped, w_conv.reshape(KERNEL, model, model), vectors, mol_grad, mol_got, n2, scale2, span, 2
    )
    mol_shape = (rows, span // KERNEL, half_model)
    mol_mine = mol_mine.reshape(mol_shape)
    mol_theirs = mol_theirs.reshape(mol_shape)

    conv_theirs = conv_weight(info, 1, grouped, grad_conv, dp_size)
    conv_got = to_core(conv_theirs)
    outer_theirs = weight(info, 1, after(grad_feed, *conv_theirs), act_own, act_other, dp_size)
    outer_got = to_core(outer_theirs)
    (conv_part,) = conv_weight(info, 0, grouped, after(grad_conv, *outer_theirs), dp_size, conv_got)
    conv_halving = Halving(conv_part.reshape(dp_size, seq_size, mp_size, -1, model), 2, "mp")
    grad_feed = sending(grad_feed, conv_halving)
    (outer_part,) = weight(info, 0, grad_feed, act_own, act_other, dp_size, outer_got)
    outer_halving = Halving(outer_part.reshape(2, dp_size, seq_size, -1, units), 2, "seq")
    grad_feed = sending(grad_feed, outer_halving)
    gh_own, gh_other, grad_branch, vec_one, bi_own, bi_other = feed_back(
        info,
        grad_feed,
        (slope_own, slope_other),
        n1,
        scale1,
        w_outer,
        w_inner,
        vectors,
        pieces,
        tile,
    )
    inner_theirs = weight(info, 1, middle, gh_own, gh_other, dp_size)
    conv_part = conv_halving.finish(*inner_theirs)
    conv_halving = Halving(conv_part, 1, "seq")
    outer_part = outer_halving.finish(*inner_theirs)
    *inner_theirs, conv_halving.sent, outer_sent = tie(*inner_theirs, conv_halving.sent, outer_part[1])
    conv_halving.go()
    outer_got = swapped(outer_sent, "mp")
    inner_got = to_core(inner_theirs)

    grad_branch = grad_branch.reshape(rows, span, model)
    *back_other, vec_other = attend_back(
        info, after(grad_branch, *inner_theirs), kept_other, square_pieces, block
    )
    (inner_part,) = weight(info, 0, after(middle, vec_other), gh_own, gh_other, dp_size, inner_got)
    inner_halving = Halving(inner_part.reshape(2, dp_size, seq_size, -1, units), 2, "seq")

    def narrow(part):
        return jnp.concatenate([part[:, :, :model], part[:, :, model:]], axis=1)

    x_late = sending(x_ext, inner_halving)
    conv_part = conv_halving.finish(x_late)
    outer_part = add(outer_part[0], after(outer_got, x_late)).reshape(dp_size, -1, units)
    merged_halving = HalvingDp(jnp.concatenate([conv_part, narrow(outer_part)], axis=1))
    x_late = sending(x_late, merged_halving)
    (other_theirs,) = project_weight(info, 1, x_late, grad_branch, (*back_other, att_other), span, dp_size)
    other_got = swapped(other_theirs, "pipe")
    *back_own, vec = attend_back(
        info,
        after(grad_branch, other_theirs),
        kept_own,
        w_attn_out,
        block,
        (vec_conv, vec_one, bi_own, bi_other, vec_other),
    )
    left, right = input_rims(info, back_own, back_other, squares, square_pieces, span)
    x_late, left, right = tie(x_late, left, right)
    rims = []
    for hop in range(1, hops + 1):
        top = WINDOW - (hop - 1) * span
        rims.append(from_chunk(right[:, WINDOW - top : WINDOW - top + width], -hop))
        rims.append(from_chunk(left[:, top - width : top], hop))
    merged_halving.step(x_late)
    x_late, merged_halving.sent = tie(x_late, merged_halving.sent)
    (own_theirs,) = project_weight(info, 1, x_late, grad_branch, (*back_own, att_own), span, dp_size)
    own_theirs, vec, inner_part, merged_halving.sent = tie(
        own_theirs, vec, inner_halving.finish(own_theirs), merged_halving.sent
    )
    merged_halving.go()
    own_got = swapped(own_theirs, "pipe")
    inner_got = swapped(inner_part[1], "mp")
    vec = low(vec + swapped(vec, "pipe"))
    other_first, other_last = project_weight(
        info, 0, after(x_late, own_theirs), grad_branch, (*back_other, att_other), span, dp_size, other_got, vec
    )
    own_got, x_late, other_first, *rims = tie(own_got, x_late, other_first, *rims)
    first_got = swapped(other_first, "mp")
    head, tail = rims[:2]
    for hop in range(1, hops):
        head, tail = add(head, rims[2 * hop]), add(tail, rims[2 * hop + 1])
    own_first, own_last = project_weight(
        info, 0, x_late, grad_branch, (*back_own, att_own), span, dp_size, own_got
    )
    last_halving = Halving(jnp.stack([own_last, other_last]).reshape(2, dp_size, seq_size, -1, model), 2, "seq")
    inner_halving = HalvingDp(add(inner_part[0], after(inner_got, own_first)))
    merged = merged_halving.finish(own_first)
    grad_branch, merged, rims = tie(grad_branch, merged, jnp.stack([head, tail]))
    grad_branch = sending(grad_branch, last_halving, inner_halving)
    mine, theirs = input_center(info, grad_branch, back_own, back_other, squares, square_pieces, span)
    first_got = after(first_got, mine)
    own_rows = first_got.shape[0] - 16
    first_part = add(own_first, first_got[:own_rows]).reshape(dp_size, seq_size, -1, model)
    vec = add(vec, first_got[own_rows:])

    def with_vec(part):
        return jnp.concatenate([part.reshape(-1, model), vec], axis=0)

    chars_grad = None
    for bit in range(bits_of("seq")):
        shaped = first_part.reshape(dp_size, first_part.shape[1] // 2, 2, -1, model)
        bit_mine = (seq >> bit) & 1
        got = swapped(with_vec(pick(shaped, 1 - bit_mine, 2)), "seq", bit)
        if chars_grad is None:
            last_part = last_halving.finish(mine)
            inner_halving.step(mine)
            last_sent, inner_halving.sent, mine, rims, mol_theirs, theirs = tie(
                last_part[1], inner_halving.sent, mine, rims, mol_theirs, theirs
            )
            last_got = swapped(last_sent, "mp")
            inner_halving.go()
            rims_got = swapped(lax.dynamic_slice_in_dim(rims, (1 - pipe) * half_model, half_model, 3), "pipe")
            chars_grad, molecules = finish(
                info,
                mine,
                swapped(theirs, "pipe"),
                head,
                tail,
                rims_got[0],
                rims_got[1],
                mol_mine,
                swapped(mol_theirs, "pipe"),
            )
            got, chars_grad, molecules = tie(got, chars_grad, molecules)
        count = got.shape[0] - 16
        first_part = add(pick(shaped, bit_mine, 2), got[:count].reshape(dp_size, shaped.shape[1], -1, model))
        vec = add(vec, got[count:])
    last_part = add(last_part[0], after(last_got, chars_grad))
    head_part = jnp.concatenate([first_part.reshape(dp_size, -1, model), last_part], axis=1)
    for bit in range(bits_of("dp")):
        half = head_part.shape[0] // 2
        got = swapped(with_vec(head_part[half:]), "dp", bit)
        count = got.shape[0] - 16
        head_part = add(head_part[:half], got[:count].reshape(head_part[:half].shape))
        vec = add(vec, got[count:])
    inner_sum = inner_halving.finish()
    head_sum = head_part[0].astype(f32)
    vec = vec.astype(f32)
    grad_b_conv, grad_gain_three, grad_shift_three, grad_gain_two, grad_shift_two, grad_b_outer = (
        vec[i] for i in range(6)
    )
    grad_b_attn_out, grad_gain_one, grad_shift_one = (vec[i] for i in range(6, 9))
    grad_b_inner = vec[9:13].reshape(-1)
    grad_b_query, grad_b_value = (vec[i] for i in range(13, 15))
    size = conv_part.shape[1]
    grad_w_conv = merged[:size].astype(f32)
    outer_sum = jnp.concatenate([merged[size : size + size // 2], merged[size + size // 2 :]], axis=1).astype(f32)
    inner_sum = inner_sum.astype(f32)

    per_device = head_sum.shape[0] // 2
    grad_w_query, grad_w_key, grad_w_value, grad_w_attn = (
        head_sum[i // 2 * per_device : (i // 2 + 1) * per_device, i % 2 * local : (i % 2 + 1) * local] for i in range(4)
    )
    return (
        molecules,
        chars_grad,
        grad_w_query,
        grad_b_query,
        grad_w_key,
        grad_w_value,
        grad_b_value,
        grad_w_attn.T,
        grad_b_attn_out,
        grad_gain_one,
        grad_shift_one,
        inner_sum,
        grad_b_inner,
        outer_sum.T,
        grad_b_outer,
        grad_gain_two,
        grad_shift_two,
        grad_w_conv,
        grad_b_conv,
        grad_gain_three,
        grad_shift_three,
    )


def solution(mesh):
    return jax.shard_map(
        on_device,
        mesh=mesh,
        in_specs=(
            P("dp", ("seq", "mp"), "pipe"),
            P("dp"),
            P(None, "mp"),
            P("mp"),
            P(None, "mp"),
            P(None, "mp"),
            P("mp"),
            P("mp", None),
            P(),
            P(),
            P(),
            P(None, "mp"),
            P("mp"),
            P("mp", None),
            P(),
            P(),
            P(),
            P(),
            P(),
            P(),
            P(),
            P("dp", ("seq", "mp"), "pipe"),
        ),
        out_specs=(
            P("dp", ("seq", "mp"), "pipe"),
            P("dp", ("seq", "mp"), "pipe"),
            P(("pipe", "dp", "seq"), "mp"),
            P(),
            P(("pipe", "dp", "seq"), "mp"),
            P(("pipe", "dp", "seq"), "mp"),
            P(),
            P("mp", ("pipe", "dp", "seq")),
            P(),
            P(),
            P(),
            P(("pipe", "dp", "seq"), "mp"),
            P(),
            P("mp", ("pipe", "dp", "seq")),
            P(),
            P(),
            P(),
            P(("pipe", "dp", "seq", "mp"), None),
            P(),
            P(),
            P(),
        ),
        check_vma=False,
    )
```

```python
import functools

import jax
import jax.numpy as jnp
from jax import lax
from jax.experimental import pallas as pl
from jax.experimental.pallas import tpu as pltpu
from jax.sharding import PartitionSpec as P

HEAD = 64
WINDOW = 128
KERNEL = 4
PAIR = 2 * HEAD
VMEM_LIMIT = 20 << 20
COST = 1000
HEADS_NEAR = True
UNITS_NEAR = True
PARTS = 1

epsilon = 1e-05
masked_score = -1e30
f32 = jnp.float32
bf16 = jnp.bfloat16


def mul(left, right):
    return jnp.dot(left, right, preferred_element_type=f32)


def mul_t(left, right):
    return lax.dot_general(left, right, (((1,), (1,)), ((), ())), preferred_element_type=f32)


def t_mul(left, right):
    return lax.dot_general(left, right, (((0,), (0,)), ((), ())), preferred_element_type=f32)


def gelu_parts(value):
    cdf = 0.5 + 0.5 * lax.erf(value * 2.0**-0.5)
    return value * cdf, cdf + value * jnp.exp(value * value * -0.5) * 0.3989422804014327


def norm_parts(value):
    centered = value - jnp.mean(value, axis=-1, keepdims=True)
    scale = lax.rsqrt(jnp.mean(centered * centered, axis=-1, keepdims=True) + epsilon)
    return centered * scale, scale


def norm_back(cotangent, normal, scale):
    first = jnp.mean(cotangent, axis=-1, keepdims=True)
    second = jnp.mean(cotangent * normal, axis=-1, keepdims=True)
    return scale * (cotangent - first - normal * second)


def col_sum(value):
    return jnp.sum(value, axis=0, keepdims=True)


def low(value):
    return value.astype(bf16)


START, PIPE, QUARTER, DP, MP, LENGTHS = range(6)


def call(body, grid, in_specs, out_specs, out_shape, args, info, scratch=(), flops=0, moved=0, limit=VMEM_LIMIT, kept=None):
    if kept:
        out_shape = [kept[i](tuple(o.shape), o.dtype) if i in kept else o for i, o in enumerate(out_shape)]
    return pl.pallas_call(
        body,
        grid_spec=pltpu.PrefetchScalarGridSpec(
            num_scalar_prefetch=1,
            grid=grid,
            in_specs=in_specs,
            out_specs=out_specs,
            scratch_shapes=scratch,
        ),
        out_shape=out_shape,
        compiler_params=pltpu.CompilerParams(vmem_limit_bytes=limit),
        cost_estimate=pl.CostEstimate(flops=int(flops) // COST, bytes_accessed=int(moved) // COST, transcendentals=0),
    )(info, *args)


def whole_block(array):
    zeros = (0,) * array.ndim
    return pl.BlockSpec(array.shape, lambda *_: zeros, pipeline_mode=pl.Buffered(1))


def lead_block(array, size=1):
    rest = (0,) * (array.ndim - 1)
    return pl.BlockSpec((size,) + tuple(array.shape[1:]), lambda i, *_: (i,) + rest)


def core_block(array, steps, size=1):
    rest = (0,) * (array.ndim - 1)
    return pl.BlockSpec((size,) + tuple(array.shape[1:]), lambda i, info: (info[PIPE] * steps + i,) + rest)


def chunk_block(array, size):
    return pl.BlockSpec((array.shape[0], size, array.shape[2]), lambda i, *_: (0, i, 0))


def fixed_block(array):
    zeros = (0,) * array.ndim
    return pl.BlockSpec(array.shape, lambda *_: zeros)


ANYWHERE = pl.BlockSpec(memory_space=pl.ANY)


def far(array):
    return pltpu.with_memory_space_constraint(array, pltpu.HBM)


def heads(array):
    return pltpu.with_memory_space_constraint(array, HEADS_MEMORY)


def hidden(array):
    return pltpu.with_memory_space_constraint(array, UNITS_MEMORY)


HEADS_MEMORY = pltpu.VMEM if HEADS_NEAR else pltpu.HBM
UNITS_MEMORY = pltpu.VMEM if UNITS_NEAR else pltpu.HBM


def shape_of(dims, kind):
    return jax.ShapeDtypeStruct(tuple(dims), kind)


def fetch(plan, sems):
    copies = [pltpu.make_async_copy(source, target, sems.at[i]) for i, (source, target) in enumerate(plan)]
    for copy in copies:
        copy.start()
    return copies


class Loads:
    def __init__(self, sems, *groups):
        self.groups, count = [], 0
        for group in groups:
            self.groups.append([(source, target, sems.at[count + i]) for i, (source, target) in enumerate(group)])
            count += len(group)

    def start(self):
        for group in self.groups:
            for copy in group:
                pltpu.make_async_copy(*copy).start()

    def ready(self, *indices):
        for index in indices:
            for copy in self.groups[index]:
                pltpu.make_async_copy(*copy).wait()

    def fill(self):
        @pl.when(pl.program_id(0) == 0)
        def _():
            self.start()
            self.ready(*range(len(self.groups)))

    def run(self, body):
        @pl.when(pl.program_id(0) == 0)
        def _():
            self.start()
            body(self.ready)

        @pl.when(pl.program_id(0) != 0)
        def _():
            body(lambda *indices: None)


def placed(info_ref, index, size):
    return pl.ds(pl.multiple_of((info_ref[QUARTER] ^ (0, 2, 1, 3)[index]) * size, size), size)


def plan_square(info_ref, pieces, targets, first=0):
    size = targets[0].shape[0] // 4
    return [
        [
            (piece.at[pl.ds((first + which) * size, size)], target.at[placed(info_ref, i, size)])
            for i, piece in enumerate(pieces)
        ]
        for which, target in enumerate(targets)
    ]


def plan_columns(source, target, step):
    return [[(source.at[:, pl.ds(at, step)], target.at[:, pl.ds(at, step)])] for at in range(0, target.shape[1], step)]


def plan_rows(source, target, step):
    return [[(source.at[pl.ds(at, step)], target.at[pl.ds(at, step)])] for at in range(0, target.shape[0], step)]


def plan_inner(info_ref, pieces, target):
    size = target.shape[0] // 4
    return [(piece.at[pl.ds(0, size)], target.at[placed(info_ref, i, size)]) for i, piece in enumerate(pieces)]


def plan_outer(info_ref, pieces, target):
    size = target.shape[0] // 2
    return [
        (piece, target.at[pl.ds(pl.multiple_of((info_ref[PIPE] ^ i) * size, size), size)])
        for i, piece in enumerate(pieces)
    ]


def plan_attn_out(info_ref, pieces, target):
    model = target.shape[1]
    size = target.shape[0] // 4
    columns = model // 2
    return [
        (
            piece.at[pl.ds(piece.shape[0] - 16 - (2 - side) * size, size)],
            target.at[placed(info_ref, i, size), pl.ds(side * columns, columns)],
        )
        for i, piece in enumerate(pieces)
        for side in range(2)
    ]


def pack_kernel(plan_of, info_ref, *refs):
    sems = refs[-1]
    for copy in fetch(plan_of(info_ref, *refs[:-1]), sems):
        copy.wait()


def pack(info, plan_of, args, out_shape, copies):
    return call(
        functools.partial(pack_kernel, plan_of),
        (1,),
        [ANYWHERE] * len(args),
        [fixed_block(o) for o in out_shape],
        out_shape,
        [far(a) for a in args],
        info,
        scratch=[pltpu.SemaphoreType.DMA((copies,))],
        moved=sum(o.size * 4 for o in out_shape),
    )


def gather_small_kernel(bq, bv, bi, *refs):
    vectors, (bias_ref, vec_ref) = refs[:-2], refs[-2:]
    local = bias_ref.shape[1]
    rows = [bq[...].reshape(1, local), bv[...].reshape(1, local)]
    inner = bi[...].reshape(1, -1)
    rows += [inner[:, i * local : (i + 1) * local] for i in range(inner.shape[1] // local)]
    rows = [row.astype(f32) for row in rows]
    rows.append(jnp.zeros((16 - len(rows), local), f32))
    bias_ref[...] = low(jnp.concatenate(rows, axis=0))
    rows = [v[...].reshape(1, -1).astype(f32) for v in vectors]
    rows.append(jnp.zeros((16 - len(rows), vec_ref.shape[1]), f32))
    vec_ref[...] = jnp.concatenate(rows, axis=0)


def gather_small(b_query, b_value, b_inner, vectors):
    return pl.pallas_call(
        gather_small_kernel,
        out_shape=[shape_of((16, b_query.shape[0]), bf16), shape_of((16, vectors[0].shape[0]), f32)],
    )(b_query, b_value, b_inner, *vectors)


def inner_bias(bias_ref, units):
    local = bias_ref.shape[1]
    return jnp.concatenate([bias_ref[2 + i : 3 + i] for i in range(units // local)], axis=1).astype(f32)


def quarter_of(info_ref, array):
    size = array.shape[0] // 4
    return pl.ds(pl.multiple_of(info_ref[QUARTER] * size, size), size)


def pack_first(info, weights, w_out, biases):
    model, local = weights[0].shape
    size, out_size, half = model // 4, w_out.shape[0] // 4, w_out.shape[1] // 2

    def plan_of(info_ref, wq, wk, wv, wo, bias, packet):
        plan = [(bias, packet.at[pl.ds(3 * size + 2 * out_size, 16)])]
        plan += [
            (w.at[quarter_of(info_ref, w)], packet.at[pl.ds(i * size, size)]) for i, w in enumerate((wq, wk, wv))
        ]
        return plan + [
            (
                wo.at[quarter_of(info_ref, wo), pl.ds(side * half, half)],
                packet.at[pl.ds(3 * size + side * out_size, out_size)],
            )
            for side in range(2)
        ]

    out_shape = [shape_of((3 * size + 2 * out_size + 16, local), bf16)]
    return pack(info, plan_of, [*weights, w_out, biases], out_shape, 6)[0]


def pack_second(info, w_inner, w_outer):
    def plan_of(info_ref, wi, wo, inner, outer):
        size = wo.shape[0] // 2
        half = pl.ds(pl.multiple_of(info_ref[PIPE] * size, size), size)
        return [(wi.at[quarter_of(info_ref, wi)], inner), (wo.at[half], outer)]

    out_shape = [shape_of((a.shape[0] // n, a.shape[1]), bf16) for a, n in ((w_inner, 4), (w_outer, 2))]
    return pack(info, plan_of, [w_inner, w_outer], out_shape, 2)


def pack_rows(info, arrays):
    rows = arrays[0].shape[0] // 2

    def plan_of(info_ref, *refs):
        theirs = pl.ds((1 - info_ref[PIPE]) * rows, rows)
        return [(ref.at[theirs], out) for ref, out in zip(refs[: len(arrays)], refs[len(arrays) :])]

    out_shape = [shape_of((rows,) + tuple(a.shape[1:]), bf16) for a in arrays]
    return pack(info, plan_of, arrays, out_shape, len(arrays))


def pack_rims(info, characters, center_got, width):
    rows, span, half = center_got.shape

    def plan_of(info_ref, chars, got, tail, head):
        mine = pl.ds(info_ref[PIPE] * rows, rows)
        return [
            (source, target.at[which])
            for target, at in ((tail, pl.ds(span - width, width)), (head, pl.ds(0, width)))
            for which, source in enumerate((chars.at[mine, at], got.at[:, at]))
        ]

    out_shape = [shape_of((2, rows, width, half), bf16)] * 2
    return pack(info, plan_of, [characters, center_got], out_shape, 4)


def pair_lanes(rows):
    return lax.broadcasted_iota(jnp.int32, (rows, PAIR), 1) < HEAD


def split_pair(both, is_first):
    zero = jnp.zeros_like(both)
    return jnp.concatenate([jnp.where(is_first, both, zero), jnp.where(is_first, zero, both)], axis=0)


def join_rows(stacked):
    block = stacked.shape[1] // 2
    return jnp.concatenate([stacked[:HEAD, :block], stacked[HEAD:, block:]], axis=0)


def window_of(block):
    dims = (block + 2 * WINDOW, block)
    q_at = lax.broadcasted_iota(jnp.int32, dims, 1)
    k_at = lax.broadcasted_iota(jnp.int32, dims, 0) - WINDOW
    return jnp.abs(q_at - k_at) < WINDOW, k_at


def window_bias(in_window, position, length):
    bias = jnp.where(in_window & (position >= 0) & (position < length), 0.0, masked_score)
    return jnp.concatenate([bias, bias], axis=1)


def alive(info_ref, span, size, stride):
    per_row = span // stride
    step = pl.program_id(0)
    first = step * size
    pieces = []
    for j in range(max(1, size // per_row)):
        index = lax.broadcasted_iota(jnp.int32, (min(size, per_row), 1), 0) + lax.rem(first, per_row)
        length = info_ref[LENGTHS + first // per_row + j]
        pieces.append((info_ref[START] + index * stride < length).astype(f32))
    return pieces[0] if len(pieces) == 1 else jnp.concatenate(pieces, axis=0)


def inner_blocks(span, block):
    return [i for i in range(span // block) if i * block >= WINDOW and (i + 1) * block + WINDOW <= span]


def attend_block(index, block, info_ref, q_ref, att_ref, lse_ref, keys_of, values_of):
    width = block + 2 * WINDOW
    rows = slice(index * block, (index + 1) * block)
    is_first = pair_lanes(block)
    lanes = lax.broadcasted_iota(jnp.int32, (block, PAIR), 1)
    q_at = lax.broadcasted_iota(jnp.int32, (block, width), 0)
    k_at = lax.broadcasted_iota(jnp.int32, (block, width), 1) - WINDOW
    position = k_at + (info_ref[START] + index * block)
    length = info_ref[LENGTHS + pl.program_id(0)]
    allowed = (jnp.abs(q_at - k_at) < WINDOW) & (position >= 0) & (position < length)
    bias = jnp.where(allowed, 0.0, masked_score)
    bias = jnp.concatenate([bias, bias], axis=0)
    totals = jnp.zeros((block, PAIR), f32)
    for pair in range(q_ref.shape[2] // PAIR):
        cols = slice(pair * PAIR, (pair + 1) * PAIR)
        scores = mul_t(split_pair(q_ref[0, rows, cols], is_first), keys_of(cols)) + bias
        top = jnp.max(scores, axis=-1, keepdims=True)
        weights = jnp.exp(scores - top)
        total = jnp.sum(weights, axis=-1, keepdims=True)
        out = mul(low(weights), values_of(cols)) * (1.0 / total)
        att_ref[0, rows, cols] = low(jnp.where(is_first, out[:block], out[block:]))
        log_total = top + jnp.log(total)
        totals = jnp.where(lanes == 2 * pair, log_total[:block], totals)
        totals = jnp.where(lanes == 2 * pair + 1, log_total[block:], totals)
    lse_ref[0, index] = totals.T[:8]


def by_core(info_ref, half, work):
    lower, upper = slice(0, half), slice(half, 2 * half)
    pl.when(info_ref[PIPE] == 0)(lambda: work(lower, upper))
    pl.when(info_ref[PIPE] == 1)(lambda: work(upper, lower))


def attend_inner_kernel(span, block, other, info_ref, center, center_got, bias_ref, *refs):
    sources, refs = (refs[:4], refs[4:]) if other else (refs[:3], refs[3:])
    q_ref, k_ref, v_ref, att_ref, lse_ref, wq_ref, wk_ref, wv_ref, x_ref, sems = refs
    targets = (wq_ref, wk_ref, wv_ref)
    plan = plan_square(info_ref, sources, targets) if other else [[pair] for pair in zip(sources, targets)]

    def place(mine, got):
        x_ref[:, mine] = center[0]
        x_ref[:, got] = center_got[0]

    by_core(info_ref, center.shape[2], place)

    def work(ready):
        x = x_ref[...]
        ready(0)
        q_ref[0] = low(low(mul(x, wq_ref[...]) + bias_ref[0:1].astype(f32)).astype(f32) * HEAD ** (-0.5))
        ready(1)
        k_ref[0] = low(mul(x, wk_ref[...]))
        ready(2)
        v_ref[0] = low(mul(x, wv_ref[...]) + bias_ref[1:2].astype(f32))
        for index in inner_blocks(span, block):
            window = slice(index * block - WINDOW, (index + 1) * block + WINDOW)
            attend_block(
                index,
                block,
                info_ref,
                q_ref,
                att_ref,
                lse_ref,
                lambda cols, window=window: k_ref[0, window, cols],
                lambda cols, window=window: v_ref[0, window, cols],
            )

    Loads(sems, *plan).run(work)


def attend_inner(info, center, center_got, sources, biases, span, block):
    rows, _, half = center_got.shape
    local = biases.shape[1]
    model = 2 * half
    other = len(sources) == 4
    out_shape = [shape_of((rows, span, local), bf16)] * 4 + [shape_of((rows, span // block, 8, block), f32)]
    return call(
        functools.partial(attend_inner_kernel, span, block, other),
        (rows,),
        [core_block(center, rows), lead_block(center_got), whole_block(biases)] + [ANYWHERE] * len(sources),
        [lead_block(o) for o in out_shape],
        out_shape,
        [far(center), center_got, biases, *map(far, sources)],
        info,
        scratch=[pltpu.VMEM((model, local), bf16)] * 3
        + [pltpu.VMEM((span, model), bf16), pltpu.SemaphoreType.DMA((12,))],
        kept=dict.fromkeys(range(5), HEADS_MEMORY),
        flops=6 * rows * span * model * local,
        moved=rows * span * model * 8,
    )


def attend_outer_kernel(span, block, info_ref, center, center_got, left, right, vec_ref, *refs):
    biases, refs = refs[:2], refs[2:]
    groups, refs = (refs[:5], refs[5:10]), refs[10:]
    own_sources, pieces, refs = refs[:3], refs[3:7], refs[7:]
    outs, refs = (refs[:4], refs[4:8]), refs[8:]
    n_ref, s_ref, mid_ref, x_ref, *refs = refs
    own_w, other_w, (k_all, v_all, sems) = refs[:3], refs[3:6], refs[6:]
    loads = Loads(
        sems,
        list(zip(own_sources[:2], own_w)),
        [(own_sources[2], own_w[2])],
        sum(plan_square(info_ref, pieces, other_w[:2], 1), []),
        plan_attn_out(info_ref, pieces, other_w[2]),
    )

    def place(mine, got):
        for at, mine_part, got_part in (
            (slice(0, WINDOW), left[0, 0], left[1, 0]),
            (slice(WINDOW, WINDOW + span), center[0], center_got[0]),
            (slice(WINDOW + span, 2 * WINDOW + span), right[0, 0], right[1, 0]),
        ):
            x_ref[0, at, mine] = mine_part
            x_ref[0, at, got] = got_part

    by_core(info_ref, center.shape[2], place)
    inner = inner_blocks(span, block)
    width = block + 2 * WINDOW

    def work(ready):
        rims = jnp.concatenate([x_ref[0, :WINDOW], x_ref[0, WINDOW + span :]], axis=0)
        branch = None
        for half, (bias_ref, group, (wk_ref, wv_ref, wo_ref), out) in enumerate(
            zip(biases, groups, (own_w, other_w), outs)
        ):
            q_ref, k_ref, v_ref, att_in, lse_in = group
            krim_ref, vrim_ref, att_ref, lse_ref = out
            ready(2 * half)
            krim_ref[0] = low(mul(rims, wk_ref[...]))
            vrim_ref[0] = low(mul(rims, wv_ref[...]) + bias_ref[1:2].astype(f32))
            join_rims(k_all, k_ref, krim_ref, span)
            join_rims(v_all, v_ref, vrim_ref, span)
            for index in range(span // block):
                rows = slice(index * block, (index + 1) * block)
                if index in inner:
                    att_ref[0, rows] = att_in[0, rows]
                    lse_ref[0, index] = lse_in[0, index]
                    continue
                window = slice(index * block, index * block + width)
                attend_block(
                    index,
                    block,
                    info_ref,
                    q_ref,
                    att_ref,
                    lse_ref,
                    lambda cols, window=window: k_all[window, cols],
                    lambda cols, window=window: v_all[window, cols],
                )
            ready(2 * half + 1)
            term = mul(att_ref[0], wo_ref[...])
            branch = term if branch is None else branch + term
        before = x_ref[0, WINDOW : WINDOW + span].astype(f32) + branch + vec_ref[B_ATTN : B_ATTN + 1]
        normal, scale = norm_parts(before)
        n_ref[0] = low(normal)
        s_ref[0] = jnp.broadcast_to(scale, s_ref.shape[1:])
        mid_ref[0] = low(normal * vec_ref[GAIN_ONE : GAIN_ONE + 1] + vec_ref[SHIFT_ONE : SHIFT_ONE + 1])

    loads.run(work)


def join_rims(target, center, rims, span):
    target[:WINDOW] = rims[0, :WINDOW]
    target[WINDOW : WINDOW + span] = center[0]
    target[WINDOW + span :] = rims[0, WINDOW:]


def attend_outer(info, x_parts, vectors, biases, groups, own_sources, pieces, span, block):
    center, center_got, left, right = x_parts
    rows, _, half = center_got.shape
    local = biases[0].shape[1]
    model = 2 * half
    extent = span + 2 * WINDOW
    per_group = [
        shape_of((rows, 2 * WINDOW, local), bf16),
        shape_of((rows, 2 * WINDOW, local), bf16),
        shape_of((rows, span, local), bf16),
        shape_of((rows, span // block, 8, block), f32),
    ]
    out_shape = 2 * per_group + [
        shape_of((rows, span, model), bf16),
        shape_of((rows, span, PAIR), f32),
        shape_of((rows, span, model), bf16),
        shape_of((rows, extent, model), bf16),
    ]
    flat = [a for group in groups for a in group]
    rim = pl.BlockSpec((2, 1, WINDOW, half), lambda i, *_: (0, i, 0, 0))
    return call(
        functools.partial(attend_outer_kernel, span, block),
        (rows,),
        [core_block(center, rows), lead_block(center_got), rim, rim, whole_block(vectors)]
        + [whole_block(a) for a in biases]
        + [lead_block(a) for a in flat]
        + [ANYWHERE] * 7,
        [lead_block(o) for o in out_shape],
        out_shape,
        [far(center), center_got, left, right, vectors, *biases, *map(heads, flat), *map(far, (*own_sources, *pieces))],
        info,
        scratch=[pltpu.VMEM((model, local), bf16), pltpu.VMEM((model, local), bf16), pltpu.VMEM((local, model), bf16)] * 2
        + [pltpu.VMEM((extent, local), bf16)] * 2
        + [pltpu.SemaphoreType.DMA((19,))],
        kept=dict.fromkeys((8, 9), pltpu.HBM),
        flops=6 * rows * span * model * local,
        moved=rows * extent * model * 8,
        limit=28 << 20,
    )


def attend_back_kernel(span, block, other, info_ref, gb_ref, q_ref, kc_ref, kr_ref, vc_ref, vr_ref, lse_ref, *refs):
    first_step = pl.program_id(0) == 0
    if other:
        pieces, refs = refs[:4], refs[4:]
        dq_ref, dk_ref, dv_ref, vec_ref, ga_ref, k_ref, v_ref, kt_ref, dk_acc, dv_acc, wo_ref, sems = refs

        Loads(sems, plan_attn_out(info_ref, pieces, wo_ref)).fill()

    else:
        wo_ref, *vecs, dq_ref, dk_ref, dv_ref, all_ref, ga_ref, k_ref, v_ref, kt_ref, dk_acc, dv_acc, vec_ref = refs

    @pl.when(first_step)
    def _():
        vec_ref[...] = jnp.zeros_like(vec_ref)

    length = info_ref[LENGTHS + pl.program_id(0)]
    start = info_ref[START]
    width = block + 2 * WINDOW
    pairs = q_ref.shape[2] // PAIR
    ga_ref[...] = low(mul_t(gb_ref[0], wo_ref[...]))
    dk_acc[...] = jnp.zeros_like(dk_acc)
    dv_acc[...] = jnp.zeros_like(dv_acc)
    join_rims(k_ref, kc_ref, kr_ref, span)
    join_rims(v_ref, vc_ref, vr_ref, span)
    kt_ref[...] = k_ref[...].T
    is_first = pair_lanes(block)
    in_window, k_at = window_of(block)
    for index in range(span // block):
        at = index * block
        keep = slice(at, at + width)
        bias = window_bias(in_window, k_at + (start + at), length)
        for pair in range(pairs):
            cols = slice(pair * PAIR, (pair + 1) * PAIR)
            q2 = split_pair(q_ref[0, at : at + block, cols], is_first)
            g2 = split_pair(ga_ref[at : at + block, cols], is_first)
            log_total = jnp.concatenate(
                [lse_ref[0, index, 2 * pair : 2 * pair + 1], lse_ref[0, index, 2 * pair + 1 : 2 * pair + 2]], axis=1
            )
            probs = jnp.exp(mul_t(k_ref[keep, cols], q2) + bias - log_total)
            grad_probs = mul_t(v_ref[keep, cols], g2)
            inner = jnp.sum(probs * grad_probs, axis=0, keepdims=True)
            grad_scores = low(probs * (grad_probs - inner))
            dk_acc[keep, cols] += mul(grad_scores, q2)
            dv_acc[keep, cols] += mul(low(probs), g2)
            grad_q = join_rows(mul(kt_ref[cols, keep], grad_scores)) * HEAD ** (-0.5)
            dq_ref[0, at : at + block, cols] = low(grad_q.T)

    dk_ref[0] = low(dk_acc[...])
    grad_values = low(dv_acc[...])
    dv_ref[0] = grad_values
    vec_ref[0:1] += col_sum(dq_ref[0].astype(f32))
    vec_ref[1:2] += col_sum(grad_values.astype(f32))
    if other:
        return

    vec_conv, vec_one, inner_own, inner_other, vec_other = vecs
    local = q_ref.shape[2]
    model = vec_one.shape[1]

    def collect(first, second, inner_first, inner_second):
        all_ref[...] = jnp.zeros_like(all_ref)
        all_ref[0:6] = vec_conv[0:6]
        all_ref[6:9] = vec_one[0:3]
        per_half = inner_first.shape[1] // model
        for half, inner in enumerate((inner_first, inner_second)):
            for i in range(per_half):
                row = 9 + half * per_half + i
                all_ref[row : row + 1] = inner[0:1, i * model : (i + 1) * model]
        row = 9 + 2 * per_half
        all_ref[row : row + 2, :local] = first[0:2]
        all_ref[row : row + 2, local:] = second[0:2]

    last_step = pl.program_id(0) == pl.num_programs(0) - 1
    pl.when(last_step & (info_ref[MP] == 0))(lambda: collect(vec_ref, vec_other, inner_own, inner_other))
    pl.when(last_step & (info_ref[MP] == 1))(lambda: collect(vec_other, vec_ref, inner_other, inner_own))


def attend_back(info, grad_branch, kept, w_out, block, vecs=None):
    rows, span, local = kept[0].shape
    extent = span + 2 * WINDOW
    model = grad_branch.shape[2]
    other = isinstance(w_out, (list, tuple))
    out_shape = [
        shape_of((rows, span, local), bf16),
        shape_of((rows, extent, local), bf16),
        shape_of((rows, extent, local), bf16),
        shape_of((8, local) if other else (16, model), f32),
    ]
    args = [grad_branch, *map(heads, kept)]
    in_specs = [lead_block(a) for a in args]
    scratch = [
        pltpu.VMEM((span, local), bf16),
        pltpu.VMEM((extent, local), bf16),
        pltpu.VMEM((extent, local), bf16),
        pltpu.VMEM((local, extent), bf16),
        pltpu.VMEM((extent, local), f32),
        pltpu.VMEM((extent, local), f32),
    ]
    if other:
        args += list(map(far, w_out))
        in_specs += [ANYWHERE] * 4
        scratch += [pltpu.VMEM((local, model), bf16), pltpu.SemaphoreType.DMA((8,))]
    else:
        args += [far(w_out), *vecs]
        in_specs += [whole_block(a) for a in args[7:]]
        scratch += [pltpu.VMEM((8, local), f32)]
    return call(
        functools.partial(attend_back_kernel, span, block, other),
        (rows,),
        in_specs,
        [lead_block(o) for o in out_shape[:3]] + [fixed_block(out_shape[3])],
        out_shape,
        args,
        info,
        scratch=scratch,
        flops=6 * rows * span * local * (model + 5 * (block + 2 * WINDOW)),
        moved=rows * extent * model * 8,
    )


B_ATTN, GAIN_ONE, SHIFT_ONE, B_OUTER, GAIN_TWO, SHIFT_TWO, B_CONV, GAIN_THREE, SHIFT_THREE = range(9)


def feed_kernel(last, span, info_ref, x_ref, bi_ref, *refs):
    if last:
        part_ref, n_ref, vec_ref = refs[:3]
        inner_pieces, outer_pieces, refs = refs[3:7], refs[7:9], refs[9:]
        act_ref, slope_ref, n2_ref, scale_ref, grp_ref, wi_ref, wo_ref, sems, sent_ref = refs
    else:
        wi, wo, act_ref, slope_ref, part_ref, wi_ref, wo_ref, sems = refs
    x = x_ref[...]
    units = wi_ref.shape[1]
    step = 512
    count = units // step
    if last:
        plans = [plan_inner(info_ref, inner_pieces, wi_ref), plan_outer(info_ref, outer_pieces, wo_ref)]
        inner_at, outer_at = [[0]] + [[]] * count, [[1]] + [[]] * count
    else:
        plans = plan_columns(wi, wi_ref, step) + plan_rows(wo, wo_ref, step)
        inner_at, outer_at = [[i] for i in range(count)], [[count + i] for i in range(count)]
    def work(ready):
        bias = inner_bias(bi_ref, units)
        total = None
        for i in range(count):
            cols = slice(i * step, (i + 1) * step)
            ready(*inner_at[i])
            act, slope = gelu_parts(mul(x, wi_ref[:, cols]) + bias[:, cols])
            act = low(act)
            act_ref[:, cols] = act
            slope_ref[:, cols] = low(slope)
            ready(*outer_at[i])
            term = mul(act, wo_ref[cols, :])
            total = term if total is None else total + term
        if not last:
            part_ref[...] = low(total)
            return

        middle = n_ref[...].astype(f32) * vec_ref[GAIN_ONE : GAIN_ONE + 1] + vec_ref[SHIFT_ONE : SHIFT_ONE + 1]
        before = middle + part_ref[...].astype(f32) + total + vec_ref[B_OUTER : B_OUTER + 1]
        normal, scale = norm_parts(before)
        n2_ref[...] = low(normal)
        scale_ref[...] = jnp.broadcast_to(scale, scale_ref.shape)
        size = x.shape[0]
        sent = normal * vec_ref[GAIN_TWO : GAIN_TWO + 1] + vec_ref[SHIFT_TWO : SHIFT_TWO + 1]
        sent = sent * alive(info_ref, span, size, 1)
        chunks = range(sent_ref.shape[0])
        for c in chunks:
            sent_ref[c] = sent[:, c * PAIR : (c + 1) * PAIR]
        for k in range(KERNEL):
            rows = pl.ds(k, size // KERNEL, stride=KERNEL)
            grp_ref[k] = low(jnp.concatenate([sent_ref[c, rows, :] for c in chunks], axis=1))

    Loads(sems, *plans).run(work)


def feed(info, middle, biases, units, span, tile, w_inner=None, w_outer=None, tail=None, pieces=None):
    tokens, model = middle.shape
    args = [middle, biases]
    in_specs = [lead_block(middle, tile), whole_block(biases)]
    out_shape = [shape_of((tokens, units), bf16), shape_of((tokens, units), bf16), shape_of((tokens, model), bf16)]
    scratch = [
        pltpu.VMEM((model, units), bf16),
        pltpu.VMEM((units, model), bf16),
        pltpu.SemaphoreType.DMA((8,)),
    ]
    if tail is None:
        args += [far(w_inner), far(w_outer)]
        in_specs += [ANYWHERE] * 2
        out_specs = [lead_block(o, tile) for o in out_shape]
    else:
        out_shape += [shape_of((tokens, PAIR), f32), shape_of((KERNEL, tokens // KERNEL, model), bf16)]
        args += [tail[0], far(tail[1]), tail[2], *map(far, pieces)]
        in_specs += [lead_block(a, tile) for a in tail[:2]] + [whole_block(tail[2])] + [ANYWHERE] * 6
        out_specs = [lead_block(o, tile) for o in out_shape[:4]] + [chunk_block(out_shape[4], tile // KERNEL)]
        scratch.append(pltpu.VMEM((model // PAIR, tile, PAIR), f32))
    return call(
        functools.partial(feed_kernel, tail is not None, span),
        (tokens // tile,),
        in_specs,
        out_specs,
        out_shape,
        args,
        info,
        scratch=scratch,
        kept={0: pltpu.VMEM, 1: pltpu.HBM},
        flops=4 * tokens * model * units * 1.5,
        moved=tokens * units * 8,
    )


def conv_kernel(mols, span, info_ref, grp_ref, wc_ref, vecs_ref, mg_ref, mg_got_ref, n2_ref, sc_ref,
                mol_ref, mol_out_ref, gc_ref, feed_ref, vec_ref, back_ref, mg_all):

    @pl.when(pl.program_id(0) == 0)
    def _():
        vec_ref[...] = jnp.zeros_like(vec_ref)

    half = mg_ref.shape[1]
    lower, upper = slice(0, half), slice(half, 2 * half)

    def place(mine, got):
        mg_all[:, mine] = mg_ref[...]
        mg_all[:, got] = mg_got_ref[...]

    pl.when(info_ref[PIPE] == 0)(lambda: place(lower, upper))
    pl.when(info_ref[PIPE] == 1)(lambda: place(upper, lower))

    def vector(index):
        return vecs_ref[index : index + 1]

    total = None
    for k in range(KERNEL):
        term = mul(grp_ref[k], wc_ref[k])
        total = term if total is None else total + term
    value, slope = gelu_parts(total + vector(B_CONV))
    normal, scale = norm_parts(value)
    live = alive(info_ref, span, mols, KERNEL)
    cotangent = mg_all[...].astype(f32) * live
    molecules = low((normal * vector(GAIN_THREE) + vector(SHIFT_THREE)) * live)

    def split(mine, got):
        mol_ref[...] = molecules[:, mine]
        mol_out_ref[...] = molecules[:, got]

    pl.when(info_ref[PIPE] == 0)(lambda: split(lower, upper))
    pl.when(info_ref[PIPE] == 1)(lambda: split(upper, lower))
    grad = low(norm_back(cotangent * vector(GAIN_THREE), normal, scale) * slope)
    gc_ref[...] = grad
    chunks = range(back_ref.shape[0])
    for k in range(KERNEL):
        back = low(mul_t(grad, wc_ref[k])).astype(f32)
        for c in chunks:
            back_ref[c, pl.ds(k, mols, stride=KERNEL), :] = back[:, c * PAIR : (c + 1) * PAIR]
    masked = jnp.concatenate([back_ref[c] for c in chunks], axis=1) * alive(info_ref, span, KERNEL * mols, 1)
    n2 = n2_ref[...].astype(f32)
    grad_two = norm_back(masked * vector(GAIN_TWO), n2, sc_ref[:, :1])
    feed_ref[...] = low(grad_two)
    vec_ref[...] += jnp.concatenate(
        [
            col_sum(grad.astype(f32)),
            col_sum(cotangent * normal),
            col_sum(cotangent),
            col_sum(masked * n2),
            col_sum(masked),
            col_sum(grad_two),
            jnp.zeros((2, grad_two.shape[1]), f32),
        ],
        axis=0,
    )


def conv(info, grouped, w_conv, vectors, mol_grad, mol_got, n2, scale2, span, steps):
    _, all_mols, model = grouped.shape
    tokens = KERNEL * all_mols
    tile = tokens // steps
    mols = tile // KERNEL
    args = [grouped, w_conv, vectors, far(mol_grad), far(mol_got), n2, scale2]
    in_specs = [
        chunk_block(grouped, mols),
        whole_block(w_conv),
        whole_block(vectors),
        core_block(mol_grad, steps, mols),
        lead_block(mol_got, mols),
        lead_block(n2, tile),
        lead_block(scale2, tile),
    ]
    out_shape = [
        shape_of((all_mols, model // 2), bf16),
        shape_of((all_mols, model // 2), bf16),
        shape_of((all_mols, model), bf16),
        shape_of((tokens, model), bf16),
        shape_of((8, model), f32),
    ]
    out_specs = [lead_block(o, mols) for o in out_shape[:3]] + [lead_block(out_shape[3], tile), fixed_block(out_shape[4])]
    return call(
        functools.partial(conv_kernel, mols, span),
        (steps,),
        in_specs,
        out_specs,
        out_shape,
        args,
        info,
        scratch=[
            pltpu.VMEM((model // PAIR, tile, PAIR), f32),
            pltpu.VMEM((mols, model), bf16),
        ],
        flops=4 * tokens * model * model * 1.5,
        moved=tokens * model * 30,
    )


def dp_place(info_ref, index, count):
    away = info_ref[DP] ^ index
    place, bits = 0, count.bit_length() - 1
    for bit in range(bits):
        place = place + (((away >> bit) & 1) << (bits - 1 - bit))
    return place


def cut(width):
    size = width // PARTS
    return [slice(i * size, (i + 1) * size) for i in range(PARTS)]


def conv_weight_kernel(mine, per_step, info_ref, grp_ref, grad_ref, *refs):
    value = t_mul(grp_ref[0], grad_ref[...])
    gots, outs = (refs[:PARTS], refs[PARTS:]) if mine else ((), refs)
    count, size = outs[0].shape[:2]
    for j in range(per_step):
        place = dp_place(info_ref, pl.program_id(0) * per_step + j, count)
        part = value[j * size : (j + 1) * size]
        for i, cols in enumerate(cut(value.shape[1])):
            if mine:
                outs[0][place, :, cols] = low(part[:, cols] + gots[i][place].astype(f32))
            else:
                outs[i][place] = low(part[:, cols])


def conv_weight(info, other_side, grouped, grad, dp_size, got=()):
    kernel, mols, model = grouped.shape
    half = kernel // 2
    args = [grouped, grad, *got]
    in_specs = [
        pl.BlockSpec((1, mols, model), lambda i, info_ref: ((info_ref[PIPE] ^ other_side) * half + i, 0, 0)),
    ] + [whole_block(a) for a in args[1:]]
    dims = (dp_size, half * model // dp_size)
    out_shape = [shape_of(dims + (model,), bf16)] if got else [shape_of(dims + (model // PARTS,), bf16)] * PARTS
    return call(
        functools.partial(conv_weight_kernel, bool(got), dp_size // half),
        (half,),
        in_specs,
        [fixed_block(o) for o in out_shape],
        out_shape,
        args,
        info,
        flops=2 * half * mols * model * model,
        moved=half * model * model * 8,
    )


def weight_kernel(mine, info_ref, left_ref, *refs):
    rights, refs = refs[:2], refs[2:]
    gots, outs = (refs[:PARTS], refs[PARTS:]) if mine else ((), refs)
    count, size = outs[0].shape[1:3]
    for index in range(2):
        value = t_mul(left_ref[...], rights[index][...])
        for d in range(count):
            place = dp_place(info_ref, d, count)
            part = value[d * size : (d + 1) * size]
            if mine:
                for i, got in enumerate(gots):

                    @pl.when(pl.program_id(0) == i)
                    def _(got=got, part=part, place=place):
                        outs[0][index, place] = low(part + got[index, place].astype(f32))

            else:
                for i, out in enumerate(outs):

                    @pl.when(pl.program_id(0) == i)
                    def _(out=out, part=part, place=place):
                        out[index, place] = low(part)


def weight(info, other_side, left, right_own, right_other, dp_size, got=()):
    tokens, model = left.shape
    columns = right_own.shape[1]
    half = model // 2
    tile = columns // PARTS
    args = [left, hidden(right_own), hidden(right_other), *got]
    in_specs = [
        pl.BlockSpec((tokens, half), lambda i, info_ref: (0, info_ref[PIPE] ^ other_side)),
        pl.BlockSpec((tokens, tile), lambda i, *_: (0, i)),
        pl.BlockSpec((tokens, tile), lambda i, *_: (0, i)),
    ] + [whole_block(a) for a in got]
    dims = (2, dp_size, half // dp_size)
    if got:
        out_shape = [shape_of(dims + (columns,), bf16)]
        out_specs = [pl.BlockSpec(dims + (tile,), lambda i, *_: (0, 0, 0, i))]
    else:
        out_shape = [shape_of(dims + (tile,), bf16)] * PARTS
        out_specs = [fixed_block(o) for o in out_shape]
    return call(
        functools.partial(weight_kernel, bool(got)),
        (PARTS,),
        in_specs,
        out_specs,
        out_shape,
        args,
        info,
        flops=4 * tokens * half * columns,
        moved=tokens * columns * 4 + half * columns * 8,
    )


def project_weight_kernel(span, dp_size, mine, extra, info_ref, x_ref, gb_ref, dq, dk, dv, att, *refs):
    got_ref, refs = (refs[0], refs[1:]) if mine else (None, refs)
    extra_ref, outs = (refs[0], refs[1:]) if extra else (None, refs)
    rows = x_ref.shape[0]
    local = dq.shape[2]
    size = x_ref.shape[2] // dp_size
    for index, right in enumerate((dq, dk, dv, att)):
        value = None
        for row in range(rows):
            if index == 0:
                left = x_ref[row, WINDOW : WINDOW + span]
            elif index == 3:
                left = gb_ref[row]
            else:
                left = x_ref[row]
            term = t_mul(left, right[row])
            value = term if value is None else value + term
        cols = slice(index * local, (index + 1) * local)
        inside = slice(index % 2 * local, (index % 2 + 1) * local)
        for d in range(dp_size):
            at = pl.ds(pl.multiple_of(dp_place(info_ref, d, dp_size) * size, size), size)
            part = value[d * size : (d + 1) * size]
            if mine:
                outs[index // 2][at, inside] = low(part + got_ref[at, cols].astype(f32))
            else:
                outs[0][at, cols] = low(part)
    if extra:
        outs[0][dp_size * size :] = extra_ref[...]


def project_weight(info, other_side, x_ext, grad_branch, grads, span, dp_size, got=None, extra=None):
    rows, extent, model = x_ext.shape
    half = model // 2
    local = grads[0].shape[2]
    mine = got is not None
    more = ([got] if mine else []) + ([] if extra is None else [extra])
    args = [heads(x_ext), grad_branch, *grads[:3], heads(grads[3]), *more]
    in_specs = [
        pl.BlockSpec((rows, extent, half), lambda i, info_ref: (0, 0, info_ref[PIPE] ^ other_side)),
        pl.BlockSpec((rows, span, half), lambda i, info_ref: (0, 0, info_ref[PIPE] ^ other_side)),
    ] + [whole_block(a) for a in args[2:]]
    if mine:
        extra_rows = 0 if extra is None else extra.shape[0]
        out_shape = [shape_of((half + extra_rows, 2 * local), bf16), shape_of((half, 2 * local), bf16)]
    else:
        out_shape = [shape_of((half, 4 * local), bf16)]
    return call(
        functools.partial(project_weight_kernel, span, dp_size, mine, extra is not None),
        (1,),
        in_specs,
        [fixed_block(o) for o in out_shape],
        out_shape,
        args,
        info,
        flops=8 * rows * extent * half * local,
        moved=rows * extent * model * 6,
    )


def feed_back_kernel(info_ref, gf_ref, sl_own, sl_other, n_ref, sc_ref, wo, wi, vecs_ref, *refs):
    inner_pieces, outer_pieces, refs = refs[:4], refs[4:6], refs[6:]
    gh_own, gh_other, gb_ref, vec_ref, bi_own, bi_other, wi_own, wo_own, wi_other, wo_other, sems = refs
    units = wo_own.shape[0]
    step = 512
    count = units // step
    loads = Loads(
        sems,
        *plan_rows(wo, wo_own, step),
        *plan_columns(wi, wi_own, step),
        plan_outer(info_ref, outer_pieces, wo_other),
        plan_inner(info_ref, inner_pieces, wi_other),
    )

    @pl.when(pl.program_id(0) == 0)
    def _():
        vec_ref[...] = jnp.zeros_like(vec_ref)
        bi_own[...] = jnp.zeros_like(bi_own)
        bi_other[...] = jnp.zeros_like(bi_other)

    def half(ready, total, slope_ref, wo_ref, wi_ref, gh_ref, bi_ref, outer_at, inner_at):
        for i in range(count):
            cols = slice(i * step, (i + 1) * step)
            ready(*outer_at[i])
            grad = low(mul_t(gf_ref[...], wo_ref[cols, :]) * slope_ref[:, cols].astype(f32))
            gh_ref[:, cols] = grad
            bi_ref[:1, cols] += col_sum(grad.astype(f32))
            ready(*inner_at[i])
            total = total + mul_t(grad, wi_ref[:, cols])
        return total

    def work(ready):
        chunks = [[i] for i in range(count)], [[count + i] for i in range(count)]
        total = half(ready, gf_ref[...].astype(f32), sl_own, wo_own, wi_own, gh_own, bi_own, *chunks)
        chunks = [[2 * count]] + [[]] * count, [[2 * count + 1]] + [[]] * count
        total = half(ready, total, sl_other, wo_other, wi_other, gh_other, bi_other, *chunks)
        normal = n_ref[...].astype(f32)
        grad_one = norm_back(total * vecs_ref[GAIN_ONE : GAIN_ONE + 1], normal, sc_ref[:, :1])
        gb_ref[...] = low(grad_one)
        vec_ref[...] += jnp.concatenate(
            [col_sum(grad_one), col_sum(total * normal), col_sum(total), jnp.zeros((5, total.shape[1]), f32)], axis=0
        )

    loads.run(work)


def feed_back(info, grad_feed, slopes, n1, scale1, w_outer, w_inner, vectors, pieces, tile):
    tokens, model = grad_feed.shape
    units = w_outer.shape[0]
    args = [grad_feed, *map(far, slopes), far(n1), far(scale1), far(w_outer), far(w_inner), vectors, *map(far, pieces)]
    in_specs = [lead_block(a, tile) for a in args[:5]] + [ANYWHERE] * 2 + [whole_block(vectors)] + [ANYWHERE] * 6
    out_shape = [
        shape_of((tokens, units), bf16),
        shape_of((tokens, units), bf16),
        shape_of((tokens, model), bf16),
        shape_of((8, model), f32),
        shape_of((8, units), f32),
        shape_of((8, units), f32),
    ]
    return call(
        feed_back_kernel,
        (tokens // tile,),
        in_specs,
        [lead_block(o, tile) for o in out_shape[:3]] + [fixed_block(o) for o in out_shape[3:]],
        out_shape,
        args,
        info,
        scratch=[pltpu.VMEM((model, units), bf16), pltpu.VMEM((units, model), bf16)] * 2
        + [pltpu.SemaphoreType.DMA((8 + 2 * (units // 512),))],
        flops=8 * tokens * model * units * 1.2,
        moved=tokens * units * 8,
        limit=26 << 20,
        kept=dict.fromkeys((0, 1), UNITS_MEMORY),
    )


def input_rims_kernel(span, info_ref, *refs):
    groups, weights, pieces, refs = (refs[:2], refs[2:4]), refs[4:6], refs[6:10], refs[10:]
    left_ref, right_ref, wk_ref, wv_ref, sems = refs
    loads = Loads(sems, *plan_square(info_ref, pieces, (wk_ref, wv_ref), 1))
    loads.start()
    ranges = (pl.ds(0, WINDOW), pl.ds(WINDOW + span, WINDOW))
    rows = left_ref.shape[0]

    def rims(grads, *weights):
        total = None
        for grad, weight in zip(grads, weights):
            cells = jnp.concatenate([grad[row, at] for at in ranges for row in range(rows)], axis=0)
            term = mul_t(cells, weight[...])
            total = term if total is None else total + term
        return total

    total = rims(groups[0], *weights)
    loads.ready(0, 1)
    total = low(total + rims(groups[1], wk_ref, wv_ref))
    for row in range(rows):
        left_ref[row] = total[row * WINDOW : (row + 1) * WINDOW]
        right_ref[row] = total[(rows + row) * WINDOW : (rows + row + 1) * WINDOW]


def input_rims(info, own, other, weights, pieces, span):
    rows, _, local = own[1].shape
    model = weights[0].shape[0]
    args = [own[1], own[2], other[1], other[2], *map(far, (*weights[1:], *pieces))]
    in_specs = [whole_block(a) for a in args[:6]] + [ANYWHERE] * 4
    out_shape = [shape_of((rows, WINDOW, model), bf16)] * 2
    return call(
        functools.partial(input_rims_kernel, span),
        (1,),
        in_specs,
        [fixed_block(o) for o in out_shape],
        out_shape,
        args,
        info,
        scratch=[pltpu.VMEM((model, local), bf16)] * 2 + [pltpu.SemaphoreType.DMA((8,))],
        flops=16 * rows * WINDOW * model * local,
        moved=rows * WINDOW * model * 12,
    )


def input_center_kernel(span, info_ref, one_ref, *refs):
    groups, weights, pieces, refs = (refs[:3], refs[3:6]), refs[6:9], refs[9:13], refs[13:]
    mine_ref, theirs_ref, *scratch, sems = refs
    plan = [[pair] for pair in zip(weights, scratch[:3])]
    loads = Loads(sems, *plan, *plan_square(info_ref, pieces, scratch[3:]))
    own_rows = pl.ds(WINDOW, span)
    half = mine_ref.shape[2]
    lower, upper = slice(0, half), slice(half, 2 * half)

    def work(ready):
        center = one_ref[0].astype(f32)
        for which, (dq, dk, dv) in enumerate(groups):
            for i, cells in enumerate((dq[0], dk[0, own_rows], dv[0, own_rows])):
                ready(3 * which + i)
                center = center + mul_t(cells, scratch[3 * which + i][...])

        def split(mine, theirs):
            mine_ref[0] = center[:, mine]
            theirs_ref[0] = low(center[:, theirs])

        pl.when(info_ref[PIPE] == 0)(lambda: split(lower, upper))
        pl.when(info_ref[PIPE] == 1)(lambda: split(upper, lower))

    loads.run(work)


def input_center(info, grad_one, own, other, weights, pieces, span):
    rows, extent, local = own[1].shape
    model = grad_one.shape[2]
    args = [grad_one, *own, *other, *map(far, (*weights, *pieces))]
    in_specs = [lead_block(a) for a in args[:7]] + [ANYWHERE] * 7
    out_shape = [shape_of((rows, span, model // 2), f32), shape_of((rows, span, model // 2), bf16)]
    return call(
        functools.partial(input_center_kernel, span),
        (rows,),
        in_specs,
        [lead_block(o) for o in out_shape],
        out_shape,
        args,
        info,
        scratch=[pltpu.VMEM((model, local), bf16)] * 6 + [pltpu.SemaphoreType.DMA((15,))],
        flops=12 * rows * span * model * local,
        moved=rows * extent * model * 12,
    )


def finish_kernel(rows, info_ref, mine, got, head, tail, head_got, tail_got, mol, mol_got, out_ref, mol_ref):
    row = pl.program_id(0)
    width = head.shape[1]
    own = (row >= rows) == (info_ref[PIPE] == 1)

    def write(center, first, last, molecules):
        out_ref[0] = center[0].astype(f32)
        out_ref[0, :width] += first[0].astype(f32)
        out_ref[0, out_ref.shape[1] - width :] += last[0].astype(f32)
        mol_ref[0] = molecules[0]

    pl.when(own)(lambda: write(mine, head, tail, mol))
    pl.when(jnp.logical_not(own))(lambda: write(got, head_got, tail_got, mol_got))


def finish(info, mine, got, head, tail, head_got, tail_got, mol, mol_got):
    rows, span, half = mine.shape
    width = head.shape[1]

    def core_rows(array):
        return pl.BlockSpec((1,) + tuple(array.shape[1:]), lambda i, info_ref: (i % rows, 0, 0))

    rims = pl.BlockSpec((1, width, half), lambda i, info_ref: (i % rows, 0, info_ref[PIPE]))
    out_shape = [shape_of((2 * rows, span, half), f32), shape_of((2 * rows,) + tuple(mol.shape[1:]), bf16)]
    return call(
        functools.partial(finish_kernel, rows),
        (2 * rows,),
        [core_rows(mine), core_rows(got), rims, rims] + [core_rows(a) for a in (head_got, tail_got, mol, mol_got)],
        [lead_block(o) for o in out_shape],
        out_shape,
        [mine, got, head, tail, head_got, tail_got, mol, mol_got],
        info,
        moved=rows * span * half * 20,
    )


def swapped(block, axis, bit=0):
    count = lax.axis_size(axis)
    return lax.ppermute(block, axis, [(i, i ^ (1 << bit)) for i in range(count)])


def to_core(blocks):
    return [swapped(block, "pipe") for block in blocks]


def from_chunk(block, distance):
    axes = ("seq", "mp")
    count = lax.axis_size("seq") * lax.axis_size("mp")
    return lax.ppermute(block, axes, [(i + distance, i) for i in range(count) if 0 <= i + distance < count])


def pick(array, index, dim):
    return lax.dynamic_index_in_dim(array, index, dim, keepdims=False)


def add(left, right):
    return low(left.astype(f32) + right.astype(f32))


def bits_of(axis):
    return lax.axis_size(axis).bit_length() - 1


class Halving:
    def __init__(self, parts, dim, axis):
        self.dim, self.axis = dim, axis
        self.keep, self.sent = self.split(parts, 0)

    def go(self):
        self.got = swapped(self.sent, self.axis)

    def split(self, parts, bit):
        dim = self.dim
        shaped = parts.reshape(parts.shape[:dim] + (parts.shape[dim] // 2, 2) + parts.shape[dim + 1 :])
        mine = (lax.axis_index(self.axis) >> bit) & 1
        return pick(shaped, mine, dim + 1), pick(shaped, 1 - mine, dim + 1)

    def finish(self, *gates):
        parts = add(self.keep, after(self.got, *gates))
        for bit in range(1, bits_of(self.axis)):
            keep, sent = self.split(parts, bit)
            parts = add(keep, swapped(sent, self.axis, bit))
        return parts.reshape(parts.shape[: self.dim] + parts.shape[self.dim + 1 :])


class HalvingDp:
    def __init__(self, parts):
        self.bit = 0
        self.split(parts)

    def split(self, parts):
        half = parts.shape[0] // 2
        self.keep, self.sent = parts[:half], parts[half:]

    def go(self):
        self.got = swapped(self.sent, "dp", self.bit)
        self.bit += 1

    def landed(self, *gates):
        return add(self.keep, after(self.got, *gates))

    def step(self, *gates):
        self.split(self.landed(*gates))

    def finish(self, *gates):
        while self.keep.shape[0] > 1:
            self.step()
            self.go()
        return self.landed(*gates)[0]


def sending(value, *halvings):
    value, *sent = tie(value, *(h.sent for h in halvings))
    for halving, block in zip(halvings, sent):
        halving.sent = block
        halving.go()
    return value


def relay(quarter):
    first = swapped(quarter, "mp")
    return first, swapped(first, "seq")


def all_pieces(first, second):
    return [first, second, swapped(first, "pipe"), swapped(second, "pipe")]


def in_order(first, mine, recv, axis):
    return jnp.where(
        first == 0, jnp.concatenate([mine, recv], axis=axis), jnp.concatenate([recv, mine], axis=axis)
    )


def after(value, *others):
    return lax.optimization_barrier((value, *others))[0] if others else value


def tie(*values):
    return lax.optimization_barrier(values)


def on_device(
    characters,
    row_lengths,
    w_query,
    b_query,
    w_key,
    w_value,
    b_value,
    w_attn_out,
    b_attn_out,
    gain_one,
    shift_one,
    w_inner,
    b_inner,
    w_outer,
    b_outer,
    gain_two,
    shift_two,
    w_conv,
    b_conv,
    gain_three,
    shift_three,
    molecule_grad,
):
    pipe = lax.axis_index("pipe")
    seq = lax.axis_index("seq")
    mp = lax.axis_index("mp")
    dp_size, seq_size, mp_size = (lax.axis_size(a) for a in ("dp", "seq", "mp"))
    all_rows, span, half_model = characters.shape
    rows = all_rows // 2
    model = 2 * half_model
    local = w_query.shape[1]
    units = w_inner.shape[1]
    tokens = rows * span
    mols = tokens // KERNEL
    block = min(WINDOW, span)
    tile = min(256, tokens)
    own_start = (seq * lax.axis_size("mp") + mp) * span

    def rows_of(array, index):
        return lax.dynamic_slice_in_dim(array, index * rows, rows, 0)

    me = 2 * (seq & 1) + pipe
    lengths = rows_of(row_lengths, pipe)
    scalars = jnp.stack([own_start, pipe, me, lax.axis_index("dp"), mp]).astype(jnp.int32)
    info = jnp.concatenate([scalars, lengths])
    squares = (w_query, w_key, w_value)
    biases, vectors = gather_small(
        b_query,
        b_value,
        b_inner,
        (b_attn_out, gain_one, shift_one, b_outer, gain_two, shift_two, b_conv, gain_three, shift_three),
    )
    hops = -(-WINDOW // span)
    width = min(span, WINDOW)

    center_send, mol_send = pack_rows(info, [characters, molecule_grad])
    center_got = swapped(center_send, "pipe")
    packet = pack_first(after(info, center_send), squares, w_attn_out, biases)
    tail, head = pack_rims(after(info, packet), characters, center_got, width)
    square_first = swapped(packet, "mp")
    inner_packet, outer_packet = pack_second(after(info, tail), w_inner, w_outer)
    center_got, tail, head, inner_packet, outer_packet = tie(center_got, tail, head, inner_packet, outer_packet)
    inner_own = attend_inner(info, characters, center_got, squares, biases, span, block)
    *inner_own, square_first = tie(*inner_own, square_first)
    square_second = swapped(square_first, "seq")
    square_first, tail, head = tie(square_first, tail, head)
    left, right = [], []
    for hop in range(1, hops + 1):
        left.insert(0, from_chunk(tail, -hop))
        right.append(from_chunk(head, hop))
    left, right = (a[0] if hops == 1 else jnp.concatenate(a, axis=2) for a in (left, right))
    square_second, left, right, inner_packet, outer_packet = tie(square_second, left, right, inner_packet, outer_packet)
    inner_first = swapped(inner_packet, "mp")
    outer_first = swapped(outer_packet, "mp")
    mol_grad = molecule_grad.reshape(2 * mols, half_model)

    square_pieces = all_pieces(square_first, square_second)
    biases_other = square_first[square_first.shape[0] - 16 :]
    inner_other = attend_inner(info, characters, center_got, square_pieces, biases_other, span, block)
    (kr_own, vr_own, att_own, lse_own, kr_other, vr_other, att_other, lse_other, n1, scale1, middle, x_ext) = attend_outer(
        info,
        (characters, center_got, left, right),
        vectors,
        (biases, biases_other),
        (inner_own, inner_other),
        (w_key, w_value, w_attn_out),
        square_pieces,
        span,
        block,
    )
    kept_own = (inner_own[0], inner_own[1], kr_own, inner_own[2], vr_own, lse_own)
    kept_other = (inner_other[0], inner_other[1], kr_other, inner_other[2], vr_other, lse_other)
    middle, inner_first = tie(middle, inner_first)
    inner_second = swapped(inner_first, "seq")
    n1, scale1, middle = (a.reshape(tokens, -1) for a in (n1, scale1, middle))
    act_own, slope_own, part = feed(
        info, middle, biases, units, span, tile, w_inner, w_outer
    )
    part, inner_second, outer_first = tie(part, inner_second, outer_first)
    pieces = (*all_pieces(inner_first, inner_second), outer_first, swapped(outer_first, "pipe"))
    mol_got = swapped(after(mol_send, part), "pipe").reshape(mols, half_model)
    act_other, slope_other, n2, scale2, grouped = feed(
        info, middle, biases_other, units, span, tile, tail=(part, n1, vectors), pieces=pieces
    )
    mol_mine, mol_theirs, grad_conv, grad_feed, vec_conv = conv(
        info, grouped, w_conv.reshape(KERNEL, model, model), vectors, mol_grad, mol_got, n2, scale2, span, 2
    )
    mol_shape = (rows, span // KERNEL, half_model)
    mol_mine = mol_mine.reshape(mol_shape)
    mol_theirs = mol_theirs.reshape(mol_shape)

    conv_theirs = conv_weight(info, 1, grouped, grad_conv, dp_size)
    conv_got = to_core(conv_theirs)
    outer_theirs = weight(info, 1, after(grad_feed, *conv_theirs), act_own, act_other, dp_size)
    outer_got = to_core(outer_theirs)
    (conv_part,) = conv_weight(info, 0, grouped, after(grad_conv, *outer_theirs), dp_size, conv_got)
    conv_halving = Halving(conv_part.reshape(dp_size, seq_size, mp_size, -1, model), 2, "mp")
    grad_feed = sending(grad_feed, conv_halving)
    (outer_part,) = weight(info, 0, grad_feed, act_own, act_other, dp_size, outer_got)
    outer_halving = Halving(outer_part.reshape(2, dp_size, seq_size, -1, units), 2, "seq")
    grad_feed = sending(grad_feed, outer_halving)
    gh_own, gh_other, grad_branch, vec_one, bi_own, bi_other = feed_back(
        info,
        grad_feed,
        (slope_own, slope_other),
        n1,
        scale1,
        w_outer,
        w_inner,
        vectors,
        pieces,
        tile,
    )
    inner_theirs = weight(info, 1, middle, gh_own, gh_other, dp_size)
    conv_part = conv_halving.finish(*inner_theirs)
    conv_halving = Halving(conv_part, 1, "seq")
    outer_part = outer_halving.finish(*inner_theirs)
    *inner_theirs, conv_halving.sent, outer_sent = tie(*inner_theirs, conv_halving.sent, outer_part[1])
    conv_halving.go()
    outer_got = swapped(outer_sent, "mp")
    inner_got = to_core(inner_theirs)

    grad_branch = grad_branch.reshape(rows, span, model)
    *back_other, vec_other = attend_back(
        info, after(grad_branch, *inner_theirs), kept_other, square_pieces, block
    )

    def narrow(part):
        return jnp.concatenate([part[:, :, :model], part[:, :, model:]], axis=1)

    conv_part = conv_halving.finish(vec_other)
    outer_part = add(outer_part[0], after(outer_got, vec_other)).reshape(dp_size, -1, units)
    merged_halving = HalvingDp(jnp.concatenate([conv_part, narrow(outer_part)], axis=1))
    middle = sending(middle, merged_halving)
    (inner_part,) = weight(info, 0, middle, gh_own, gh_other, dp_size, inner_got)
    x_late, inner_sent = tie(x_ext, inner_part[1])
    inner_got = swapped(inner_sent, "mp")
    (other_theirs,) = project_weight(info, 1, x_late, grad_branch, (*back_other, att_other), span, dp_size)
    other_got = swapped(other_theirs, "pipe")
    *back_own, vec = attend_back(
        info,
        after(grad_branch, other_theirs),
        kept_own,
        w_attn_out,
        block,
        (vec_conv, vec_one, bi_own, bi_other, vec_other),
    )
    merged_halving.step(vec)
    x_late, merged_halving.sent = tie(x_late, merged_halving.sent)
    (own_theirs,) = project_weight(info, 1, x_late, grad_branch, (*back_own, att_own), span, dp_size)
    late_info, own_theirs, vec, merged_halving.sent = tie(info, own_theirs, vec, merged_halving.sent)
    merged_halving.go()
    own_got = swapped(own_theirs, "pipe")
    vec = low(vec + swapped(vec, "pipe"))
    left, right = input_rims(late_info, back_own, back_other, squares, square_pieces, span)
    inner_part = add(inner_part[0], after(inner_got, left))
    inner_halving = Halving(inner_part.reshape(dp_size, seq_size, -1, units), 1, "seq")
    x_late, left, right = tie(x_late, left, right)
    x_late = sending(x_late, inner_halving)
    rims = []
    for hop in range(1, hops + 1):
        top = WINDOW - (hop - 1) * span
        rims.append(from_chunk(right[:, WINDOW - top : WINDOW - top + width], -hop))
        rims.append(from_chunk(left[:, top - width : top], hop))
    other_first, other_last = project_weight(
        info, 0, x_late, grad_branch, (*back_other, att_other), span, dp_size, other_got, vec
    )
    own_got, x_late, other_first = tie(own_got, x_late, other_first)
    first_got = swapped(other_first, "mp")
    own_first, own_last = project_weight(
        info, 0, x_late, grad_branch, (*back_own, att_own), span, dp_size, own_got
    )
    last_halving = Halving(jnp.stack([own_last, other_last]).reshape(2, dp_size, seq_size, -1, model), 2, "seq")
    inner_part = inner_halving.finish(own_first)
    grad_branch, inner_part = tie(grad_branch, inner_part)
    grad_branch = sending(grad_branch, last_halving)
    mine, theirs = input_center(info, grad_branch, back_own, back_other, squares, square_pieces, span)
    first_got, mine, *rims = tie(first_got, mine, *rims)
    head, tail = rims[:2]
    for hop in range(1, hops):
        head, tail = add(head, rims[2 * hop]), add(tail, rims[2 * hop + 1])
    rims = jnp.stack([head, tail])
    merged = merged_halving.finish(mine)
    own_rows = first_got.shape[0] - 16
    first_part = add(own_first, first_got[:own_rows]).reshape(dp_size, seq_size, -1, model)
    vec = add(vec, first_got[own_rows:])

    def with_vec(part):
        return jnp.concatenate([part.reshape(-1, model), vec], axis=0)

    chars_grad = None
    for bit in range(bits_of("seq")):
        shaped = first_part.reshape(dp_size, first_part.shape[1] // 2, 2, -1, model)
        bit_mine = (seq >> bit) & 1
        got = swapped(with_vec(pick(shaped, 1 - bit_mine, 2)), "seq", bit)
        if chars_grad is None:
            last_part = last_halving.finish(mine)
            inner_halving = HalvingDp(inner_part)
            last_sent, inner_halving.sent, mine, rims, mol_theirs, theirs = tie(
                last_part[1], inner_halving.sent, mine, rims, mol_theirs, theirs
            )
            last_got = swapped(last_sent, "mp")
            inner_halving.go()
            rims_got = swapped(lax.dynamic_slice_in_dim(rims, (1 - pipe) * half_model, half_model, 3), "pipe")
            chars_grad, molecules = finish(
                info,
                mine,
                swapped(theirs, "pipe"),
                head,
                tail,
                rims_got[0],
                rims_got[1],
                mol_mine,
                swapped(mol_theirs, "pipe"),
            )
            got, chars_grad, molecules = tie(got, chars_grad, molecules)
        count = got.shape[0] - 16
        first_part = add(pick(shaped, bit_mine, 2), got[:count].reshape(dp_size, shaped.shape[1], -1, model))
        vec = add(vec, got[count:])
    last_part = add(last_part[0], after(last_got, chars_grad))
    head_part = jnp.concatenate([first_part.reshape(dp_size, -1, model), last_part], axis=1)
    for bit in range(bits_of("dp")):
        half = head_part.shape[0] // 2
        got = swapped(with_vec(head_part[half:]), "dp", bit)
        count = got.shape[0] - 16
        head_part = add(head_part[:half], got[:count].reshape(head_part[:half].shape))
        vec = add(vec, got[count:])
    inner_sum = inner_halving.finish()
    head_sum = head_part[0].astype(f32)
    vec = vec.astype(f32)
    grad_b_conv, grad_gain_three, grad_shift_three, grad_gain_two, grad_shift_two, grad_b_outer = (
        vec[i] for i in range(6)
    )
    grad_b_attn_out, grad_gain_one, grad_shift_one = (vec[i] for i in range(6, 9))
    grad_b_inner = vec[9:13].reshape(-1)
    grad_b_query, grad_b_value = (vec[i] for i in range(13, 15))
    size = conv_part.shape[1]
    grad_w_conv = merged[:size].astype(f32)
    outer_sum = jnp.concatenate([merged[size : size + size // 2], merged[size + size // 2 :]], axis=1).astype(f32)
    inner_sum = inner_sum.astype(f32)

    per_device = head_sum.shape[0] // 2
    grad_w_query, grad_w_key, grad_w_value, grad_w_attn = (
        head_sum[i // 2 * per_device : (i // 2 + 1) * per_device, i % 2 * local : (i % 2 + 1) * local] for i in range(4)
    )
    return (
        molecules,
        chars_grad,
        grad_w_query,
        grad_b_query,
        grad_w_key,
        grad_w_value,
        grad_b_value,
        grad_w_attn.T,
        grad_b_attn_out,
        grad_gain_one,
        grad_shift_one,
        inner_sum,
        grad_b_inner,
        outer_sum.T,
        grad_b_outer,
        grad_gain_two,
        grad_shift_two,
        grad_w_conv,
        grad_b_conv,
        grad_gain_three,
        grad_shift_three,
    )


def solution(mesh):
    return jax.shard_map(
        on_device,
        mesh=mesh,
        in_specs=(
            P("dp", ("seq", "mp"), "pipe"),
            P("dp"),
            P(None, "mp"),
            P("mp"),
            P(None, "mp"),
            P(None, "mp"),
            P("mp"),
            P("mp", None),
            P(),
            P(),
            P(),
            P(None, "mp"),
            P("mp"),
            P("mp", None),
            P(),
            P(),
            P(),
            P(),
            P(),
            P(),
            P(),
            P("dp", ("seq", "mp"), "pipe"),
        ),
        out_specs=(
            P("dp", ("seq", "mp"), "pipe"),
            P("dp", ("seq", "mp"), "pipe"),
            P(("pipe", "dp", "seq"), "mp"),
            P(),
            P(("pipe", "dp", "seq"), "mp"),
            P(("pipe", "dp", "seq"), "mp"),
            P(),
            P("mp", ("pipe", "dp", "seq")),
            P(),
            P(),
            P(),
            P(("pipe", "dp", "seq"), "mp"),
            P(),
            P("mp", ("pipe", "dp", "seq")),
            P(),
            P(),
            P(),
            P(("pipe", "dp", "seq", "mp"), None),
            P(),
            P(),
            P(),
        ),
        check_vma=False,
    )
```

```python
import functools

import jax
import jax.numpy as jnp
from jax import lax
from jax.experimental import pallas as pl
from jax.experimental.pallas import tpu as pltpu
from jax.sharding import PartitionSpec as P

HEAD = 64
WINDOW = 128
KERNEL = 4
PAIR = 2 * HEAD
VMEM_LIMIT = 20 << 20
COST = 1000
HEADS_NEAR = True
UNITS_NEAR = True
PARTS = 1

epsilon = 1e-05
masked_score = -1e30
f32 = jnp.float32
bf16 = jnp.bfloat16


def mul(left, right):
    return jnp.dot(left, right, preferred_element_type=f32)


def mul_t(left, right):
    return lax.dot_general(left, right, (((1,), (1,)), ((), ())), preferred_element_type=f32)


def t_mul(left, right):
    return lax.dot_general(left, right, (((0,), (0,)), ((), ())), preferred_element_type=f32)


def gelu_parts(value):
    cdf = 0.5 + 0.5 * lax.erf(value * 2.0**-0.5)
    return value * cdf, cdf + value * jnp.exp(value * value * -0.5) * 0.3989422804014327


def norm_parts(value):
    centered = value - jnp.mean(value, axis=-1, keepdims=True)
    scale = lax.rsqrt(jnp.mean(centered * centered, axis=-1, keepdims=True) + epsilon)
    return centered * scale, scale


def norm_back(cotangent, normal, scale):
    first = jnp.mean(cotangent, axis=-1, keepdims=True)
    second = jnp.mean(cotangent * normal, axis=-1, keepdims=True)
    return scale * (cotangent - first - normal * second)


def col_sum(value):
    return jnp.sum(value, axis=0, keepdims=True)


def low(value):
    return value.astype(bf16)


START, PIPE, QUARTER, DP, MP, LENGTHS = range(6)


def call(body, grid, in_specs, out_specs, out_shape, args, info, scratch=(), flops=0, moved=0, limit=VMEM_LIMIT, kept=None):
    if kept:
        out_shape = [kept[i](tuple(o.shape), o.dtype) if i in kept else o for i, o in enumerate(out_shape)]
    return pl.pallas_call(
        body,
        grid_spec=pltpu.PrefetchScalarGridSpec(
            num_scalar_prefetch=1,
            grid=grid,
            in_specs=in_specs,
            out_specs=out_specs,
            scratch_shapes=scratch,
        ),
        out_shape=out_shape,
        compiler_params=pltpu.CompilerParams(vmem_limit_bytes=limit),
        cost_estimate=pl.CostEstimate(flops=int(flops) // COST, bytes_accessed=int(moved) // COST, transcendentals=0),
    )(info, *args)


def whole_block(array):
    zeros = (0,) * array.ndim
    return pl.BlockSpec(array.shape, lambda *_: zeros, pipeline_mode=pl.Buffered(1))


def lead_block(array, size=1):
    rest = (0,) * (array.ndim - 1)
    return pl.BlockSpec((size,) + tuple(array.shape[1:]), lambda i, *_: (i,) + rest)


def core_block(array, steps, size=1):
    rest = (0,) * (array.ndim - 1)
    return pl.BlockSpec((size,) + tuple(array.shape[1:]), lambda i, info: (info[PIPE] * steps + i,) + rest)


def chunk_block(array, size):
    return pl.BlockSpec((array.shape[0], size, array.shape[2]), lambda i, *_: (0, i, 0))


def fixed_block(array):
    zeros = (0,) * array.ndim
    return pl.BlockSpec(array.shape, lambda *_: zeros)


ANYWHERE = pl.BlockSpec(memory_space=pl.ANY)


def far(array):
    return pltpu.with_memory_space_constraint(array, pltpu.HBM)


def heads(array):
    return pltpu.with_memory_space_constraint(array, HEADS_MEMORY)


def hidden(array):
    return pltpu.with_memory_space_constraint(array, UNITS_MEMORY)


HEADS_MEMORY = pltpu.VMEM if HEADS_NEAR else pltpu.HBM
UNITS_MEMORY = pltpu.VMEM if UNITS_NEAR else pltpu.HBM


def shape_of(dims, kind):
    return jax.ShapeDtypeStruct(tuple(dims), kind)


def fetch(plan, sems):
    copies = [pltpu.make_async_copy(source, target, sems.at[i]) for i, (source, target) in enumerate(plan)]
    for copy in copies:
        copy.start()
    return copies


class Loads:
    def __init__(self, sems, *groups):
        self.groups, count = [], 0
        for group in groups:
            self.groups.append([(source, target, sems.at[count + i]) for i, (source, target) in enumerate(group)])
            count += len(group)

    def start(self):
        for group in self.groups:
            for copy in group:
                pltpu.make_async_copy(*copy).start()

    def ready(self, *indices):
        for index in indices:
            for copy in self.groups[index]:
                pltpu.make_async_copy(*copy).wait()

    def fill(self):
        @pl.when(pl.program_id(0) == 0)
        def _():
            self.start()
            self.ready(*range(len(self.groups)))

    def run(self, body):
        @pl.when(pl.program_id(0) == 0)
        def _():
            self.start()
            body(self.ready)

        @pl.when(pl.program_id(0) != 0)
        def _():
            body(lambda *indices: None)


def placed(info_ref, index, size):
    return pl.ds(pl.multiple_of((info_ref[QUARTER] ^ (0, 2, 1, 3)[index]) * size, size), size)


def plan_square(info_ref, pieces, targets, first=0):
    size = targets[0].shape[0] // 4
    return [
        [
            (piece.at[pl.ds((first + which) * size, size)], target.at[placed(info_ref, i, size)])
            for i, piece in enumerate(pieces)
        ]
        for which, target in enumerate(targets)
    ]


def plan_columns(source, target, step):
    return [[(source.at[:, pl.ds(at, step)], target.at[:, pl.ds(at, step)])] for at in range(0, target.shape[1], step)]


def plan_rows(source, target, step):
    return [[(source.at[pl.ds(at, step)], target.at[pl.ds(at, step)])] for at in range(0, target.shape[0], step)]


def plan_inner(info_ref, pieces, target):
    size = target.shape[0] // 4
    return [(piece.at[pl.ds(0, size)], target.at[placed(info_ref, i, size)]) for i, piece in enumerate(pieces)]


def plan_outer(info_ref, pieces, target):
    size = target.shape[0] // 2
    return [
        (piece, target.at[pl.ds(pl.multiple_of((info_ref[PIPE] ^ i) * size, size), size)])
        for i, piece in enumerate(pieces)
    ]


def plan_attn_out(info_ref, pieces, target):
    model = target.shape[1]
    size = target.shape[0] // 4
    columns = model // 2
    return [
        (
            piece.at[pl.ds(piece.shape[0] - 16 - (2 - side) * size, size)],
            target.at[placed(info_ref, i, size), pl.ds(side * columns, columns)],
        )
        for i, piece in enumerate(pieces)
        for side in range(2)
    ]


def pack_kernel(plan_of, info_ref, *refs):
    sems = refs[-1]
    for copy in fetch(plan_of(info_ref, *refs[:-1]), sems):
        copy.wait()


def pack(info, plan_of, args, out_shape, copies):
    return call(
        functools.partial(pack_kernel, plan_of),
        (1,),
        [ANYWHERE] * len(args),
        [fixed_block(o) for o in out_shape],
        out_shape,
        [far(a) for a in args],
        info,
        scratch=[pltpu.SemaphoreType.DMA((copies,))],
        moved=sum(o.size * 4 for o in out_shape),
    )


def gather_small_kernel(bq, bv, bi, *refs):
    vectors, (bias_ref, vec_ref) = refs[:-2], refs[-2:]
    local = bias_ref.shape[1]
    rows = [bq[...].reshape(1, local), bv[...].reshape(1, local)]
    inner = bi[...].reshape(1, -1)
    rows += [inner[:, i * local : (i + 1) * local] for i in range(inner.shape[1] // local)]
    rows = [row.astype(f32) for row in rows]
    rows.append(jnp.zeros((16 - len(rows), local), f32))
    bias_ref[...] = low(jnp.concatenate(rows, axis=0))
    rows = [v[...].reshape(1, -1).astype(f32) for v in vectors]
    rows.append(jnp.zeros((16 - len(rows), vec_ref.shape[1]), f32))
    vec_ref[...] = jnp.concatenate(rows, axis=0)


def gather_small(b_query, b_value, b_inner, vectors):
    return pl.pallas_call(
        gather_small_kernel,
        out_shape=[shape_of((16, b_query.shape[0]), bf16), shape_of((16, vectors[0].shape[0]), f32)],
    )(b_query, b_value, b_inner, *vectors)


def inner_bias(bias_ref, units):
    local = bias_ref.shape[1]
    return jnp.concatenate([bias_ref[2 + i : 3 + i] for i in range(units // local)], axis=1).astype(f32)


def quarter_of(info_ref, array):
    size = array.shape[0] // 4
    return pl.ds(pl.multiple_of(info_ref[QUARTER] * size, size), size)


def pack_first(info, weights, w_out, biases):
    model, local = weights[0].shape
    size, out_size, half = model // 4, w_out.shape[0] // 4, w_out.shape[1] // 2

    def plan_of(info_ref, wq, wk, wv, wo, bias, packet):
        plan = [(bias, packet.at[pl.ds(3 * size + 2 * out_size, 16)])]
        plan += [
            (w.at[quarter_of(info_ref, w)], packet.at[pl.ds(i * size, size)]) for i, w in enumerate((wq, wk, wv))
        ]
        return plan + [
            (
                wo.at[quarter_of(info_ref, wo), pl.ds(side * half, half)],
                packet.at[pl.ds(3 * size + side * out_size, out_size)],
            )
            for side in range(2)
        ]

    out_shape = [shape_of((3 * size + 2 * out_size + 16, local), bf16)]
    return pack(info, plan_of, [*weights, w_out, biases], out_shape, 6)[0]


def pack_second(info, w_inner, w_outer):
    def plan_of(info_ref, wi, wo, inner, outer):
        size = wo.shape[0] // 2
        half = pl.ds(pl.multiple_of(info_ref[PIPE] * size, size), size)
        return [(wi.at[quarter_of(info_ref, wi)], inner), (wo.at[half], outer)]

    out_shape = [shape_of((a.shape[0] // n, a.shape[1]), bf16) for a, n in ((w_inner, 4), (w_outer, 2))]
    return pack(info, plan_of, [w_inner, w_outer], out_shape, 2)


def pack_rows(info, arrays):
    rows = arrays[0].shape[0] // 2

    def plan_of(info_ref, *refs):
        theirs = pl.ds((1 - info_ref[PIPE]) * rows, rows)
        return [(ref.at[theirs], out) for ref, out in zip(refs[: len(arrays)], refs[len(arrays) :])]

    out_shape = [shape_of((rows,) + tuple(a.shape[1:]), bf16) for a in arrays]
    return pack(info, plan_of, arrays, out_shape, len(arrays))


def pack_rims(info, characters, center_got, width):
    rows, span, half = center_got.shape

    def plan_of(info_ref, chars, got, tail, head):
        mine = pl.ds(info_ref[PIPE] * rows, rows)
        return [
            (source, target.at[which])
            for target, at in ((tail, pl.ds(span - width, width)), (head, pl.ds(0, width)))
            for which, source in enumerate((chars.at[mine, at], got.at[:, at]))
        ]

    out_shape = [shape_of((2, rows, width, half), bf16)] * 2
    return pack(info, plan_of, [characters, center_got], out_shape, 4)


def pair_lanes(rows):
    return lax.broadcasted_iota(jnp.int32, (rows, PAIR), 1) < HEAD


def split_pair(both, is_first):
    zero = jnp.zeros_like(both)
    return jnp.concatenate([jnp.where(is_first, both, zero), jnp.where(is_first, zero, both)], axis=0)


def join_rows(stacked):
    block = stacked.shape[1] // 2
    return jnp.concatenate([stacked[:HEAD, :block], stacked[HEAD:, block:]], axis=0)


def window_of(block):
    dims = (block + 2 * WINDOW, block)
    q_at = lax.broadcasted_iota(jnp.int32, dims, 1)
    k_at = lax.broadcasted_iota(jnp.int32, dims, 0) - WINDOW
    return jnp.abs(q_at - k_at) < WINDOW, k_at


def window_bias(in_window, position, length):
    bias = jnp.where(in_window & (position >= 0) & (position < length), 0.0, masked_score)
    return jnp.concatenate([bias, bias], axis=1)


def alive(info_ref, span, size, stride):
    per_row = span // stride
    step = pl.program_id(0)
    first = step * size
    pieces = []
    for j in range(max(1, size // per_row)):
        index = lax.broadcasted_iota(jnp.int32, (min(size, per_row), 1), 0) + lax.rem(first, per_row)
        length = info_ref[LENGTHS + first // per_row + j]
        pieces.append((info_ref[START] + index * stride < length).astype(f32))
    return pieces[0] if len(pieces) == 1 else jnp.concatenate(pieces, axis=0)


def inner_blocks(span, block):
    return [i for i in range(span // block) if i * block >= WINDOW and (i + 1) * block + WINDOW <= span]


def attend_block(index, block, info_ref, q_ref, att_ref, lse_ref, keys_of, values_of):
    width = block + 2 * WINDOW
    rows = slice(index * block, (index + 1) * block)
    is_first = pair_lanes(block)
    lanes = lax.broadcasted_iota(jnp.int32, (block, PAIR), 1)
    q_at = lax.broadcasted_iota(jnp.int32, (block, width), 0)
    k_at = lax.broadcasted_iota(jnp.int32, (block, width), 1) - WINDOW
    position = k_at + (info_ref[START] + index * block)
    length = info_ref[LENGTHS + pl.program_id(0)]
    allowed = (jnp.abs(q_at - k_at) < WINDOW) & (position >= 0) & (position < length)
    bias = jnp.where(allowed, 0.0, masked_score)
    bias = jnp.concatenate([bias, bias], axis=0)
    totals = jnp.zeros((block, PAIR), f32)
    for pair in range(q_ref.shape[2] // PAIR):
        cols = slice(pair * PAIR, (pair + 1) * PAIR)
        scores = mul_t(split_pair(q_ref[0, rows, cols], is_first), keys_of(cols)) + bias
        top = jnp.max(scores, axis=-1, keepdims=True)
        weights = jnp.exp(scores - top)
        total = jnp.sum(weights, axis=-1, keepdims=True)
        out = mul(low(weights), values_of(cols)) * (1.0 / total)
        att_ref[0, rows, cols] = low(jnp.where(is_first, out[:block], out[block:]))
        log_total = top + jnp.log(total)
        totals = jnp.where(lanes == 2 * pair, log_total[:block], totals)
        totals = jnp.where(lanes == 2 * pair + 1, log_total[block:], totals)
    lse_ref[0, index] = totals.T[:8]


def by_core(info_ref, half, work):
    lower, upper = slice(0, half), slice(half, 2 * half)
    pl.when(info_ref[PIPE] == 0)(lambda: work(lower, upper))
    pl.when(info_ref[PIPE] == 1)(lambda: work(upper, lower))


def attend_inner_kernel(span, block, other, info_ref, center, center_got, bias_ref, *refs):
    sources, refs = (refs[:4], refs[4:]) if other else (refs[:3], refs[3:])
    q_ref, k_ref, v_ref, att_ref, lse_ref, wq_ref, wk_ref, wv_ref, x_ref, sems = refs
    targets = (wq_ref, wk_ref, wv_ref)
    plan = plan_square(info_ref, sources, targets) if other else [[pair] for pair in zip(sources, targets)]

    def place(mine, got):
        x_ref[:, mine] = center[0]
        x_ref[:, got] = center_got[0]

    by_core(info_ref, center.shape[2], place)

    def work(ready):
        x = x_ref[...]
        ready(0)
        q_ref[0] = low(low(mul(x, wq_ref[...]) + bias_ref[0:1].astype(f32)).astype(f32) * HEAD ** (-0.5))
        ready(1)
        k_ref[0] = low(mul(x, wk_ref[...]))
        ready(2)
        v_ref[0] = low(mul(x, wv_ref[...]) + bias_ref[1:2].astype(f32))
        for index in inner_blocks(span, block):
            window = slice(index * block - WINDOW, (index + 1) * block + WINDOW)
            attend_block(
                index,
                block,
                info_ref,
                q_ref,
                att_ref,
                lse_ref,
                lambda cols, window=window: k_ref[0, window, cols],
                lambda cols, window=window: v_ref[0, window, cols],
            )

    Loads(sems, *plan).run(work)


def attend_inner(info, center, center_got, sources, biases, span, block):
    rows, _, half = center_got.shape
    local = biases.shape[1]
    model = 2 * half
    other = len(sources) == 4
    out_shape = [shape_of((rows, span, local), bf16)] * 4 + [shape_of((rows, span // block, 8, block), f32)]
    return call(
        functools.partial(attend_inner_kernel, span, block, other),
        (rows,),
        [core_block(center, rows), lead_block(center_got), whole_block(biases)] + [ANYWHERE] * len(sources),
        [lead_block(o) for o in out_shape],
        out_shape,
        [far(center), center_got, biases, *(sources if other else map(far, sources))],
        info,
        scratch=[pltpu.VMEM((model, local), bf16)] * 3
        + [pltpu.VMEM((span, model), bf16), pltpu.SemaphoreType.DMA((12,))],
        kept=dict.fromkeys(range(5), HEADS_MEMORY),
        flops=6 * rows * span * model * local,
        moved=rows * span * model * 8,
    )


def attend_outer_kernel(span, block, info_ref, center, center_got, left, right, vec_ref, *refs):
    biases, refs = refs[:2], refs[2:]
    groups, refs = (refs[:5], refs[5:10]), refs[10:]
    own_sources, pieces, refs = refs[:3], refs[3:7], refs[7:]
    outs, refs = (refs[:4], refs[4:8]), refs[8:]
    n_ref, s_ref, mid_ref, x_ref, *refs = refs
    own_w, other_w, (k_all, v_all, sems) = refs[:3], refs[3:6], refs[6:]
    loads = Loads(
        sems,
        list(zip(own_sources[:2], own_w)),
        [(own_sources[2], own_w[2])],
        sum(plan_square(info_ref, pieces, other_w[:2], 1), []),
        plan_attn_out(info_ref, pieces, other_w[2]),
    )

    def place(mine, got):
        for at, mine_part, got_part in (
            (slice(0, WINDOW), left[0, 0], left[1, 0]),
            (slice(WINDOW, WINDOW + span), center[0], center_got[0]),
            (slice(WINDOW + span, 2 * WINDOW + span), right[0, 0], right[1, 0]),
        ):
            x_ref[0, at, mine] = mine_part
            x_ref[0, at, got] = got_part

    by_core(info_ref, center.shape[2], place)
    inner = inner_blocks(span, block)
    width = block + 2 * WINDOW

    def work(ready):
        rims = jnp.concatenate([x_ref[0, :WINDOW], x_ref[0, WINDOW + span :]], axis=0)
        branch = None
        for half, (bias_ref, group, (wk_ref, wv_ref, wo_ref), out) in enumerate(
            zip(biases, groups, (own_w, other_w), outs)
        ):
            q_ref, k_ref, v_ref, att_in, lse_in = group
            krim_ref, vrim_ref, att_ref, lse_ref = out
            ready(2 * half)
            krim_ref[0] = low(mul(rims, wk_ref[...]))
            vrim_ref[0] = low(mul(rims, wv_ref[...]) + bias_ref[1:2].astype(f32))
            join_rims(k_all, k_ref, krim_ref, span)
            join_rims(v_all, v_ref, vrim_ref, span)
            for index in range(span // block):
                rows = slice(index * block, (index + 1) * block)
                if index in inner:
                    att_ref[0, rows] = att_in[0, rows]
                    lse_ref[0, index] = lse_in[0, index]
                    continue
                window = slice(index * block, index * block + width)
                attend_block(
                    index,
                    block,
                    info_ref,
                    q_ref,
                    att_ref,
                    lse_ref,
                    lambda cols, window=window: k_all[window, cols],
                    lambda cols, window=window: v_all[window, cols],
                )
            ready(2 * half + 1)
            term = mul(att_ref[0], wo_ref[...])
            branch = term if branch is None else branch + term
        before = x_ref[0, WINDOW : WINDOW + span].astype(f32) + branch + vec_ref[B_ATTN : B_ATTN + 1]
        normal, scale = norm_parts(before)
        n_ref[0] = low(normal)
        s_ref[0] = jnp.broadcast_to(scale, s_ref.shape[1:])
        mid_ref[0] = low(normal * vec_ref[GAIN_ONE : GAIN_ONE + 1] + vec_ref[SHIFT_ONE : SHIFT_ONE + 1])

    loads.run(work)


def join_rims(target, center, rims, span):
    target[:WINDOW] = rims[0, :WINDOW]
    target[WINDOW : WINDOW + span] = center[0]
    target[WINDOW + span :] = rims[0, WINDOW:]


def attend_outer(info, x_parts, vectors, biases, groups, own_sources, pieces, span, block):
    center, center_got, left, right = x_parts
    rows, _, half = center_got.shape
    local = biases[0].shape[1]
    model = 2 * half
    extent = span + 2 * WINDOW
    per_group = [
        shape_of((rows, 2 * WINDOW, local), bf16),
        shape_of((rows, 2 * WINDOW, local), bf16),
        shape_of((rows, span, local), bf16),
        shape_of((rows, span // block, 8, block), f32),
    ]
    out_shape = 2 * per_group + [
        shape_of((rows, span, model), bf16),
        shape_of((rows, span, PAIR), f32),
        shape_of((rows, span, model), bf16),
        shape_of((rows, extent, model), bf16),
    ]
    flat = [a for group in groups for a in group]
    rim = pl.BlockSpec((2, 1, WINDOW, half), lambda i, *_: (0, i, 0, 0))
    return call(
        functools.partial(attend_outer_kernel, span, block),
        (rows,),
        [core_block(center, rows), lead_block(center_got), rim, rim, whole_block(vectors)]
        + [whole_block(a) for a in biases]
        + [lead_block(a) for a in flat]
        + [ANYWHERE] * 7,
        [lead_block(o) for o in out_shape],
        out_shape,
        [far(center), center_got, left, right, vectors, *biases, *map(heads, flat), *map(far, (*own_sources, *pieces))],
        info,
        scratch=[pltpu.VMEM((model, local), bf16), pltpu.VMEM((model, local), bf16), pltpu.VMEM((local, model), bf16)] * 2
        + [pltpu.VMEM((extent, local), bf16)] * 2
        + [pltpu.SemaphoreType.DMA((19,))],
        kept=dict.fromkeys((8, 9), pltpu.HBM),
        flops=6 * rows * span * model * local,
        moved=rows * extent * model * 8,
        limit=28 << 20,
    )


def attend_back_kernel(span, block, other, info_ref, gb_ref, q_ref, kc_ref, kr_ref, vc_ref, vr_ref, lse_ref, *refs):
    first_step = pl.program_id(0) == 0
    if other:
        pieces, refs = refs[:4], refs[4:]
        dq_ref, dk_ref, dv_ref, vec_ref, ga_ref, k_ref, v_ref, kt_ref, dk_acc, dv_acc, wo_ref, sems = refs

        Loads(sems, plan_attn_out(info_ref, pieces, wo_ref)).fill()

    else:
        wo_ref, *vecs, dq_ref, dk_ref, dv_ref, all_ref, ga_ref, k_ref, v_ref, kt_ref, dk_acc, dv_acc, vec_ref = refs

    @pl.when(first_step)
    def _():
        vec_ref[...] = jnp.zeros_like(vec_ref)

    length = info_ref[LENGTHS + pl.program_id(0)]
    start = info_ref[START]
    width = block + 2 * WINDOW
    pairs = q_ref.shape[2] // PAIR
    ga_ref[...] = low(mul_t(gb_ref[0], wo_ref[...]))
    dk_acc[...] = jnp.zeros_like(dk_acc)
    dv_acc[...] = jnp.zeros_like(dv_acc)
    join_rims(k_ref, kc_ref, kr_ref, span)
    join_rims(v_ref, vc_ref, vr_ref, span)
    kt_ref[...] = k_ref[...].T
    is_first = pair_lanes(block)
    in_window, k_at = window_of(block)
    for index in range(span // block):
        at = index * block
        keep = slice(at, at + width)
        bias = window_bias(in_window, k_at + (start + at), length)
        for pair in range(pairs):
            cols = slice(pair * PAIR, (pair + 1) * PAIR)
            q2 = split_pair(q_ref[0, at : at + block, cols], is_first)
            g2 = split_pair(ga_ref[at : at + block, cols], is_first)
            log_total = jnp.concatenate(
                [lse_ref[0, index, 2 * pair : 2 * pair + 1], lse_ref[0, index, 2 * pair + 1 : 2 * pair + 2]], axis=1
            )
            probs = jnp.exp(mul_t(k_ref[keep, cols], q2) + bias - log_total)
            grad_probs = mul_t(v_ref[keep, cols], g2)
            inner = jnp.sum(probs * grad_probs, axis=0, keepdims=True)
            grad_scores = low(probs * (grad_probs - inner))
            dk_acc[keep, cols] += mul(grad_scores, q2)
            dv_acc[keep, cols] += mul(low(probs), g2)
            grad_q = join_rows(mul(kt_ref[cols, keep], grad_scores)) * HEAD ** (-0.5)
            dq_ref[0, at : at + block, cols] = low(grad_q.T)

    dk_ref[0] = low(dk_acc[...])
    grad_values = low(dv_acc[...])
    dv_ref[0] = grad_values
    vec_ref[0:1] += col_sum(dq_ref[0].astype(f32))
    vec_ref[1:2] += col_sum(grad_values.astype(f32))
    if other:
        return

    vec_conv, vec_one, inner_own, inner_other, vec_other = vecs
    local = q_ref.shape[2]
    model = vec_one.shape[1]

    def collect(first, second, inner_first, inner_second):
        all_ref[...] = jnp.zeros_like(all_ref)
        all_ref[0:6] = vec_conv[0:6]
        all_ref[6:9] = vec_one[0:3]
        per_half = inner_first.shape[1] // model
        for half, inner in enumerate((inner_first, inner_second)):
            for i in range(per_half):
                row = 9 + half * per_half + i
                all_ref[row : row + 1] = inner[0:1, i * model : (i + 1) * model]
        row = 9 + 2 * per_half
        all_ref[row : row + 2, :local] = first[0:2]
        all_ref[row : row + 2, local:] = second[0:2]

    last_step = pl.program_id(0) == pl.num_programs(0) - 1
    pl.when(last_step & (info_ref[MP] == 0))(lambda: collect(vec_ref, vec_other, inner_own, inner_other))
    pl.when(last_step & (info_ref[MP] == 1))(lambda: collect(vec_other, vec_ref, inner_other, inner_own))


def attend_back(info, grad_branch, kept, w_out, block, vecs=None):
    rows, span, local = kept[0].shape
    extent = span + 2 * WINDOW
    model = grad_branch.shape[2]
    other = isinstance(w_out, (list, tuple))
    out_shape = [
        shape_of((rows, span, local), bf16),
        shape_of((rows, extent, local), bf16),
        shape_of((rows, extent, local), bf16),
        shape_of((8, local) if other else (16, model), f32),
    ]
    args = [grad_branch, *map(heads, kept)]
    in_specs = [lead_block(a) for a in args]
    scratch = [
        pltpu.VMEM((span, local), bf16),
        pltpu.VMEM((extent, local), bf16),
        pltpu.VMEM((extent, local), bf16),
        pltpu.VMEM((local, extent), bf16),
        pltpu.VMEM((extent, local), f32),
        pltpu.VMEM((extent, local), f32),
    ]
    if other:
        args += list(map(far, w_out))
        in_specs += [ANYWHERE] * 4
        scratch += [pltpu.VMEM((local, model), bf16), pltpu.SemaphoreType.DMA((8,))]
    else:
        args += [far(w_out), *vecs]
        in_specs += [whole_block(a) for a in args[7:]]
        scratch += [pltpu.VMEM((8, local), f32)]
    return call(
        functools.partial(attend_back_kernel, span, block, other),
        (rows,),
        in_specs,
        [lead_block(o) for o in out_shape[:3]] + [fixed_block(out_shape[3])],
        out_shape,
        args,
        info,
        scratch=scratch,
        flops=6 * rows * span * local * (model + 5 * (block + 2 * WINDOW)),
        moved=rows * extent * model * 8,
    )


B_ATTN, GAIN_ONE, SHIFT_ONE, B_OUTER, GAIN_TWO, SHIFT_TWO, B_CONV, GAIN_THREE, SHIFT_THREE = range(9)


def feed_kernel(last, span, info_ref, x_ref, bi_ref, *refs):
    if last:
        part_ref, n_ref, vec_ref = refs[:3]
        inner_pieces, outer_pieces, refs = refs[3:7], refs[7:9], refs[9:]
        act_ref, slope_ref, n2_ref, scale_ref, grp_ref, wi_ref, wo_ref, sems, sent_ref = refs
    else:
        wi, wo, act_ref, slope_ref, part_ref, wi_ref, wo_ref, sems = refs
    x = x_ref[...]
    units = wi_ref.shape[1]
    step = 512
    count = units // step
    if last:
        plans = [plan_inner(info_ref, inner_pieces, wi_ref), plan_outer(info_ref, outer_pieces, wo_ref)]
        inner_at, outer_at = [[0]] + [[]] * count, [[1]] + [[]] * count
    else:
        plans = plan_columns(wi, wi_ref, step) + plan_rows(wo, wo_ref, step)
        inner_at, outer_at = [[i] for i in range(count)], [[count + i] for i in range(count)]
    def work(ready):
        bias = inner_bias(bi_ref, units)
        total = None
        for i in range(count):
            cols = slice(i * step, (i + 1) * step)
            ready(*inner_at[i])
            act, slope = gelu_parts(mul(x, wi_ref[:, cols]) + bias[:, cols])
            act = low(act)
            act_ref[:, cols] = act
            slope_ref[:, cols] = low(slope)
            ready(*outer_at[i])
            term = mul(act, wo_ref[cols, :])
            total = term if total is None else total + term
        if not last:
            part_ref[...] = low(total)
            return

        middle = n_ref[...].astype(f32) * vec_ref[GAIN_ONE : GAIN_ONE + 1] + vec_ref[SHIFT_ONE : SHIFT_ONE + 1]
        before = middle + part_ref[...].astype(f32) + total + vec_ref[B_OUTER : B_OUTER + 1]
        normal, scale = norm_parts(before)
        n2_ref[...] = low(normal)
        scale_ref[...] = jnp.broadcast_to(scale, scale_ref.shape)
        size = x.shape[0]
        sent = normal * vec_ref[GAIN_TWO : GAIN_TWO + 1] + vec_ref[SHIFT_TWO : SHIFT_TWO + 1]
        sent = sent * alive(info_ref, span, size, 1)
        chunks = range(sent_ref.shape[0])
        for c in chunks:
            sent_ref[c] = sent[:, c * PAIR : (c + 1) * PAIR]
        for k in range(KERNEL):
            rows = pl.ds(k, size // KERNEL, stride=KERNEL)
            grp_ref[k] = low(jnp.concatenate([sent_ref[c, rows, :] for c in chunks], axis=1))

    Loads(sems, *plans).run(work)


def feed(info, middle, biases, units, span, tile, w_inner=None, w_outer=None, tail=None, pieces=None):
    tokens, model = middle.shape
    args = [middle, biases]
    in_specs = [lead_block(middle, tile), whole_block(biases)]
    out_shape = [shape_of((tokens, units), bf16), shape_of((tokens, units), bf16), shape_of((tokens, model), bf16)]
    scratch = [
        pltpu.VMEM((model, units), bf16),
        pltpu.VMEM((units, model), bf16),
        pltpu.SemaphoreType.DMA((8,)),
    ]
    if tail is None:
        args += [far(w_inner), far(w_outer)]
        in_specs += [ANYWHERE] * 2
        out_specs = [lead_block(o, tile) for o in out_shape]
    else:
        out_shape += [shape_of((tokens, PAIR), f32), shape_of((KERNEL, tokens // KERNEL, model), bf16)]
        args += [tail[0], far(tail[1]), tail[2], *pieces]
        in_specs += [lead_block(a, tile) for a in tail[:2]] + [whole_block(tail[2])] + [ANYWHERE] * 6
        out_specs = [lead_block(o, tile) for o in out_shape[:4]] + [chunk_block(out_shape[4], tile // KERNEL)]
        scratch.append(pltpu.VMEM((model // PAIR, tile, PAIR), f32))
    return call(
        functools.partial(feed_kernel, tail is not None, span),
        (tokens // tile,),
        in_specs,
        out_specs,
        out_shape,
        args,
        info,
        scratch=scratch,
        kept={0: pltpu.VMEM, 1: pltpu.HBM},
        flops=4 * tokens * model * units * 1.5,
        moved=tokens * units * 8,
    )


def conv_kernel(mols, span, info_ref, grp_ref, wc_ref, vecs_ref, mg_ref, mg_got_ref, n2_ref, sc_ref,
                mol_ref, mol_out_ref, gc_ref, feed_ref, vec_ref, back_ref, mg_all):

    @pl.when(pl.program_id(0) == 0)
    def _():
        vec_ref[...] = jnp.zeros_like(vec_ref)

    half = mg_ref.shape[1]
    lower, upper = slice(0, half), slice(half, 2 * half)

    def place(mine, got):
        mg_all[:, mine] = mg_ref[...]
        mg_all[:, got] = mg_got_ref[...]

    pl.when(info_ref[PIPE] == 0)(lambda: place(lower, upper))
    pl.when(info_ref[PIPE] == 1)(lambda: place(upper, lower))

    def vector(index):
        return vecs_ref[index : index + 1]

    total = None
    for k in range(KERNEL):
        term = mul(grp_ref[k], wc_ref[k])
        total = term if total is None else total + term
    value, slope = gelu_parts(total + vector(B_CONV))
    normal, scale = norm_parts(value)
    live = alive(info_ref, span, mols, KERNEL)
    cotangent = mg_all[...].astype(f32) * live
    molecules = low((normal * vector(GAIN_THREE) + vector(SHIFT_THREE)) * live)

    def split(mine, got):
        mol_ref[...] = molecules[:, mine]
        mol_out_ref[...] = molecules[:, got]

    pl.when(info_ref[PIPE] == 0)(lambda: split(lower, upper))
    pl.when(info_ref[PIPE] == 1)(lambda: split(upper, lower))
    grad = low(norm_back(cotangent * vector(GAIN_THREE), normal, scale) * slope)
    gc_ref[...] = grad
    chunks = range(back_ref.shape[0])
    for k in range(KERNEL):
        back = low(mul_t(grad, wc_ref[k])).astype(f32)
        for c in chunks:
            back_ref[c, pl.ds(k, mols, stride=KERNEL), :] = back[:, c * PAIR : (c + 1) * PAIR]
    masked = jnp.concatenate([back_ref[c] for c in chunks], axis=1) * alive(info_ref, span, KERNEL * mols, 1)
    n2 = n2_ref[...].astype(f32)
    grad_two = norm_back(masked * vector(GAIN_TWO), n2, sc_ref[:, :1])
    feed_ref[...] = low(grad_two)
    vec_ref[...] += jnp.concatenate(
        [
            col_sum(grad.astype(f32)),
            col_sum(cotangent * normal),
            col_sum(cotangent),
            col_sum(masked * n2),
            col_sum(masked),
            col_sum(grad_two),
            jnp.zeros((2, grad_two.shape[1]), f32),
        ],
        axis=0,
    )


def conv(info, grouped, w_conv, vectors, mol_grad, mol_got, n2, scale2, span, steps):
    _, all_mols, model = grouped.shape
    tokens = KERNEL * all_mols
    tile = tokens // steps
    mols = tile // KERNEL
    args = [grouped, w_conv, vectors, far(mol_grad), far(mol_got), n2, scale2]
    in_specs = [
        chunk_block(grouped, mols),
        whole_block(w_conv),
        whole_block(vectors),
        core_block(mol_grad, steps, mols),
        lead_block(mol_got, mols),
        lead_block(n2, tile),
        lead_block(scale2, tile),
    ]
    out_shape = [
        shape_of((all_mols, model // 2), bf16),
        shape_of((all_mols, model // 2), bf16),
        shape_of((all_mols, model), bf16),
        shape_of((tokens, model), bf16),
        shape_of((8, model), f32),
    ]
    out_specs = [lead_block(o, mols) for o in out_shape[:3]] + [lead_block(out_shape[3], tile), fixed_block(out_shape[4])]
    return call(
        functools.partial(conv_kernel, mols, span),
        (steps,),
        in_specs,
        out_specs,
        out_shape,
        args,
        info,
        scratch=[
            pltpu.VMEM((model // PAIR, tile, PAIR), f32),
            pltpu.VMEM((mols, model), bf16),
        ],
        flops=4 * tokens * model * model * 1.5,
        moved=tokens * model * 30,
    )


def dp_place(info_ref, index, count):
    away = info_ref[DP] ^ index
    place, bits = 0, count.bit_length() - 1
    for bit in range(bits):
        place = place + (((away >> bit) & 1) << (bits - 1 - bit))
    return place


def cut(width):
    size = width // PARTS
    return [slice(i * size, (i + 1) * size) for i in range(PARTS)]


def conv_weight_kernel(mine, per_step, info_ref, grp_ref, grad_ref, *refs):
    value = t_mul(grp_ref[0], grad_ref[...])
    gots, outs = (refs[:PARTS], refs[PARTS:]) if mine else ((), refs)
    count, size = outs[0].shape[:2]
    for j in range(per_step):
        place = dp_place(info_ref, pl.program_id(0) * per_step + j, count)
        part = value[j * size : (j + 1) * size]
        for i, cols in enumerate(cut(value.shape[1])):
            if mine:
                outs[0][place, :, cols] = low(part[:, cols] + gots[i][place].astype(f32))
            else:
                outs[i][place] = low(part[:, cols])


def conv_weight(info, other_side, grouped, grad, dp_size, got=()):
    kernel, mols, model = grouped.shape
    half = kernel // 2
    args = [grouped, grad, *got]
    in_specs = [
        pl.BlockSpec((1, mols, model), lambda i, info_ref: ((info_ref[PIPE] ^ other_side) * half + i, 0, 0)),
    ] + [whole_block(a) for a in args[1:]]
    dims = (dp_size, half * model // dp_size)
    out_shape = [shape_of(dims + (model,), bf16)] if got else [shape_of(dims + (model // PARTS,), bf16)] * PARTS
    return call(
        functools.partial(conv_weight_kernel, bool(got), dp_size // half),
        (half,),
        in_specs,
        [fixed_block(o) for o in out_shape],
        out_shape,
        args,
        info,
        flops=2 * half * mols * model * model,
        moved=half * model * model * 8,
    )


def weight_kernel(mine, info_ref, left_ref, *refs):
    rights, refs = refs[:2], refs[2:]
    gots, outs = (refs[:PARTS], refs[PARTS:]) if mine else ((), refs)
    count, size = outs[0].shape[1:3]
    for index in range(2):
        value = t_mul(left_ref[...], rights[index][...])
        for d in range(count):
            place = dp_place(info_ref, d, count)
            part = value[d * size : (d + 1) * size]
            if mine:
                for i, got in enumerate(gots):

                    @pl.when(pl.program_id(0) == i)
                    def _(got=got, part=part, place=place):
                        outs[0][index, place] = low(part + got[index, place].astype(f32))

            else:
                for i, out in enumerate(outs):

                    @pl.when(pl.program_id(0) == i)
                    def _(out=out, part=part, place=place):
                        out[index, place] = low(part)


def weight(info, other_side, left, right_own, right_other, dp_size, got=()):
    tokens, model = left.shape
    columns = right_own.shape[1]
    half = model // 2
    tile = columns // PARTS
    args = [left, hidden(right_own), hidden(right_other), *got]
    in_specs = [
        pl.BlockSpec((tokens, half), lambda i, info_ref: (0, info_ref[PIPE] ^ other_side)),
        pl.BlockSpec((tokens, tile), lambda i, *_: (0, i)),
        pl.BlockSpec((tokens, tile), lambda i, *_: (0, i)),
    ] + [whole_block(a) for a in got]
    dims = (2, dp_size, half // dp_size)
    if got:
        out_shape = [shape_of(dims + (columns,), bf16)]
        out_specs = [pl.BlockSpec(dims + (tile,), lambda i, *_: (0, 0, 0, i))]
    else:
        out_shape = [shape_of(dims + (tile,), bf16)] * PARTS
        out_specs = [fixed_block(o) for o in out_shape]
    return call(
        functools.partial(weight_kernel, bool(got)),
        (PARTS,),
        in_specs,
        out_specs,
        out_shape,
        args,
        info,
        flops=4 * tokens * half * columns,
        moved=tokens * columns * 4 + half * columns * 8,
    )


def project_weight_kernel(span, dp_size, mine, extra, info_ref, x_ref, gb_ref, dq, dk, dv, att, *refs):
    got_ref, refs = (refs[0], refs[1:]) if mine else (None, refs)
    extra_ref, outs = (refs[0], refs[1:]) if extra else (None, refs)
    rows = x_ref.shape[0]
    local = dq.shape[2]
    size = x_ref.shape[2] // dp_size
    for index, right in enumerate((dq, dk, dv, att)):
        value = None
        for row in range(rows):
            if index == 0:
                left = x_ref[row, WINDOW : WINDOW + span]
            elif index == 3:
                left = gb_ref[row]
            else:
                left = x_ref[row]
            term = t_mul(left, right[row])
            value = term if value is None else value + term
        cols = slice(index * local, (index + 1) * local)
        inside = slice(index % 2 * local, (index % 2 + 1) * local)
        for d in range(dp_size):
            at = pl.ds(pl.multiple_of(dp_place(info_ref, d, dp_size) * size, size), size)
            part = value[d * size : (d + 1) * size]
            if mine:
                outs[index // 2][at, inside] = low(part + got_ref[at, cols].astype(f32))
            else:
                outs[0][at, cols] = low(part)
    if extra:
        outs[0][dp_size * size :] = extra_ref[...]


def project_weight(info, other_side, x_ext, grad_branch, grads, span, dp_size, got=None, extra=None):
    rows, extent, model = x_ext.shape
    half = model // 2
    local = grads[0].shape[2]
    mine = got is not None
    more = ([got] if mine else []) + ([] if extra is None else [extra])
    args = [heads(x_ext), grad_branch, *grads[:3], heads(grads[3]), *more]
    in_specs = [
        pl.BlockSpec((rows, extent, half), lambda i, info_ref: (0, 0, info_ref[PIPE] ^ other_side)),
        pl.BlockSpec((rows, span, half), lambda i, info_ref: (0, 0, info_ref[PIPE] ^ other_side)),
    ] + [whole_block(a) for a in args[2:]]
    if mine:
        extra_rows = 0 if extra is None else extra.shape[0]
        out_shape = [shape_of((half + extra_rows, 2 * local), bf16), shape_of((half, 2 * local), bf16)]
    else:
        out_shape = [shape_of((half, 4 * local), bf16)]
    return call(
        functools.partial(project_weight_kernel, span, dp_size, mine, extra is not None),
        (1,),
        in_specs,
        [fixed_block(o) for o in out_shape],
        out_shape,
        args,
        info,
        flops=8 * rows * extent * half * local,
        moved=rows * extent * model * 6,
    )


def feed_back_kernel(info_ref, gf_ref, sl_own, sl_other, n_ref, sc_ref, wo, wi, vecs_ref, *refs):
    inner_pieces, outer_pieces, refs = refs[:4], refs[4:6], refs[6:]
    gh_own, gh_other, gb_ref, vec_ref, bi_own, bi_other, wi_own, wo_own, wi_other, wo_other, sems = refs
    units = wo_own.shape[0]
    step = 512
    count = units // step
    loads = Loads(
        sems,
        *plan_rows(wo, wo_own, step),
        *plan_columns(wi, wi_own, step),
        plan_outer(info_ref, outer_pieces, wo_other),
        plan_inner(info_ref, inner_pieces, wi_other),
    )

    @pl.when(pl.program_id(0) == 0)
    def _():
        vec_ref[...] = jnp.zeros_like(vec_ref)
        bi_own[...] = jnp.zeros_like(bi_own)
        bi_other[...] = jnp.zeros_like(bi_other)

    def half(ready, total, slope_ref, wo_ref, wi_ref, gh_ref, bi_ref, outer_at, inner_at):
        for i in range(count):
            cols = slice(i * step, (i + 1) * step)
            ready(*outer_at[i])
            grad = low(mul_t(gf_ref[...], wo_ref[cols, :]) * slope_ref[:, cols].astype(f32))
            gh_ref[:, cols] = grad
            bi_ref[:1, cols] += col_sum(grad.astype(f32))
            ready(*inner_at[i])
            total = total + mul_t(grad, wi_ref[:, cols])
        return total

    def work(ready):
        chunks = [[i] for i in range(count)], [[count + i] for i in range(count)]
        total = half(ready, gf_ref[...].astype(f32), sl_own, wo_own, wi_own, gh_own, bi_own, *chunks)
        chunks = [[2 * count]] + [[]] * count, [[2 * count + 1]] + [[]] * count
        total = half(ready, total, sl_other, wo_other, wi_other, gh_other, bi_other, *chunks)
        normal = n_ref[...].astype(f32)
        grad_one = norm_back(total * vecs_ref[GAIN_ONE : GAIN_ONE + 1], normal, sc_ref[:, :1])
        gb_ref[...] = low(grad_one)
        vec_ref[...] += jnp.concatenate(
            [col_sum(grad_one), col_sum(total * normal), col_sum(total), jnp.zeros((5, total.shape[1]), f32)], axis=0
        )

    loads.run(work)


def feed_back(info, grad_feed, slopes, n1, scale1, w_outer, w_inner, vectors, pieces, tile):
    tokens, model = grad_feed.shape
    units = w_outer.shape[0]
    args = [grad_feed, *map(far, slopes), far(n1), far(scale1), far(w_outer), far(w_inner), vectors, *map(far, pieces)]
    in_specs = [lead_block(a, tile) for a in args[:5]] + [ANYWHERE] * 2 + [whole_block(vectors)] + [ANYWHERE] * 6
    out_shape = [
        shape_of((tokens, units), bf16),
        shape_of((tokens, units), bf16),
        shape_of((tokens, model), bf16),
        shape_of((8, model), f32),
        shape_of((8, units), f32),
        shape_of((8, units), f32),
    ]
    return call(
        feed_back_kernel,
        (tokens // tile,),
        in_specs,
        [lead_block(o, tile) for o in out_shape[:3]] + [fixed_block(o) for o in out_shape[3:]],
        out_shape,
        args,
        info,
        scratch=[pltpu.VMEM((model, units), bf16), pltpu.VMEM((units, model), bf16)] * 2
        + [pltpu.SemaphoreType.DMA((8 + 2 * (units // 512),))],
        flops=8 * tokens * model * units * 1.2,
        moved=tokens * units * 8,
        limit=26 << 20,
        kept=dict.fromkeys((0, 1), UNITS_MEMORY),
    )


def input_rims_kernel(span, info_ref, *refs):
    groups, weights, pieces, refs = (refs[:2], refs[2:4]), refs[4:6], refs[6:10], refs[10:]
    left_ref, right_ref, wk_ref, wv_ref, sems = refs
    loads = Loads(sems, *plan_square(info_ref, pieces, (wk_ref, wv_ref), 1))
    loads.start()
    ranges = (pl.ds(0, WINDOW), pl.ds(WINDOW + span, WINDOW))
    rows = left_ref.shape[0]

    def rims(grads, *weights):
        total = None
        for grad, weight in zip(grads, weights):
            cells = jnp.concatenate([grad[row, at] for at in ranges for row in range(rows)], axis=0)
            term = mul_t(cells, weight[...])
            total = term if total is None else total + term
        return total

    total = rims(groups[0], *weights)
    loads.ready(0, 1)
    total = low(total + rims(groups[1], wk_ref, wv_ref))
    for row in range(rows):
        left_ref[row] = total[row * WINDOW : (row + 1) * WINDOW]
        right_ref[row] = total[(rows + row) * WINDOW : (rows + row + 1) * WINDOW]


def input_rims(info, own, other, weights, pieces, span):
    rows, _, local = own[1].shape
    model = weights[0].shape[0]
    args = [own[1], own[2], other[1], other[2], *map(far, (*weights[1:], *pieces))]
    in_specs = [whole_block(a) for a in args[:6]] + [ANYWHERE] * 4
    out_shape = [shape_of((rows, WINDOW, model), bf16)] * 2
    return call(
        functools.partial(input_rims_kernel, span),
        (1,),
        in_specs,
        [fixed_block(o) for o in out_shape],
        out_shape,
        args,
        info,
        scratch=[pltpu.VMEM((model, local), bf16)] * 2 + [pltpu.SemaphoreType.DMA((8,))],
        flops=16 * rows * WINDOW * model * local,
        moved=rows * WINDOW * model * 12,
    )


def input_center_kernel(span, info_ref, one_ref, *refs):
    groups, weights, pieces, refs = (refs[:3], refs[3:6]), refs[6:9], refs[9:13], refs[13:]
    mine_ref, theirs_ref, *scratch, sems = refs
    plan = [[pair] for pair in zip(weights, scratch[:3])]
    loads = Loads(sems, *plan, *plan_square(info_ref, pieces, scratch[3:]))
    own_rows = pl.ds(WINDOW, span)
    half = mine_ref.shape[2]
    lower, upper = slice(0, half), slice(half, 2 * half)

    def work(ready):
        center = one_ref[0].astype(f32)
        for which, (dq, dk, dv) in enumerate(groups):
            for i, cells in enumerate((dq[0], dk[0, own_rows], dv[0, own_rows])):
                ready(3 * which + i)
                center = center + mul_t(cells, scratch[3 * which + i][...])

        def split(mine, theirs):
            mine_ref[0] = center[:, mine]
            theirs_ref[0] = low(center[:, theirs])

        pl.when(info_ref[PIPE] == 0)(lambda: split(lower, upper))
        pl.when(info_ref[PIPE] == 1)(lambda: split(upper, lower))

    loads.run(work)


def input_center(info, grad_one, own, other, weights, pieces, span):
    rows, extent, local = own[1].shape
    model = grad_one.shape[2]
    args = [grad_one, *own, *other, *map(far, (*weights, *pieces))]
    in_specs = [lead_block(a) for a in args[:7]] + [ANYWHERE] * 7
    out_shape = [shape_of((rows, span, model // 2), f32), shape_of((rows, span, model // 2), bf16)]
    return call(
        functools.partial(input_center_kernel, span),
        (rows,),
        in_specs,
        [lead_block(o) for o in out_shape],
        out_shape,
        args,
        info,
        scratch=[pltpu.VMEM((model, local), bf16)] * 6 + [pltpu.SemaphoreType.DMA((15,))],
        flops=12 * rows * span * model * local,
        moved=rows * extent * model * 12,
    )


def finish_kernel(rows, info_ref, mine, got, head, tail, head_got, tail_got, mol, mol_got, out_ref, mol_ref):
    row = pl.program_id(0)
    width = head.shape[1]
    own = (row >= rows) == (info_ref[PIPE] == 1)

    def write(center, first, last, molecules):
        out_ref[0] = center[0].astype(f32)
        out_ref[0, :width] += first[0].astype(f32)
        out_ref[0, out_ref.shape[1] - width :] += last[0].astype(f32)
        mol_ref[0] = molecules[0]

    pl.when(own)(lambda: write(mine, head, tail, mol))
    pl.when(jnp.logical_not(own))(lambda: write(got, head_got, tail_got, mol_got))


def finish(info, mine, got, head, tail, head_got, tail_got, mol, mol_got):
    rows, span, half = mine.shape
    width = head.shape[1]

    def core_rows(array):
        return pl.BlockSpec((1,) + tuple(array.shape[1:]), lambda i, info_ref: (i % rows, 0, 0))

    rims = pl.BlockSpec((1, width, half), lambda i, info_ref: (i % rows, 0, info_ref[PIPE]))
    out_shape = [shape_of((2 * rows, span, half), f32), shape_of((2 * rows,) + tuple(mol.shape[1:]), bf16)]
    return call(
        functools.partial(finish_kernel, rows),
        (2 * rows,),
        [core_rows(mine), core_rows(got), rims, rims] + [core_rows(a) for a in (head_got, tail_got, mol, mol_got)],
        [lead_block(o) for o in out_shape],
        out_shape,
        [mine, got, head, tail, head_got, tail_got, mol, mol_got],
        info,
        moved=rows * span * half * 20,
    )


def swapped(block, axis, bit=0):
    count = lax.axis_size(axis)
    return lax.ppermute(block, axis, [(i, i ^ (1 << bit)) for i in range(count)])


def to_core(blocks):
    return [swapped(block, "pipe") for block in blocks]


def from_chunk(block, distance):
    axes = ("seq", "mp")
    count = lax.axis_size("seq") * lax.axis_size("mp")
    return lax.ppermute(block, axes, [(i + distance, i) for i in range(count) if 0 <= i + distance < count])


def pick(array, index, dim):
    return lax.dynamic_index_in_dim(array, index, dim, keepdims=False)


def add(left, right):
    return low(left.astype(f32) + right.astype(f32))


def bits_of(axis):
    return lax.axis_size(axis).bit_length() - 1


class Halving:
    def __init__(self, parts, dim, axis):
        self.dim, self.axis = dim, axis
        self.keep, self.sent = self.split(parts, 0)

    def go(self):
        self.got = swapped(self.sent, self.axis)

    def split(self, parts, bit):
        dim = self.dim
        shaped = parts.reshape(parts.shape[:dim] + (parts.shape[dim] // 2, 2) + parts.shape[dim + 1 :])
        mine = (lax.axis_index(self.axis) >> bit) & 1
        return pick(shaped, mine, dim + 1), pick(shaped, 1 - mine, dim + 1)

    def finish(self, *gates):
        parts = add(self.keep, after(self.got, *gates))
        for bit in range(1, bits_of(self.axis)):
            keep, sent = self.split(parts, bit)
            parts = add(keep, swapped(sent, self.axis, bit))
        return parts.reshape(parts.shape[: self.dim] + parts.shape[self.dim + 1 :])


class HalvingDp:
    def __init__(self, parts):
        self.bit = 0
        self.split(parts)

    def split(self, parts):
        half = parts.shape[0] // 2
        self.keep, self.sent = parts[:half], parts[half:]

    def go(self):
        self.got = swapped(self.sent, "dp", self.bit)
        self.bit += 1

    def landed(self, *gates):
        return add(self.keep, after(self.got, *gates))

    def step(self, *gates):
        self.split(self.landed(*gates))

    def finish(self, *gates):
        while self.keep.shape[0] > 1:
            self.step()
            self.go()
        return self.landed(*gates)[0]


def sending(value, *halvings):
    value, *sent = tie(value, *(h.sent for h in halvings))
    for halving, block in zip(halvings, sent):
        halving.sent = block
        halving.go()
    return value


def relay(quarter):
    first = swapped(quarter, "mp")
    return first, swapped(first, "seq")


def all_pieces(first, second):
    return [first, second, swapped(first, "pipe"), swapped(second, "pipe")]


def in_order(first, mine, recv, axis):
    return jnp.where(
        first == 0, jnp.concatenate([mine, recv], axis=axis), jnp.concatenate([recv, mine], axis=axis)
    )


def after(value, *others):
    return lax.optimization_barrier((value, *others))[0] if others else value


def tie(*values):
    return lax.optimization_barrier(values)


def on_device(
    characters,
    row_lengths,
    w_query,
    b_query,
    w_key,
    w_value,
    b_value,
    w_attn_out,
    b_attn_out,
    gain_one,
    shift_one,
    w_inner,
    b_inner,
    w_outer,
    b_outer,
    gain_two,
    shift_two,
    w_conv,
    b_conv,
    gain_three,
    shift_three,
    molecule_grad,
):
    pipe = lax.axis_index("pipe")
    seq = lax.axis_index("seq")
    mp = lax.axis_index("mp")
    dp_size, seq_size, mp_size = (lax.axis_size(a) for a in ("dp", "seq", "mp"))
    all_rows, span, half_model = characters.shape
    rows = all_rows // 2
    model = 2 * half_model
    local = w_query.shape[1]
    units = w_inner.shape[1]
    tokens = rows * span
    mols = tokens // KERNEL
    block = min(WINDOW, span)
    tile = min(256, tokens)
    own_start = (seq * lax.axis_size("mp") + mp) * span

    def rows_of(array, index):
        return lax.dynamic_slice_in_dim(array, index * rows, rows, 0)

    me = 2 * (seq & 1) + pipe
    lengths = rows_of(row_lengths, pipe)
    scalars = jnp.stack([own_start, pipe, me, lax.axis_index("dp"), mp]).astype(jnp.int32)
    info = jnp.concatenate([scalars, lengths])
    squares = (w_query, w_key, w_value)
    biases, vectors = gather_small(
        b_query,
        b_value,
        b_inner,
        (b_attn_out, gain_one, shift_one, b_outer, gain_two, shift_two, b_conv, gain_three, shift_three),
    )
    hops = -(-WINDOW // span)
    width = min(span, WINDOW)

    center_send, mol_send = pack_rows(info, [characters, molecule_grad])
    center_got = swapped(center_send, "pipe")
    packet = pack_first(after(info, center_send), squares, w_attn_out, biases)
    tail, head = pack_rims(after(info, packet), characters, center_got, width)
    square_first = swapped(packet, "mp")
    inner_packet, outer_packet = pack_second(after(info, tail), w_inner, w_outer)
    center_got, tail, head, inner_packet, outer_packet = tie(center_got, tail, head, inner_packet, outer_packet)
    inner_own = attend_inner(info, characters, center_got, squares, biases, span, block)
    *inner_own, square_first = tie(*inner_own, square_first)
    square_second = swapped(square_first, "seq")
    square_first, tail, head = tie(square_first, tail, head)
    left, right = [], []
    for hop in range(1, hops + 1):
        left.insert(0, from_chunk(tail, -hop))
        right.append(from_chunk(head, hop))
    left, right = (a[0] if hops == 1 else jnp.concatenate(a, axis=2) for a in (left, right))
    square_second, left, right, inner_packet, outer_packet = tie(square_second, left, right, inner_packet, outer_packet)
    inner_first = swapped(inner_packet, "mp")
    outer_first = swapped(outer_packet, "mp")
    mol_grad = molecule_grad.reshape(2 * mols, half_model)

    square_pieces = all_pieces(square_first, square_second)
    biases_other = square_first[square_first.shape[0] - 16 :]
    inner_other = attend_inner(info, characters, center_got, square_pieces, biases_other, span, block)
    (kr_own, vr_own, att_own, lse_own, kr_other, vr_other, att_other, lse_other, n1, scale1, middle, x_ext) = attend_outer(
        info,
        (characters, center_got, left, right),
        vectors,
        (biases, biases_other),
        (inner_own, inner_other),
        (w_key, w_value, w_attn_out),
        square_pieces,
        span,
        block,
    )
    kept_own = (inner_own[0], inner_own[1], kr_own, inner_own[2], vr_own, lse_own)
    kept_other = (inner_other[0], inner_other[1], kr_other, inner_other[2], vr_other, lse_other)
    middle, inner_first = tie(middle, inner_first)
    inner_second = swapped(inner_first, "seq")
    n1, scale1, middle = (a.reshape(tokens, -1) for a in (n1, scale1, middle))
    act_own, slope_own, part = feed(
        info, middle, biases, units, span, tile, w_inner, w_outer
    )
    part, inner_second, outer_first = tie(part, inner_second, outer_first)
    pieces = (*all_pieces(inner_first, inner_second), outer_first, swapped(outer_first, "pipe"))
    mol_got = swapped(after(mol_send, part), "pipe").reshape(mols, half_model)
    act_other, slope_other, n2, scale2, grouped = feed(
        info, middle, biases_other, units, span, tile, tail=(part, n1, vectors), pieces=pieces
    )
    mol_mine, mol_theirs, grad_conv, grad_feed, vec_conv = conv(
        info, grouped, w_conv.reshape(KERNEL, model, model), vectors, mol_grad, mol_got, n2, scale2, span, 2
    )
    mol_shape = (rows, span // KERNEL, half_model)
    mol_mine = mol_mine.reshape(mol_shape)
    mol_theirs = mol_theirs.reshape(mol_shape)

    conv_theirs = conv_weight(info, 1, grouped, grad_conv, dp_size)
    conv_got = to_core(conv_theirs)
    outer_theirs = weight(info, 1, after(grad_feed, *conv_theirs), act_own, act_other, dp_size)
    outer_got = to_core(outer_theirs)
    (conv_part,) = conv_weight(info, 0, grouped, after(grad_conv, *outer_theirs), dp_size, conv_got)
    conv_halving = Halving(conv_part.reshape(dp_size, seq_size, mp_size, -1, model), 2, "mp")
    grad_feed = sending(grad_feed, conv_halving)
    (outer_part,) = weight(info, 0, grad_feed, act_own, act_other, dp_size, outer_got)
    outer_halving = Halving(outer_part.reshape(2, dp_size, seq_size, -1, units), 2, "seq")
    grad_feed = sending(grad_feed, outer_halving)
    gh_own, gh_other, grad_branch, vec_one, bi_own, bi_other = feed_back(
        info,
        grad_feed,
        (slope_own, slope_other),
        n1,
        scale1,
        w_outer,
        w_inner,
        vectors,
        pieces,
        tile,
    )
    inner_theirs = weight(info, 1, middle, gh_own, gh_other, dp_size)
    conv_part = conv_halving.finish(*inner_theirs)
    conv_halving = Halving(conv_part, 1, "seq")
    outer_part = outer_halving.finish(*inner_theirs)
    *inner_theirs, conv_halving.sent, outer_sent = tie(*inner_theirs, conv_halving.sent, outer_part[1])
    conv_halving.go()
    outer_got = swapped(outer_sent, "mp")
    inner_got = to_core(inner_theirs)

    grad_branch = grad_branch.reshape(rows, span, model)
    *back_other, vec_other = attend_back(
        info, after(grad_branch, *inner_theirs), kept_other, square_pieces, block
    )

    def narrow(part):
        return jnp.concatenate([part[:, :, :model], part[:, :, model:]], axis=1)

    conv_part = conv_halving.finish(vec_other)
    outer_part = add(outer_part[0], after(outer_got, vec_other)).reshape(dp_size, -1, units)
    merged_halving = HalvingDp(jnp.concatenate([conv_part, narrow(outer_part)], axis=1))
    middle = sending(middle, merged_halving)
    (inner_part,) = weight(info, 0, middle, gh_own, gh_other, dp_size, inner_got)
    x_late, inner_sent = tie(x_ext, inner_part[1])
    inner_got = swapped(inner_sent, "mp")
    (other_theirs,) = project_weight(info, 1, x_late, grad_branch, (*back_other, att_other), span, dp_size)
    other_got = swapped(other_theirs, "pipe")
    *back_own, vec = attend_back(
        info,
        after(grad_branch, other_theirs),
        kept_own,
        w_attn_out,
        block,
        (vec_conv, vec_one, bi_own, bi_other, vec_other),
    )
    merged_halving.step(vec)
    x_late, merged_halving.sent = tie(x_late, merged_halving.sent)
    (own_theirs,) = project_weight(info, 1, x_late, grad_branch, (*back_own, att_own), span, dp_size)
    late_info, own_theirs, vec, merged_halving.sent = tie(info, own_theirs, vec, merged_halving.sent)
    merged_halving.go()
    own_got = swapped(own_theirs, "pipe")
    vec = low(vec + swapped(vec, "pipe"))
    left, right = input_rims(late_info, back_own, back_other, squares, square_pieces, span)
    inner_part = add(inner_part[0], after(inner_got, left))
    inner_halving = Halving(inner_part.reshape(dp_size, seq_size, -1, units), 1, "seq")
    x_late, left, right = tie(x_late, left, right)
    x_late = sending(x_late, inner_halving)
    rims = []
    for hop in range(1, hops + 1):
        top = WINDOW - (hop - 1) * span
        rims.append(from_chunk(right[:, WINDOW - top : WINDOW - top + width], -hop))
        rims.append(from_chunk(left[:, top - width : top], hop))
    other_first, other_last = project_weight(
        info, 0, x_late, grad_branch, (*back_other, att_other), span, dp_size, other_got, vec
    )
    own_got, x_late, other_first = tie(own_got, x_late, other_first)
    first_got = swapped(other_first, "mp")
    own_first, own_last = project_weight(
        info, 0, x_late, grad_branch, (*back_own, att_own), span, dp_size, own_got
    )
    last_halving = Halving(jnp.stack([own_last, other_last]).reshape(2, dp_size, seq_size, -1, model), 2, "seq")
    inner_part = inner_halving.finish(own_first)
    grad_branch, inner_part = tie(grad_branch, inner_part)
    grad_branch = sending(grad_branch, last_halving)
    mine, theirs = input_center(info, grad_branch, back_own, back_other, squares, square_pieces, span)
    first_got, mine, *rims = tie(first_got, mine, *rims)
    head, tail = rims[:2]
    for hop in range(1, hops):
        head, tail = add(head, rims[2 * hop]), add(tail, rims[2 * hop + 1])
    rims = jnp.stack([head, tail])
    merged = merged_halving.finish(mine)
    own_rows = first_got.shape[0] - 16
    first_part = add(own_first, first_got[:own_rows]).reshape(dp_size, seq_size, -1, model)
    vec = add(vec, first_got[own_rows:])

    def with_vec(part):
        return jnp.concatenate([part.reshape(-1, model), vec], axis=0)

    chars_grad = None
    for bit in range(bits_of("seq")):
        shaped = first_part.reshape(dp_size, first_part.shape[1] // 2, 2, -1, model)
        bit_mine = (seq >> bit) & 1
        got = swapped(with_vec(pick(shaped, 1 - bit_mine, 2)), "seq", bit)
        if chars_grad is None:
            last_part = last_halving.finish(mine)
            inner_halving = HalvingDp(inner_part)
            last_sent, inner_halving.sent, mine, rims, mol_theirs, theirs = tie(
                last_part[1], inner_halving.sent, mine, rims, mol_theirs, theirs
            )
            last_got = swapped(last_sent, "mp")
            inner_halving.go()
            rims_got = swapped(lax.dynamic_slice_in_dim(rims, (1 - pipe) * half_model, half_model, 3), "pipe")
            chars_grad, molecules = finish(
                info,
                mine,
                swapped(theirs, "pipe"),
                head,
                tail,
                rims_got[0],
                rims_got[1],
                mol_mine,
                swapped(mol_theirs, "pipe"),
            )
            got, chars_grad, molecules = tie(got, chars_grad, molecules)
        count = got.shape[0] - 16
        first_part = add(pick(shaped, bit_mine, 2), got[:count].reshape(dp_size, shaped.shape[1], -1, model))
        vec = add(vec, got[count:])
    last_part = add(last_part[0], after(last_got, chars_grad))
    head_part = jnp.concatenate([first_part.reshape(dp_size, -1, model), last_part], axis=1)
    for bit in range(bits_of("dp")):
        half = head_part.shape[0] // 2
        got = swapped(with_vec(head_part[half:]), "dp", bit)
        count = got.shape[0] - 16
        head_part = add(head_part[:half], got[:count].reshape(head_part[:half].shape))
        vec = add(vec, got[count:])
    inner_sum = inner_halving.finish()
    head_sum = head_part[0].astype(f32)
    vec = vec.astype(f32)
    grad_b_conv, grad_gain_three, grad_shift_three, grad_gain_two, grad_shift_two, grad_b_outer = (
        vec[i] for i in range(6)
    )
    grad_b_attn_out, grad_gain_one, grad_shift_one = (vec[i] for i in range(6, 9))
    grad_b_inner = vec[9:13].reshape(-1)
    grad_b_query, grad_b_value = (vec[i] for i in range(13, 15))
    size = conv_part.shape[1]
    grad_w_conv = merged[:size].astype(f32)
    outer_sum = jnp.concatenate([merged[size : size + size // 2], merged[size + size // 2 :]], axis=1).astype(f32)
    inner_sum = inner_sum.astype(f32)

    per_device = head_sum.shape[0] // 2
    grad_w_query, grad_w_key, grad_w_value, grad_w_attn = (
        head_sum[i // 2 * per_device : (i // 2 + 1) * per_device, i % 2 * local : (i % 2 + 1) * local] for i in range(4)
    )
    return (
        molecules,
        chars_grad,
        grad_w_query,
        grad_b_query,
        grad_w_key,
        grad_w_value,
        grad_b_value,
        grad_w_attn.T,
        grad_b_attn_out,
        grad_gain_one,
        grad_shift_one,
        inner_sum,
        grad_b_inner,
        outer_sum.T,
        grad_b_outer,
        grad_gain_two,
        grad_shift_two,
        grad_w_conv,
        grad_b_conv,
        grad_gain_three,
        grad_shift_three,
    )


def solution(mesh):
    return jax.shard_map(
        on_device,
        mesh=mesh,
        in_specs=(
            P("dp", ("seq", "mp"), "pipe"),
            P("dp"),
            P(None, "mp"),
            P("mp"),
            P(None, "mp"),
            P(None, "mp"),
            P("mp"),
            P("mp", None),
            P(),
            P(),
            P(),
            P(None, "mp"),
            P("mp"),
            P("mp", None),
            P(),
            P(),
            P(),
            P(),
            P(),
            P(),
            P(),
            P("dp", ("seq", "mp"), "pipe"),
        ),
        out_specs=(
            P("dp", ("seq", "mp"), "pipe"),
            P("dp", ("seq", "mp"), "pipe"),
            P(("pipe", "dp", "seq"), "mp"),
            P(),
            P(("pipe", "dp", "seq"), "mp"),
            P(("pipe", "dp", "seq"), "mp"),
            P(),
            P("mp", ("pipe", "dp", "seq")),
            P(),
            P(),
            P(),
            P(("pipe", "dp", "seq"), "mp"),
            P(),
            P("mp", ("pipe", "dp", "seq")),
            P(),
            P(),
            P(),
            P(("pipe", "dp", "seq", "mp"), None),
            P(),
            P(),
            P(),
        ),
        check_vma=False,
    )
```
